32 devices in a mesh: dp: 8 (over y, x, core), tensor: 4 (over z).
Axes of the slice: x: 2, y: 2, z: 4, core: 2. Of those that a mesh axis runs over, the one named last changes fastest.
Arguments:
- tokens: bfloat16 [32768, 512], P(('dp', 'tensor')), may hold values from -6 to 6
- cotangent: bfloat16 [32768, 512], P(('dp', 'tensor')), may hold values from -6 to 6
- seq_lengths: int32 [8, 2], P('dp'), may hold values from 1023 to 3073, as said below
- features: bfloat16 [8, 64, 256], replicated, may hold values from -6 to 6
- ln1_gain: float32 [512], replicated, may hold values from 0.1 to 1.9
- w_qkv: bfloat16 [512, 1536], replicated, may hold values from -0.25 to 0.25
- w_out: bfloat16 [512, 512], replicated, may hold values from -1.5 to 1.5
- b_out: bfloat16 [512], replicated, may hold values from -2 to 2
- ln2_gain: float32 [512], replicated, may hold values from 0.1 to 1.9
- w_in: bfloat16 [512, 2048], P(None, 'tensor'), may hold values from -0.25 to 0.25
- b_in: bfloat16 [2048], P('tensor'), may hold values from -2 to 2
- w_down: bfloat16 [2048, 512], P('tensor'), may hold values from -0.125 to 0.125
- b_down: bfloat16 [512], replicated, may hold values from -2 to 2
Outputs:
- layer_out: bfloat16 [32768, 512], P(('dp', 'tensor'))
- input_grad: float32 [32768, 512], P(('dp', 'tensor'))
- grad_ln1_gain: float32 [512], replicated
- grad_w_qkv: float32 [512, 1536], replicated
- grad_w_out: float32 [512, 512], replicated
- grad_b_out: float32 [512], replicated
- grad_ln2_gain: float32 [512], replicated
- grad_w_in: float32 [512, 2048], P(None, 'tensor')
- grad_b_in: float32 [2048], P('tensor')
- grad_w_down: float32 [2048, 512], P('tensor')
- grad_b_down: float32 [512], replicated
The draws below stay inside these ranges and needn't reach their ends.
Inputs may be any that keep to these rules, and one draw needn't show every extreme that they name: `seq_lengths`: each row sums to 4096: one sequence of exactly 3073 rows and one of 1023 rows, in a drawn order.
All inputs are finite; a program needn't handle non-finite values.
Results may differ from the reference program's by a relative error of at most 0.019.
The reference program's roundings to bfloat16 on the way count: a program that leaves them out, or rounds other values in their place, can miss the bound.
Values may be sent and summed in bfloat16 or wider, within the bound.
A program may use at most 192 MiB of HBM per device.

```python
import jax
import jax.numpy as jnp
from jax import lax

D = 512
HEADS = 8
HD = 64
M = 256
FF = 2048
TOK_DEV = 1024
SEQS = 2
BLK = 512
GROUP_TOK = 4096
GROUPS = 8
TOKENS = 32768


def draw_seq_lengths(key, part):
    key = jax.random.fold_in(key, 11)
    chosen = jax.random.randint(key, (GROUPS, 1), 0, SEQS)
    column = jnp.arange(SEQS)[None, :]
    longest = GROUP_TOK - TOK_DEV + 1
    shortest = TOK_DEV - 1
    return jnp.where(column == chosen, longest, shortest).astype(jnp.int32)


def level_of(rng, dims, shards, low, high):
    level = 1.0
    for dim, blocks in shards:
        draws = jax.random.uniform(jax.random.fold_in(jax.random.fold_in(rng, 6), dim), (blocks,), jnp.float32, low / len(shards), high / len(shards))
        level = level * jnp.repeat(jnp.exp(draws), dims[dim] // blocks).reshape((-1,) + (1,) * (len(dims) - 1 - dim))
    return level


def normal_values(rng, shape, width, most, split=(), held_as=jnp.bfloat16):
    loudness = level_of(rng, shape, split, -0.22, 0.18) if split else 1.0
    values = jax.random.normal(rng, shape, jnp.float32) * width * loudness
    return jnp.minimum(jnp.maximum(values, -most), most).astype(held_as)


def setup_inputs(seed: int = 0) -> dict:
    splits = jax.random.split(jax.random.key(seed), 14)
    tokens = normal_values(splits[0], (TOKENS, D), 1.0, 6.0, ((0, 32),))
    cotangent = normal_values(splits[1], (TOKENS, D), 1.0, 6.0, ((0, 32),))
    seq_lengths = draw_seq_lengths(jax.random.fold_in(splits[13], 71), 0)
    features = normal_values(splits[3], (HEADS, HD, M), 1.0, 6.0)
    ln1_gain = jnp.clip(1.0 + 0.18 * jax.random.normal(splits[4], (D,), jnp.float32), 0.1, 1.9)
    w_qkv = normal_values(splits[5], (D, 3 * D), D ** -0.5, 0.25)
    w_out = normal_values(splits[6], (D, D), (D // 32) ** -0.5, 1.5)
    b_out = normal_values(splits[7], (D,), 0.3, 2.0)
    ln2_gain = jnp.clip(1.0 + 0.18 * jax.random.normal(splits[8], (D,), jnp.float32), 0.1, 1.9)
    w_in = normal_values(splits[9], (D, FF), D ** -0.5, 0.25, ((1, 4),))
    b_in = normal_values(splits[10], (FF,), 0.3, 2.0, ((0, 4),))
    w_down = normal_values(splits[11], (FF, D), FF ** -0.5, 0.125, ((0, 4),))
    b_down = normal_values(splits[12], (D,), 0.3, 2.0)
    return dict(tokens=tokens, cotangent=cotangent, seq_lengths=seq_lengths, features=features, ln1_gain=ln1_gain, w_qkv=w_qkv, w_out=w_out, b_out=b_out, ln2_gain=ln2_gain, w_in=w_in, b_in=b_in, w_down=w_down, b_down=b_down)


@jax.custom_vjp
def low(v):
    return lax.optimization_barrier(v.astype(jnp.bfloat16)).astype(jnp.float32)

@jax.custom_vjp
def low_back(v):
    return v

def low_keep(v):
    return (low(v), None)

def low_pass(kept, grad):
    return (grad,)

def back_keep(v):
    return (v, None)

def back_low(kept, grad):
    return (low(grad),)
low.defvjp(low_keep, low_pass)
low_back.defvjp(back_keep, back_low)
EPSILON = 1e-05

def matmul(left_side, right_side):
    return jnp.dot(left_side, right_side, precision=lax.Precision.HIGHEST)

def layer_norm(values, gain):
    centre = lax.optimization_barrier(jnp.mean(values, -1, keepdims=True))
    shifted = values - centre
    spread = lax.optimization_barrier(jnp.mean(shifted * shifted, -1, keepdims=True))
    return shifted * lax.rsqrt(spread + EPSILON) * gain

def segment_ids(lengths):
    offsets = (jnp.cumsum(lengths) - lengths).astype(jnp.int32)
    places = jnp.arange(GROUP_TOK, dtype=jnp.int32)
    counted = lax.optimization_barrier(jnp.sum((places[:, None] >= offsets[None, :]).astype(jnp.int32), 1))
    return (counted - 1).astype(jnp.int32)

def features_of(values, feature_map):
    project = jnp.einsum('rhd,hdm->rhm', values, feature_map, precision=lax.Precision.HIGHEST)
    argument = low_back(project - 0.5 * lax.optimization_barrier(jnp.sum(values * values, -1, keepdims=True)))
    return low(jnp.exp(argument) * M ** (-0.5))

def attend_block(carried, inputs):
    states, totals, previous = carried
    query_feat, key_feat, values, segment = inputs
    highest = lax.Precision.HIGHEST
    scores = low_back(jnp.einsum('ihm,jhm->hij', query_feat, key_feat, precision=highest))
    row_index = jnp.arange(BLK)
    keep_pair = (row_index[:, None] >= row_index[None, :]) & (segment[:, None] == segment[None, :])
    masked = jnp.where(keep_pair[None], scores, 0.0)
    reached = (segment == previous).astype(query_feat.dtype)[:, None]
    inner_num = jnp.einsum('hij,jhe->ihe', low(masked), values, precision=highest)
    outer_num = jnp.einsum('ihm,hme->ihe', query_feat, low(states), precision=highest)
    numerator = low_back(inner_num + reached[:, :, None] * outer_num)
    outer_den = jnp.einsum('ihm,hm->ih', query_feat, low(totals), precision=highest)
    denominator = lax.optimization_barrier(jnp.sum(masked, -1)).T + reached * outer_den
    closing = segment[-1]
    ending = (segment == closing)[:, None, None]
    keeping = previous == closing
    picked = jnp.where(ending, key_feat, 0.0)
    increment = low_back(jnp.einsum('jhm,jhe->hme', picked, values, precision=highest))
    new_states = jnp.where(keeping, states, 0.0) + increment
    new_totals = jnp.where(keeping, totals, 0.0) + lax.optimization_barrier(jnp.sum(picked, 0))
    return ((new_states, new_totals, closing), numerator / denominator[:, :, None])

def attention(query_s, key_s, value_s, feature_map, segment):
    query_feat = features_of(query_s, feature_map)
    key_feat = features_of(key_s, feature_map)
    block_count = GROUP_TOK // BLK

    def blocked(array):
        return array.reshape((block_count, BLK) + array.shape[1:])
    initial = (jnp.zeros((HEADS, M, HD), jnp.float32), jnp.zeros((HEADS, M), jnp.float32), jnp.array(-1, dtype=jnp.int32))
    _, outputs = lax.scan(jax.checkpoint(attend_block), initial, (blocked(query_feat), blocked(key_feat), blocked(value_s), blocked(segment)))
    return outputs.reshape(GROUP_TOK, D)

def block_layer(params, tokens, feature_map, segment):
    ln1_gain, w_qkv, w_out, b_out, ln2_gain, w_in, b_in, w_down, b_down = params
    normed = low(layer_norm(tokens, ln1_gain))
    mixed_qkv = low_back(matmul(normed, w_qkv))
    shrink = HD ** (-0.25)
    query_s = low(mixed_qkv[:, :D] * shrink).reshape(GROUP_TOK, HEADS, HD)
    key_s = low(mixed_qkv[:, D:2 * D] * shrink).reshape(GROUP_TOK, HEADS, HD)
    value_s = low(mixed_qkv[:, 2 * D:]).reshape(GROUP_TOK, HEADS, HD)
    attended = low(attention(query_s, key_s, value_s, feature_map, segment))
    branch = low_back(matmul(attended, w_out) + b_out)
    hidden = tokens + branch
    normed_two = low(layer_norm(hidden, ln2_gain))
    inner_pre = low_back(matmul(normed_two, w_in) + b_in)
    active = low(jax.nn.gelu(inner_pre))
    return hidden + low_back(matmul(active, w_down) + b_down)

def reference(tokens, cotangent, seq_lengths, features, ln1_gain, w_qkv, w_out, b_out, ln2_gain, w_in, b_in, w_down, b_down):
    params = tuple((array.astype(jnp.float32) for array in (ln1_gain, w_qkv, w_out, b_out, ln2_gain, w_in, b_in, w_down, b_down)))
    feature_map = features.astype(jnp.float32)
    inputs = tokens.astype(jnp.float32).reshape(GROUPS, GROUP_TOK, D)
    upstream = cotangent.astype(jnp.float32).reshape(GROUPS, GROUP_TOK, D)

    def group_step(totals, group_inputs):
        block_in, block_grad, lengths = group_inputs
        segment = segment_ids(lengths)

        def forward(weights, values):
            return block_layer(weights, values, feature_map, segment)
        result, pullback = jax.vjp(forward, params, block_in)
        weight_grads, input_grad = pullback(block_grad)
        totals = jax.tree.map(jnp.add, totals, weight_grads)
        return (totals, (result.astype(jnp.bfloat16), input_grad))
    start_sum = jax.tree.map(jnp.zeros_like, params)
    totals, (results, input_grads) = lax.scan(group_step, start_sum, (inputs, upstream, seq_lengths))
    return (results.reshape(TOKENS, D), input_grads.reshape(TOKENS, D), totals[0], totals[1], totals[2], totals[3], totals[4], totals[5], totals[6], totals[7], totals[8])
```

```python
import functools

import jax
import jax.numpy as jnp
from jax import lax
from jax.experimental import pallas as pl
from jax.experimental.pallas import tpu as pltpu
from jax.sharding import PartitionSpec as P

MESH = pl.DeviceIdType.MESH
F32 = jnp.float32
BF16 = jnp.bfloat16
EPSILON = 1e-05
BR = 256
SQRT_2_OVER_PI = 0.7978845608028654
CUBIC = 0.044715


def dot(a, b):
    return jnp.dot(a, b, preferred_element_type=F32)


def dot_rt(a, b):
    return lax.dot_general(a, b, (((1,), (1,)), ((), ())), preferred_element_type=F32)


def dot_lt(a, b):
    return lax.dot_general(a, b, (((0,), (0,)), ((), ())), preferred_element_type=F32)


def xor(a, b, size):
    out, bit = 0, 1
    while bit < size:
        out = out + bit * lax.rem(lax.div(a, bit) + (b // bit if isinstance(b, int) else lax.div(b, bit)), 2)
        bit *= 2
    return out


def iota(shape, axis):
    return lax.broadcasted_iota(jnp.int32, shape, axis)


def layer_kernel(
    tn,
    dpn,
    lens,
    tok,
    cot,
    feats,
    g1,
    wqkv,
    wout,
    bout,
    g2,
    win,
    bin_,
    wdn,
    bdn,
    layer_out,
    igrad,
    fin,
    vec_out,
    wfull,
    n1s,
    qs,
    ks,
    vs,
    phq,
    phk,
    featx,
    bsw,
    mask,
    maskt,
    lst,
    sb,
    rsw_s,
    attn,
    facc,
    xh2,
    rstd2,
    n2s,
    ad,
    chf_in,
    chf_out,
    chb_in,
    chb_out,
    gbuf,
    ra,
    rb,
    rc,
    rca,
    vec,
    va,
    vb,
    vc,
    wz_s,
    wz_r,
    wc_s,
    wc_r,
    chf_s,
    chf_r,
    chb_s,
    chb_r,
    a_s,
    a_r,
    b_s,
    b_r,
    c_s,
    c_r,
    d_s,
    d_r,
    e_s,
    e_r,
    va_s,
    va_r,
    vb_s,
    vb_r,
    vc_s,
    vc_r,
):
    rows_n, width = tok.shape
    heads, hw, feat_n = feats.shape
    pairs = heads // 2
    pw = 2 * hw
    nb = rows_n // BR
    seqs = lens.shape[1]
    shrink = hw ** (-0.25)
    featscale = feat_n ** (-0.5)
    npeer = dpn // 2
    rp = width // npeer

    dp = lax.axis_index("dp")
    t = lax.axis_index("tensor")
    cb = lax.rem(dp, 2)
    q = lax.div(dp, 2)
    core_dev = (dp + 1 - 2 * cb, t)

    def peer(k):
        return xor(q, k, npeer)

    def peer_dev(k):
        return (2 * peer(k) + cb, t)

    def z_dev(k):
        return (dp, xor(t, k, tn))

    def own_rows():
        return pl.ds(pl.multiple_of(q * rp, rp), rp)

    bar = pltpu.get_barrier_semaphore()
    targets = [core_dev] + [peer_dev(k) for k in range(1, npeer)] + [z_dev(k) for k in range(1, tn)]
    for dev in targets:
        pl.semaphore_signal(bar, inc=1, device_id=dev, device_id_type=MESH)
    pl.semaphore_wait(bar, len(targets))

    def remote(src, dst, ss, rs, dev):
        return pltpu.make_async_remote_copy(
            src_ref=src, dst_ref=dst, send_sem=ss, recv_sem=rs, device_id=dev, device_id_type=MESH
        )

    def wz_copy(k):
        return remote(wfull.at[0, cb], wfull.at[k, cb], wz_s.at[k - 1], wz_r.at[k - 1], z_dev(k))

    def wc_copy(k):
        return remote(wfull.at[k, cb], wfull.at[k, cb], wc_s.at[k - 1], wc_r.at[k - 1], core_dev)

    def chf_copy(p):
        return remote(chf_out.at[p], chf_in.at[p], chf_s.at[p], chf_r.at[p], (dp, lax.rem(t + 1, tn)))

    def chb_copy(p):
        return remote(chb_out.at[p], chb_in.at[p], chb_s.at[p], chb_r.at[p], (dp, lax.rem(t + tn - 1, tn)))

    def a_copy(s):
        s = jnp.int32(s)
        return remote(gbuf.at[s, 1 - cb], ra.at[lax.rem(s, 2)], a_s.at[s], a_r.at[s], core_dev)

    def b_copy(s, k):
        s = jnp.int32(s)
        rows = pl.ds(pl.multiple_of(peer(k) * rp, rp), rp)
        return remote(gbuf.at[s, cb, rows], rb.at[lax.rem(s, 4), k - 1], b_s.at[s, k - 1], b_r.at[s, k - 1], peer_dev(k))

    def c_copy(s):
        return remote(gbuf.at[s, cb, own_rows()], rc.at[s - 1], c_s.at[0, s - 1], c_r.at[0, s - 1], z_dev(s))

    def ca_copy(i, k):
        return remote(
            rca.at[i, 0], rca.at[i, k], c_s.at[1 + i, k - 1], c_r.at[1 + i, k - 1], z_dev(k)
        )

    def d_copy(i, k):
        here = fin.at[i, cb, own_rows()]
        return remote(here, here, d_s.at[i, k - 1], d_r.at[i, k - 1], peer_dev(k))

    def d_recv(i, k):
        rows = pl.ds(pl.multiple_of(peer(k) * rp, rp), rp)
        here = fin.at[i, cb, rows]
        return remote(here, here, d_s.at[i, k - 1], d_r.at[i, k - 1], peer_dev(k))

    def e_copy(i):
        return remote(fin.at[i, cb], fin.at[i, cb], e_s.at[i], e_r.at[i], core_dev)

    def e_recv(i):
        return remote(fin.at[i, 1 - cb], fin.at[i, 1 - cb], e_s.at[i], e_r.at[i], core_dev)

    def a_start(s):
        a_copy(s).start()

    def a_finish(s):
        s = jnp.int32(s)
        a_copy(s).wait()
        gbuf[s, cb] = (gbuf[s, cb].astype(F32) + ra[lax.rem(s, 2)].astype(F32)).astype(BF16)
        for k in range(1, npeer):
            b_copy(s, k).start()

    def b_sum(s):
        s = jnp.int32(s)
        for k in range(1, npeer):
            b_copy(s, k).wait()
        total = gbuf[s, cb, own_rows()].astype(F32)
        for k in range(1, npeer):
            total = total + rb[lax.rem(s, 4), k - 1].astype(F32)
        return total.astype(BF16)

    def b_finish(s):
        gbuf[s, cb, own_rows()] = b_sum(s)

    def c_start(s):
        c_copy(s).start()

    def c_finish():
        total = gbuf[0, cb, own_rows()].astype(F32)
        for k in range(1, tn):
            c_copy(k).wait()
            total = total + rc[k - 1].astype(F32)
        fin[0, cb, own_rows()] = total.astype(BF16)
        for k in range(1, npeer):
            d_copy(0, k).start()

    def ca_start(i):
        rca[i, 0] = b_sum(tn + i)
        for k in range(1, tn):
            ca_copy(i, k).start()

    def ca_finish(i):
        for k in range(1, tn):
            ca_copy(i, k).wait()
        total = rca[i, xor(t, 0, tn)].astype(F32)
        for j in range(1, tn):
            total = total + rca[i, xor(t, j, tn)].astype(F32)
        fin[1 + i, cb, own_rows()] = total.astype(BF16)
        for k in range(1, npeer):
            d_copy(1 + i, k).start()

    def d_finish(i):
        for k in range(1, npeer):
            d_copy(i, k).wait_send()
            d_recv(i, k).wait_recv()
        e_copy(i).start()

    def e_finish(i):
        e_copy(i).wait_send()
        e_recv(i).wait_recv()

    offsets = [jnp.int32(0)]
    for c in range(1, seqs):
        offsets.append(offsets[-1] + lens[0, c - 1])
    first = t * rows_n

    def seg_at(r):
        seg = -1
        for off in offsets:
            seg = seg + jnp.where(r >= off, 1, 0)
        return seg

    def seg_array(shape, axis, start):
        places = iota(shape, axis) + start
        seg = jnp.full(shape, -1, jnp.int32)
        for off in offsets:
            seg = seg + jnp.where(places >= off, 1, 0)
        return seg

    before = seg_at(first - 1)
    closing = seg_at(first + rows_n - 1)
    passing = jnp.where(before == closing, 1.0, 0.0)

    def prev_of(b):
        return seg_at(first + b * BR - 1)

    def last_of(b):
        return seg_at(first + b * BR + BR - 1)

    def keep_of(b):
        return jnp.where(prev_of(b) == last_of(b), 1.0, 0.0)

    def ending(b):
        return seg_array((BR, pw), 0, first + b * BR) == last_of(b)

    def reached(b):
        return seg_array((BR, pw), 0, first + b * BR) == prev_of(b)

    def block(b):
        return pl.ds(pl.multiple_of(b * BR, BR), BR)

    def lanes(p):
        return pl.ds(pl.multiple_of(p * pw, pw), pw)

    low_lane = iota((BR, pw), 1) < hw
    low_row = iota((pw, feat_n), 0) < hw
    row_id = iota((pw, feat_n), 0)

    wfull[0, 0, :width] = win[...]
    wfull[0, 0, width:] = jnp.broadcast_to(bin_[...].astype(F32), (16, bin_.shape[1])).astype(BF16)
    wfull[0, 1, :width] = wdn[...]
    wfull[0, 1, width:] = jnp.zeros((16, wdn.shape[1]), BF16)
    for k in range(1, tn):
        wz_copy(k).start()

    featx[...] = jnp.zeros_like(featx)
    for p in range(pairs):
        for o in range(2):
            featx[p, o * hw : (o + 1) * hw, o * feat_n : (o + 1) * feat_n] = feats[2 * p + o]
            for rep in (1, 2):
                featx[
                    p, rep * pw + o * hw : rep * pw + (o + 1) * hw, o * feat_n : (o + 1) * feat_n
                ] = jnp.full((hw, feat_n), -0.5, BF16)
    ri, ci = iota((2 * pw, pw), 0), iota((2 * pw, pw), 1)
    swap = (lax.rem(ri, pw) < hw) != (ci < hw)
    bsw[...] = jnp.where(swap, 1.0, 0.0).astype(BF16)

    def build_mask(b, _):
        seg_i = seg_array((BR, BR), 0, first + b * BR)
        seg_j = seg_array((BR, BR), 1, first + b * BR)
        same = seg_i == seg_j
        i, j = iota((BR, BR), 0), iota((BR, BR), 1)
        mask[b] = jnp.where(same & (i >= j), 1.0, 0.0)
        maskt[b] = jnp.where(same & (j >= i), 1.0, 0.0)
        return 0

    lax.fori_loop(0, nb, build_mask, 0)
    lst[0] = jnp.zeros(lst.shape[1:], F32)
    vec[...] = jnp.zeros_like(vec)

    @pl.when(t == 0)
    def _():
        chf_in[...] = jnp.zeros_like(chf_in)

    @pl.when(t == tn - 1)
    def _():
        chb_in[...] = jnp.zeros_like(chb_in)

    def features_of(x, p):
        wide = x.astype(F32)
        square = wide * wide
        high = square.astype(BF16)
        rest = (square - high.astype(F32)).astype(BF16)
        arg = dot(jnp.concatenate([x, high, rest], 1), featx[p])
        return (jnp.exp(arg) * featscale).astype(BF16)

    def normalized(x):
        centre = jnp.mean(x, -1, keepdims=True)
        shifted = x - centre
        inverse = lax.rsqrt(jnp.mean(shifted * shifted, -1, keepdims=True) + EPSILON)
        return shifted * inverse, inverse

    def values_of(p, b):
        wide = vs[p, block(b)].astype(F32)
        return jnp.where(low_lane, wide, 1.0), jnp.where(low_lane, 1.0, wide)

    def keys_block(b, _):
        scaled, _inv = normalized(tok[block(b)].astype(F32))
        normed = (scaled * g1[...]).astype(BF16)
        n1s[block(b)] = normed
        key = (dot(normed, wqkv[:, width : 2 * width]) * shrink).astype(BF16)
        val = dot(normed, wqkv[:, 2 * width :]).astype(BF16)
        end = ending(b)
        keep = keep_of(b)
        for p in range(pairs):
            kp = key[:, p * pw : (p + 1) * pw]
            ks[p, block(b)] = kp
            vs[p, block(b)] = val[:, p * pw : (p + 1) * pw]
            feat = features_of(kp, p)
            phk[p, block(b)] = feat
            wide = val[:, p * pw : (p + 1) * pw].astype(F32)
            even = jnp.where(end, jnp.where(low_lane, wide, 1.0), 0.0).astype(BF16)
            odd = jnp.where(end, jnp.where(low_lane, 1.0, wide), 0.0).astype(BF16)
            ue = dot_lt(even, feat[:, :feat_n])
            uo = dot_lt(odd, feat[:, feat_n:])
            lst[b + 1, p, :pw] = keep * lst[b, p, :pw] + jnp.where(low_row, ue, uo)
            lst[b + 1, p, pw : pw + 8] = keep * lst[b, p, pw : pw + 8] + ue[hw : hw + 8]
            lst[b + 1, p, pw + 8 :] = keep * lst[b, p, pw + 8 :] + uo[:8]
        return 0

    lax.fori_loop(0, nb, keys_block, 0)

    def chf_handle(p):
        @pl.when(t > 0)
        def _():
            chf_copy(p).wait_recv()

        @pl.when(t < tn - 1)
        def _():
            chf_out[p] = (lst[nb, p] + passing * chf_in[p].astype(F32)).astype(BF16)
            chf_copy(p).start()

    @pl.when(t == 0)
    def _():
        for p in range(pairs):
            chf_handle(p)

    forward_lag = jnp.minimum(2 * (t - 1), pairs)

    def forward_slot(k):
        p = k - forward_lag

        @pl.when((t > 0) & (p >= 0) & (p < pairs))
        def _():
            chf_handle(p)

    def queries_block(b, _):
        forward_slot(b)
        query = (dot(n1s[block(b)], wqkv[:, :width]) * shrink).astype(BF16)
        for p in range(pairs):
            qp = query[:, p * pw : (p + 1) * pw]
            qs[p, block(b)] = qp
            phq[p, block(b)] = features_of(qp, p)
        return 0

    lax.fori_loop(0, nb, queries_block, 0)
    for k in range(nb, pairs):
        forward_slot(k)

    def state_halves(state):
        top = state[:pw]
        even = jnp.where(low_row, top, jnp.broadcast_to(state[pw : pw + 1], top.shape)).astype(BF16)
        odd = jnp.where(low_row, jnp.broadcast_to(state[pw + 8 : pw + 9], top.shape), top).astype(BF16)
        return even, odd

    def attend_pair(p, _):
        forward_slot(pairs + p)

        @pl.when((p >= 1) & (p < tn))
        def _():
            k = jnp.maximum(p, 1)
            wz_copy(k).wait()
            wc_copy(k).start()

        incoming = chf_in[p].astype(F32)
        for b in range(nb):
            first_pass = jnp.where(before == prev_of(b), 1.0, 0.0)
            state = (lst[b, p] + first_pass * incoming).astype(BF16)
            sb[b, p] = state
            se, so = state_halves(state.astype(F32))
            reach = reached(b)
            ve, vo = values_of(p, b)
            outs = []
            for o, (val, st) in enumerate(((ve, se), (vo, so))):
                fq = phq[p, block(b), o * feat_n : (o + 1) * feat_n]
                fk = phk[p, block(b), o * feat_n : (o + 1) * feat_n]
                scores = jnp.where(mask[b] > 0, dot_rt(fq, fk), 0.0).astype(BF16)
                outs.append(
                    dot(scores, val.astype(BF16)) + jnp.where(reach, dot_rt(fq, st), 0.0)
                )
            inverse = 1.0 / jnp.where(low_lane, outs[1], outs[0])
            rsw_s[block(b), lanes(p)] = inverse
            num = jnp.where(low_lane, outs[0], outs[1])
            attn[block(b), lanes(p)] = (num * pltpu.roll(inverse, hw, 1)).astype(BF16)
        return 0

    lax.fori_loop(0, pairs, attend_pair, 0)
    for k in range(pairs, tn):
        wz_copy(k).wait()
        wc_copy(k).start()

    def hidden_block(b, _):
        h1 = tok[block(b)].astype(F32) + (dot(attn[block(b)], wout[...]) + bout[...])
        scaled, inverse = normalized(h1)
        xh2[block(b)] = scaled
        rstd2[block(b)] = inverse
        n2s[block(b)] = (scaled * g2[...]).astype(BF16)
        facc[block(b)] = h1 + bdn[...]
        return 0

    lax.fori_loop(0, nb, hidden_block, 0)

    def feed_chunk(s, _):
        @pl.when(s > 0)
        def _():
            k = jnp.maximum(s, 1)
            wc_copy(k).wait_send()
            other = wfull.at[k, 1 - cb]
            remote(other, other, wc_s.at[k - 1], wc_r.at[k - 1], core_dev).wait_recv()

        def rows_block(b, total):
            w_in = wfull[s, 0, :width]
            w_dn = wfull[s, 1, :width]
            u = dot(n2s[block(b)], w_in) + wfull[s, 0, width : width + 16].astype(F32)[:1]
            u2 = u * u
            th = jnp.tanh(u * (SQRT_2_OVER_PI + SQRT_2_OVER_PI * CUBIC * u2))
            half = 0.5 + 0.5 * th
            act = (u * half).astype(BF16)
            slope = half + (0.5 * u) * (1.0 - th * th) * (
                SQRT_2_OVER_PI + 3.0 * SQRT_2_OVER_PI * CUBIC * u2
            )
            ad[0, block(b)] = act
            facc[block(b)] += dot(act, w_dn)
            du = (slope * dot_rt(cot[block(b)], w_dn)).astype(BF16)
            ad[1, block(b)] = du
            back = dot_rt(du, w_in)

            @pl.when(s == 0)
            def _():
                igrad[block(b)] = back

            @pl.when(s > 0)
            def _():
                igrad[block(b)] += back

            return total + jnp.sum(du.astype(F32), 0, keepdims=True)

        total = lax.fori_loop(0, nb, rows_block, jnp.zeros((1, wdn.shape[0]), F32))
        vec[pl.ds(4 + s, 1)] = total

        @pl.when(s >= 1)
        def _():
            a_finish(jnp.maximum(s - 1, 0))

        @pl.when(s >= 2)
        def _():
            b_finish(jnp.maximum(s - 2, 0))

        @pl.when(s >= 3)
        def _():
            c_start(jnp.maximum(s - 2, 1))

        gbuf[s, 0] = dot_lt(n2s[...], ad[1]).astype(BF16)
        gbuf[s, 1] = dot_lt(cot[...], ad[0]).astype(BF16)
        a_start(s)
        return 0

    lax.fori_loop(0, tn, feed_chunk, 0)

    def norm_back(dn, gain, scaled, inverse):
        g = dn * gain
        inner = jnp.mean(g, -1, keepdims=True)
        cross = jnp.mean(g * scaled, -1, keepdims=True)
        return inverse * (g - inner - scaled * cross)

    lane_id = iota((BR, pw), 1)

    def branch_block(b, carry):
        gl2, gbo, gbd = carry
        layer_out[block(b)] = facc[block(b)].astype(BF16)
        dy = cot[block(b)].astype(F32)
        dn2 = igrad[block(b)]
        scaled = xh2[block(b)]
        dh1 = dy + norm_back(dn2, g2[...], scaled, rstd2[block(b)])
        igrad[block(b)] = dh1
        dob = dh1.astype(BF16)
        n2s[block(b)] = dob
        dattn = dot_rt(dob, wout[...])
        for p in range(pairs):
            da = dattn[:, p * pw : (p + 1) * pw]
            inverse = rsw_s[block(b), p * pw : (p + 1) * pw]
            dnum = da * pltpu.roll(inverse, hw, 1)
            prod = da * attn[block(b), p * pw : (p + 1) * pw].astype(F32)
            high = prod.astype(BF16)
            rest = (prod - high.astype(F32)).astype(BF16)
            dden = -dot(jnp.concatenate([high, rest], 1), bsw[...]) * inverse
            dhi = dden.astype(BF16).astype(F32)
            dlo = dden - dhi
            even = jnp.where(lane_id == hw, dhi, jnp.where(lane_id == hw + 1, dlo, 0.0))
            odd = jnp.where(lane_id == 0, dhi, jnp.where(lane_id == 1, dlo, 0.0))
            ad[0, block(b), p * pw : (p + 1) * pw] = jnp.where(low_lane, dnum, even).astype(BF16)
            ad[1, block(b), p * pw : (p + 1) * pw] = jnp.where(low_lane, odd, dnum).astype(BF16)
        return (
            gl2 + jnp.sum(dn2 * scaled, 0, keepdims=True),
            gbo + jnp.sum(dob.astype(F32), 0, keepdims=True),
            gbd + jnp.sum(dy, 0, keepdims=True),
        )

    zero_row = jnp.zeros((1, width), F32)
    gl2, gbo, gbd = lax.fori_loop(0, nb, branch_block, (zero_row,) * 3)
    vec[1:2] = gbo
    vec[2:3] = gl2
    vec[3:4] = gbd
    a_finish(tn - 1)
    for s in range(max(tn - 2, 0), tn - 1):
        b_finish(s)
        if s >= 1:
            c_start(s)
    gbuf[tn, 0] = dot_lt(attn[...], n2s[...]).astype(BF16)

    half_blocks = nb // 2

    def grad_at(j, b):
        if isinstance(b, int):
            return j, b // half_blocks, pl.ds((b % half_blocks) * BR, BR)
        rows = pl.ds(pl.multiple_of(lax.rem(b, half_blocks) * BR, BR), BR)
        return j, lax.div(b, half_blocks), rows

    def weight_grad(j):
        half = rows_n // 2
        total = dot_lt(n1s[:half], wfull[j, 0, :half])
        return (total + dot_lt(n1s[half:], wfull[j, 1, :half])).astype(BF16)

    def arg_back(darg, x, p):
        both = dot_rt(darg, featx[p, : 2 * pw])
        return (both[:, :pw] + (2.0 * x.astype(F32)) * both[:, pw:]) * shrink

    def chb_handle(p):
        @pl.when(t < tn - 1)
        def _():
            chb_copy(p).wait_recv()

        @pl.when(t > 0)
        def _():
            own = lst[nb - 1, p]
            for b in range(nb - 2, -1, -1):
                own = keep_of(b) * own + lst[b, p]
            chb_out[p] = (own + passing * chb_in[p].astype(F32)).astype(BF16)
            chb_copy(p).start()

    backward_lag = jnp.minimum(2 * (tn - 1 - t), pairs)

    def backward_slot(k):
        p = k - backward_lag

        @pl.when((p >= 0) & (p < pairs))
        def _():
            chb_handle(p)

    def query_pair(p, _):
        for b in range(nb):
            se, so = state_halves(sb[b, p].astype(F32))
            reach = reached(b)
            ve, vo = values_of(p, b)
            dargs, grads = [], []
            for o, (val, st) in enumerate(((ve, se), (vo, so))):
                dn = ad[o, block(b), lanes(p)]
                cdn = jnp.where(reach, dn.astype(F32), 0.0).astype(BF16)
                fq = phq[p, block(b), o * feat_n : (o + 1) * feat_n]
                fk = phk[p, block(b), o * feat_n : (o + 1) * feat_n]
                da = jnp.where(mask[b] > 0, dot_rt(dn, val.astype(BF16)), 0.0).astype(BF16)
                dfq = dot(da, fk) + dot(cdn, st)
                dargs.append((dfq * fq.astype(F32)).astype(BF16))
                grads.append(dot_lt(cdn, fq))
            ge, go = grads
            lst[b, p, :pw] = jnp.where(low_row, ge, go)
            lst[b, p, pw : pw + 8] = jnp.broadcast_to(ge[hw : hw + 1] + ge[hw + 1 : hw + 2], (8, feat_n))
            lst[b, p, pw + 8 :] = jnp.broadcast_to(go[0:1] + go[1:2], (8, feat_n))
            wfull[grad_at(0, b) + (lanes(p),)] = arg_back(
                jnp.concatenate(dargs, 1), qs[p, block(b)], p
            ).astype(BF16)
        backward_slot(p)

        @pl.when(p == 0)
        def _():
            b_finish(tn - 1)
            if tn > 1:
                c_start(tn - 1)

        @pl.when(p == 1)
        def _():
            c_finish()

        @pl.when(p == 3)
        def _():
            d_finish(0)

        return 0

    lax.fori_loop(0, pairs, query_pair, 0)
    gbuf[tn, 1] = weight_grad(0)
    a_start(tn)

    def key_pair(p, _):
        backward_slot(pairs + p)
        grad = chb_in[p].astype(F32)
        for b in range(nb - 1, -1, -1):
            top = grad[:pw]
            halves = []
            for o in range(2):
                dz = jnp.broadcast_to(grad[pw + 8 * o : pw + 8 * o + 1], top.shape)
                dz_hi = dz.astype(BF16).astype(F32)
                at = hw * (1 - o)
                filler = jnp.where(row_id == at, dz_hi, jnp.where(row_id == at + 1, dz - dz_hi, 0.0))
                halves.append(
                    (jnp.where(low_row, top, filler) if o == 0 else jnp.where(low_row, filler, top)).astype(BF16)
                )
            end = ending(b)
            ve, vo = values_of(p, b)
            dargs, dvs = [], []
            for o, (val, ds) in enumerate(((ve, halves[0]), (vo, halves[1]))):
                dn = ad[o, block(b), lanes(p)]
                fq = phq[p, block(b), o * feat_n : (o + 1) * feat_n]
                fk = phk[p, block(b), o * feat_n : (o + 1) * feat_n]
                at = jnp.where(maskt[b] > 0, dot_rt(fk, fq), 0.0).astype(BF16)
                dat = jnp.where(maskt[b] > 0, dot_rt(val.astype(BF16), dn), 0.0).astype(BF16)
                ev = jnp.where(end, val, 0.0).astype(BF16)
                dfk = dot(dat, fq) + dot(ev, ds)
                dargs.append((dfk * fk.astype(F32)).astype(BF16))
                dvs.append(dot(at, dn) + jnp.where(end, dot_rt(fk, ds), 0.0))
            wfull[grad_at(1, b) + (lanes(p),)] = arg_back(
                jnp.concatenate(dargs, 1), ks[p, block(b)], p
            ).astype(BF16)
            wfull[grad_at(2, b) + (lanes(p),)] = jnp.where(
                low_lane, dvs[0], dvs[1]
            ).astype(BF16)
            if b > 0:
                grad = keep_of(b) * grad + lst[b, p]

        @pl.when(p == 0)
        def _():
            a_finish(tn)

        @pl.when(p == 2)
        def _():
            ca_start(0)

        @pl.when(p == 3)
        def _():
            e_finish(0)

        return 0

    lax.fori_loop(0, pairs, key_pair, 0)

    @pl.when(t < tn - 1)
    def _():
        for p in range(pairs):
            chf_copy(p).wait_send()

    @pl.when(t > 0)
    def _():
        for p in range(pairs):
            chb_copy(p).wait_send()

    gbuf[tn + 1, 0] = weight_grad(1)
    gbuf[tn + 1, 1] = weight_grad(2)
    a_start(tn + 1)
    ca_finish(0)

    def input_block(b, gl1):
        dn1 = dot_rt(wfull[grad_at(0, b)], wqkv[:, :width])
        for j in range(1, 3):
            dn1 = dn1 + dot_rt(wfull[grad_at(j, b)], wqkv[:, j * width : (j + 1) * width])
        scaled, inverse = normalized(tok[block(b)].astype(F32))
        igrad[block(b)] += norm_back(dn1, g1[...], scaled, inverse)
        return gl1 + jnp.sum(dn1 * scaled, 0, keepdims=True)

    vec[0:1] = lax.fori_loop(0, nb, input_block, zero_row)
    va_copy = remote(vec, va, va_s, va_r, core_dev)
    va_copy.start()
    a_finish(tn + 1)
    d_finish(1)
    va_copy.wait()
    vb[0] = vec[...] + va[...]
    vb_copies = [remote(vb.at[0], vb.at[k], vb_s.at[k - 1], vb_r.at[k - 1], peer_dev(k)) for k in range(1, npeer)]
    for copy in vb_copies:
        copy.start()
    ca_start(1)
    for copy in vb_copies:
        copy.wait()
    total = vb[xor(q, 0, npeer)]
    for j in range(1, npeer):
        total = total + vb[xor(q, j, npeer)]
    vc[0] = total
    vc_copies = [remote(vc.at[0], vc.at[k], vc_s.at[k - 1], vc_r.at[k - 1], z_dev(k)) for k in range(1, tn)]
    for copy in vc_copies:
        copy.start()
    ca_finish(1)
    for copy in vc_copies:
        copy.wait()
    total = vc[xor(t, 0, tn)]
    for j in range(1, tn):
        total = total + vc[xor(t, j, tn)]
    own = vc[0, 4:5]
    for k in range(1, tn):
        own = own + vc[k, 4 + k : 5 + k]
    vec_out[...] = total
    vec_out[4:5] = own
    e_finish(1)
    d_finish(2)
    e_finish(2)


def local(
    tn,
    dpn,
    tokens,
    cotangent,
    seq_lengths,
    features,
    ln1_gain,
    w_qkv,
    w_out,
    b_out,
    ln2_gain,
    w_in,
    b_in,
    w_down,
    b_down,
):
    rows_n, width = tokens.shape
    heads, hw, feat_n = features.shape
    pairs, pw, nb = heads // 2, 2 * hw, rows_n // BR
    ffl = w_in.shape[1]
    npeer = dpn // 2
    rp = width // npeer
    vrows = -(-(4 + tn) // 8) * 8
    dma = pltpu.SemaphoreType.DMA
    vmem = pl.BlockSpec(memory_space=pltpu.VMEM)

    def scratch(shape, dtype=BF16):
        return pltpu.VMEM(shape, dtype)

    out = pl.pallas_call(
        functools.partial(layer_kernel, tn, dpn),
        out_shape=(
            jax.ShapeDtypeStruct((rows_n, width), BF16),
            jax.ShapeDtypeStruct((rows_n, width), F32),
            jax.ShapeDtypeStruct((3, 2, width, width), BF16),
            jax.ShapeDtypeStruct((vrows, width), F32),
        ),
        in_specs=[pl.BlockSpec(memory_space=pltpu.SMEM)] + [vmem] * 12,
        out_specs=(vmem,) * 4,
        scratch_shapes=[
            scratch((tn, 2, width + 16, ffl)),
            scratch((rows_n, width)),
            scratch((pairs, rows_n, pw)),
            scratch((pairs, rows_n, pw)),
            scratch((pairs, rows_n, pw)),
            scratch((pairs, rows_n, 2 * feat_n)),
            scratch((pairs, rows_n, 2 * feat_n)),
            scratch((pairs, 3 * pw, 2 * feat_n)),
            scratch((2 * pw, pw)),
            scratch((nb, BR, BR), F32),
            scratch((nb, BR, BR), F32),
            scratch((nb + 1, pairs, pw + 16, feat_n), F32),
            scratch((nb, pairs, pw + 16, feat_n)),
            scratch((rows_n, width), F32),
            scratch((rows_n, width)),
            scratch((rows_n, width), F32),
            scratch((rows_n, width), F32),
            scratch((rows_n, 1), F32),
            scratch((rows_n, width)),
            scratch((2, rows_n, width)),
            scratch((pairs, pw + 16, feat_n)),
            scratch((pairs, pw + 16, feat_n)),
            scratch((pairs, pw + 16, feat_n)),
            scratch((pairs, pw + 16, feat_n)),
            scratch((tn + 2, 2, width, width)),
            scratch((2, width, width)),
            scratch((4, npeer - 1, rp, width)),
            scratch((tn - 1, rp, width)),
            scratch((2, tn, rp, width)),
            scratch((vrows, width), F32),
            scratch((vrows, width), F32),
            scratch((npeer, vrows, width), F32),
            scratch((tn, vrows, width), F32),
            dma((tn - 1,)),
            dma((tn - 1,)),
            dma((tn - 1,)),
            dma((tn - 1,)),
            dma((pairs,)),
            dma((pairs,)),
            dma((pairs,)),
            dma((pairs,)),
            dma((tn + 2,)),
            dma((tn + 2,)),
            dma((tn + 2, npeer - 1)),
            dma((tn + 2, npeer - 1)),
            dma((3, tn - 1)),
            dma((3, tn - 1)),
            dma((3, npeer - 1)),
            dma((3, npeer - 1)),
            dma((3,)),
            dma((3,)),
            dma(()),
            dma(()),
            dma((npeer - 1,)),
            dma((npeer - 1,)),
            dma((tn - 1,)),
            dma((tn - 1,)),
        ],
        compiler_params=pltpu.CompilerParams(
            collective_id=0, has_side_effects=True, vmem_limit_bytes=63 * 1024 * 1024
        ),
    )(
        seq_lengths,
        tokens,
        cotangent,
        features,
        ln1_gain[None],
        w_qkv,
        w_out,
        b_out.astype(F32)[None],
        ln2_gain[None],
        w_in,
        b_in[None],
        w_down,
        b_down.astype(F32)[None],
    )
    layer_out, input_grad, fin, vec = out
    fin = fin.astype(F32)
    return (
        layer_out,
        input_grad,
        vec[0],
        jnp.concatenate([fin[1, 1], fin[2, 0], fin[2, 1]], 1),
        fin[1, 0],
        vec[1],
        vec[2],
        fin[0, 0],
        vec[4],
        fin[0, 1].T,
        vec[3],
    )


def solution(mesh):
    tn, dpn = mesh.shape["tensor"], mesh.shape["dp"]
    rows = P(("dp", "tensor"), None)
    return jax.shard_map(
        functools.partial(local, tn, dpn),
        mesh=mesh,
        in_specs=(
            rows,
            rows,
            P("dp", None),
            P(),
            P(),
            P(),
            P(),
            P(),
            P(),
            P(None, "tensor"),
            P("tensor"),
            P("tensor", None),
            P(),
        ),
        out_specs=(
            rows,
            rows,
            P(),
            P(),
            P(),
            P(),
            P(),
            P(None, "tensor"),
            P("tensor"),
            P("tensor", None),
            P(),
        ),
        check_vma=False,
    )
```

```python
import functools

import jax
import jax.numpy as jnp
from jax import lax
from jax.experimental import pallas as pl
from jax.experimental.pallas import tpu as pltpu
from jax.sharding import PartitionSpec as P

MESH = pl.DeviceIdType.MESH
F32 = jnp.float32
BF16 = jnp.bfloat16
EPSILON = 1e-05
BR = 256
WR = 512
SQRT_2_OVER_PI = 0.7978845608028654
CUBIC = 0.044715


def dot(a, b):
    return jnp.dot(a, b, preferred_element_type=F32)


def dot_rt(a, b):
    return lax.dot_general(a, b, (((1,), (1,)), ((), ())), preferred_element_type=F32)


def dot_lt(a, b):
    return lax.dot_general(a, b, (((0,), (0,)), ((), ())), preferred_element_type=F32)


def xor(a, b, size):
    out, bit = 0, 1
    while bit < size:
        out = out + bit * lax.rem(lax.div(a, bit) + (b // bit if isinstance(b, int) else lax.div(b, bit)), 2)
        bit *= 2
    return out


def iota(shape, axis):
    return lax.broadcasted_iota(jnp.int32, shape, axis)


def layer_kernel(
    tn,
    dpn,
    lens,
    tok_h,
    cot_h,
    feats_h,
    g1,
    wqkv_h,
    wout_h,
    biases,
    g2,
    win_h,
    wdn_h,
    layer_h,
    igrad_h,
    fin,
    fink,
    vec_out,
    tok,
    cot,
    feats,
    wqkv,
    wout,
    layer_out,
    igrad,
    wfull,
    bfull,
    n1s,
    qs,
    ks,
    vs,
    phq,
    phk,
    featx,
    bsw,
    mask,
    maskt,
    lst,
    sb,
    rsw_s,
    attn,
    facc,
    xh2,
    rstd2,
    n2s,
    ad,
    chf_in,
    chf_out,
    chb_in,
    chb_out,
    gbuf,
    ra,
    rb,
    rc,
    kbuf,
    kra,
    krb,
    krc,
    vec,
    va,
    vb,
    vc,
    in_s,
    out_s,
    bz_s,
    bz_r,
    wz_s,
    wz_r,
    wx_s,
    wx_r,
    wc_s,
    wc_r,
    chf_s,
    chf_r,
    chb_s,
    chb_r,
    a_s,
    a_r,
    b_s,
    b_r,
    c_s,
    c_r,
    d_s,
    d_r,
    e_s,
    e_r,
    ka_s,
    ka_r,
    kb_s,
    kb_r,
    kc_s,
    kc_r,
    kd_s,
    kd_r,
    ke_s,
    ke_r,
    va_s,
    va_r,
    vb_s,
    vb_r,
    vc_s,
    vc_r,
):
    rows_n, width = tok.shape
    heads, hw, feat_n = feats.shape
    pairs = heads // 2
    pw = 2 * hw
    nb = rows_n // BR
    seqs = lens.shape[1]
    shrink = hw ** (-0.25)
    featscale = feat_n ** (-0.5)
    npeer = dpn // 2
    rp = width // npeer

    dp = lax.axis_index("dp")
    t = lax.axis_index("tensor")
    cb = lax.rem(dp, 2)
    q = lax.div(dp, 2)
    core_dev = (dp + 1 - 2 * cb, t)

    peers = [xor(q, k, npeer) for k in range(npeer)]
    zs = [xor(t, k, tn) for k in range(tn)]

    def peer_dev(k):
        return (2 * peers[k] + cb, t)

    def z_dev(k):
        return (dp, zs[k])

    row_starts = [pl.multiple_of(peer * rp, rp) for peer in peers]

    def own_rows():
        return pl.ds(row_starts[0], rp)

    def peer_rows(k):
        return pl.ds(row_starts[k], rp)

    def load(i, src, dst):
        return pltpu.make_async_copy(src, dst, in_s.at[i])

    loads = {
        "win": load(0, win_h, wfull.at[0, 0]),
        "wdn": load(1, wdn_h, wfull.at[0, 1]),
        "tok": load(2, tok_h, tok),
        "wqkv": load(3, wqkv_h, wqkv),
        "feats": load(4, feats_h, feats),
        "wout": load(5, wout_h, wout),
        "cot": load(6, cot_h, cot),
    }
    for copy in loads.values():
        copy.start()

    def store_layer():
        return pltpu.make_async_copy(layer_out, layer_h, out_s.at[0])

    def store_grad(b):
        rows = pl.ds(pl.multiple_of(b * WR, WR), WR)
        return pltpu.make_async_copy(igrad.at[rows], igrad_h.at[rows], out_s.at[1 + b])

    bar = pltpu.get_barrier_semaphore()
    targets = [core_dev] + [peer_dev(k) for k in range(1, npeer)] + [z_dev(k) for k in range(1, tn)]
    for dev in targets:
        pl.semaphore_signal(bar, inc=1, device_id=dev, device_id_type=MESH)

    def remote(src, dst, ss, rs, dev):
        return pltpu.make_async_remote_copy(
            src_ref=src, dst_ref=dst, send_sem=ss, recv_sem=rs, device_id=dev, device_id_type=MESH
        )

    def bz_copy(k):
        return remote(bfull.at[0], bfull.at[k], bz_s.at[k - 1], bz_r.at[k - 1], z_dev(k))

    def wz_copy(k):
        return remote(
            wfull.at[0, cb, own_rows()], wfull.at[k, cb, own_rows()], wz_s.at[k - 1], wz_r.at[k - 1], z_dev(k)
        )

    def wx_copy(k, j):
        here = wfull.at[k, cb, own_rows()]
        return remote(here, here, wx_s.at[k - 1, j - 1], wx_r.at[k - 1, j - 1], peer_dev(j))

    def wx_recv(k, j):
        here = wfull.at[k, cb, peer_rows(j)]
        return remote(here, here, wx_s.at[k - 1, j - 1], wx_r.at[k - 1, j - 1], peer_dev(j))

    def wc_copy(k):
        return remote(wfull.at[k, cb], wfull.at[k, cb], wc_s.at[k - 1], wc_r.at[k - 1], core_dev)

    def wc_recv(k):
        here = wfull.at[k, 1 - cb]
        return remote(here, here, wc_s.at[k - 1], wc_r.at[k - 1], core_dev)

    def w_spread(k):
        wz_copy(k).wait()
        for j in range(1, npeer):
            wx_copy(k, j).start()

    def w_swap(k):
        for j in range(1, npeer):
            wx_copy(k, j).wait_send()
            wx_recv(k, j).wait_recv()
        wc_copy(k).start()

    levels = (tn - 1).bit_length()
    up_first = (1, 3, 5, 8), (9, 11, 14, 16)

    def up_due(at, p):
        return up_first[at - 1][p % 4] if at < 3 and p < 4 else 14 + p

    def down_due(hops, p):
        due = min(3 * hops + p, 8 + 2 * p)
        return due + due % 2 if due > 8 else due

    def up_copy(p):
        return remote(chf_out.at[p], chf_in.at[p], chf_s.at[p], chf_r.at[p], (dp, lax.rem(t + 1, tn)))

    def up_handle(p):
        @pl.when(t > 0)
        def _():
            up_copy(p).wait_recv()

        chf_out[p] = (lst[nb, p] + passing * chf_in[p].astype(F32)).astype(BF16)
        up_copy(p).start()

    def up_slots(k, low, high):
        for at in range(1, tn - 1):
            for p in range(pairs):
                if low <= up_due(at, p) < high:

                    @pl.when((t == at) & (k == up_due(at, p)))
                    def _(p=p):
                        up_handle(p)

    def down_copy(p):
        return remote(chb_out.at[p], chb_in.at[p], chb_s.at[p], chb_r.at[p], (dp, lax.rem(t + tn - 1, tn)))

    def down_handle(p):
        @pl.when(t < tn - 1)
        def _():
            down_copy(p).wait_recv()

        own = lst[nb - 1, p]
        for b in range(nb - 2, -1, -1):
            own = keep_of(b) * own + lst[b, p]
        chb_out[p] = (own + passing * chb_in[p].astype(F32)).astype(BF16)
        down_copy(p).start()

    def down_slots(k, low, high):
        for hops in range(tn - 1):
            for p in range(pairs):
                if low <= down_due(hops, p) < high:

                    @pl.when((t == tn - 1 - hops) & (k == down_due(hops, p)))
                    def _(p=p):
                        down_handle(p)

    def a_copy(s):
        s = jnp.int32(s)
        return remote(gbuf.at[s, 1 - cb], ra.at[lax.rem(s, 2)], a_s.at[s], a_r.at[s], core_dev)

    def b_copy(s, k):
        s = jnp.int32(s)
        return remote(gbuf.at[s, cb, peer_rows(k)], rb.at[lax.rem(s, 4), k - 1], b_s.at[s, k - 1], b_r.at[s, k - 1], peer_dev(k))

    def c_copy(s):
        return remote(gbuf.at[s, cb, own_rows()], rc.at[s - 1], c_s.at[s - 1], c_r.at[s - 1], z_dev(s & -s))

    def d_copy(k):
        here = fin.at[cb, own_rows()]
        return remote(here, here, d_s.at[k - 1], d_r.at[k - 1], peer_dev(k))

    def d_recv(k):
        here = fin.at[cb, peer_rows(k)]
        return remote(here, here, d_s.at[k - 1], d_r.at[k - 1], peer_dev(k))

    def e_copy():
        return remote(fin.at[cb], fin.at[cb], e_s, e_r, core_dev)

    def e_recv():
        return remote(fin.at[1 - cb], fin.at[1 - cb], e_s, e_r, core_dev)

    def ka_copy(i):
        i = jnp.int32(i)
        return remote(kbuf.at[i, 1 - cb], kra.at[lax.rem(i, 4)], ka_s.at[i], ka_r.at[i], core_dev)

    def kb_copy(i, k):
        return remote(
            kbuf.at[i, cb, peer_rows(k)], krb.at[i, k - 1], kb_s.at[i, k - 1], kb_r.at[i, k - 1], peer_dev(k)
        )

    def kc_copy(i, k):
        return remote(krc.at[i, 0], krc.at[i, k], kc_s.at[i, k - 1], kc_r.at[i, k - 1], z_dev(k))

    def ks_copy(i, l):
        return remote(
            krc.at[i, 2 * l], krc.at[i, 2 * l + 1], kc_s.at[i, l], kc_r.at[i, l], z_dev(1 << l)
        )

    def kd_copy(i, k):
        here = fink.at[i, cb, own_rows()]
        return remote(here, here, kd_s.at[i, k - 1], kd_r.at[i, k - 1], peer_dev(k))

    def kd_recv(i, k):
        here = fink.at[i, cb, peer_rows(k)]
        return remote(here, here, kd_s.at[i, k - 1], kd_r.at[i, k - 1], peer_dev(k))

    def ke_copy(i):
        return remote(fink.at[i, cb], fink.at[i, cb], ke_s.at[i], ke_r.at[i], core_dev)

    def ke_recv(i):
        return remote(fink.at[i, 1 - cb], fink.at[i, 1 - cb], ke_s.at[i], ke_r.at[i], core_dev)

    def a_start(s):
        a_copy(s).start()

    def a_finish(s):
        s = jnp.int32(s)
        a_copy(s).wait()
        gbuf[s, cb] = (gbuf[s, cb].astype(F32) + ra[lax.rem(s, 2)].astype(F32)).astype(BF16)
        for k in range(1, npeer):
            b_copy(s, k).start()

    def b_sum(s):
        s = jnp.int32(s)
        for k in range(1, npeer):
            b_copy(s, k).wait()
        total = gbuf[s, cb, own_rows()].astype(F32)
        for k in range(1, npeer):
            total = total + rb[lax.rem(s, 4), k - 1].astype(F32)
        return total.astype(BF16)

    def b_finish(s):
        gbuf[s, cb, own_rows()] = b_sum(s)

    def c_add(s):
        step = 1
        while step < (s & -s if s else tn):
            c_copy(s + step).wait()
            gbuf[s, cb, own_rows()] = (
                gbuf[s, cb, own_rows()].astype(F32) + rc[s + step - 1].astype(F32)
            ).astype(BF16)
            step *= 2

    def c_start(s):
        c_add(s)
        c_copy(s).start()

    def c_finish():
        total = gbuf[0, cb, own_rows()].astype(F32)
        step = 1
        while step < tn:
            c_copy(step).wait()
            total = total + rc[step - 1].astype(F32)
            step *= 2
        fin[cb, own_rows()] = total.astype(BF16)
        for k in range(1, npeer):
            d_copy(k).start()

    def d_finish():
        for k in range(1, npeer):
            d_copy(k).wait_send()
            d_recv(k).wait_recv()
        e_copy().start()

    def e_finish():
        e_copy().wait_send()
        e_recv().wait_recv()

    def k_a_start(i, both):
        kbuf[i, 0] = both[:, :pw].astype(BF16)
        kbuf[i, 1] = both[:, pw:].astype(BF16)
        ka_copy(i).start()

    def k_a_finish(i):
        i = jnp.int32(i)
        ka_copy(i).wait()
        kbuf[i, cb] = (kbuf[i, cb].astype(F32) + kra[lax.rem(i, 4)].astype(F32)).astype(BF16)
        for k in range(1, npeer):
            kb_copy(i, k).start()

    def k_b_sum(i):
        for k in range(1, npeer):
            kb_copy(i, k).wait()
        total = kbuf[i, cb, own_rows()].astype(F32)
        for k in range(1, npeer):
            total = total + krb[i, k - 1].astype(F32)
        krc[i, 0] = total.astype(BF16)

    def k_spread(i, total):
        fink[i, cb, own_rows()] = total.astype(BF16)
        for k in range(1, npeer):
            kd_copy(i, k).start()

    def k_b_finish(i):
        k_b_sum(i)
        for k in range(1, tn):
            kc_copy(i, k).start()

    def k_c_finish(i):
        for k in range(1, tn):
            kc_copy(i, k).wait()
        total = krc[i, zs[0]].astype(F32)
        for j in range(1, tn):
            total = total + krc[i, zs[j]].astype(F32)
        k_spread(i, total)

    def s_b_finish(i):
        k_b_sum(i)
        ks_copy(i, 0).start()

    def s_sum(i, l):
        ks_copy(i, l).wait()
        return krc[i, 2 * l].astype(F32) + krc[i, 2 * l + 1].astype(F32)

    def s_middle(i):
        for l in range(levels - 1):
            krc[i, 2 * l + 2] = s_sum(i, l).astype(BF16)
            ks_copy(i, l + 1).start()

    def s_c_finish(i):
        k_spread(i, s_sum(i, levels - 1))

    def k_d_finish(i):
        for k in range(1, npeer):
            kd_copy(i, k).wait_send()
            kd_recv(i, k).wait_recv()
        ke_copy(i).start()

    def k_e_finish(i):
        ke_copy(i).wait_send()
        ke_recv(i).wait_recv()

    offsets = [jnp.int32(0)]
    for c in range(1, seqs):
        offsets.append(offsets[-1] + lens[0, c - 1])
    first = t * rows_n

    def seg_at(r):
        seg = -1
        for off in offsets:
            seg = seg + jnp.where(r >= off, 1, 0)
        return seg

    def seg_array(shape, axis, start):
        places = iota(shape, axis) + start
        seg = jnp.full(shape, -1, jnp.int32)
        for off in offsets:
            seg = seg + jnp.where(places >= off, 1, 0)
        return seg

    before = seg_at(first - 1)
    closing = seg_at(first + rows_n - 1)
    passing = jnp.where(before == closing, 1.0, 0.0)

    def prev_of(b):
        return seg_at(first + b * BR - 1)

    def last_of(b):
        return seg_at(first + b * BR + BR - 1)

    def keep_of(b):
        return jnp.where(prev_of(b) == last_of(b), 1.0, 0.0)

    def ending(b):
        return seg_array((BR, pw), 0, first + b * BR) == last_of(b)

    def reached(b):
        return seg_array((BR, pw), 0, first + b * BR) == prev_of(b)

    def block(b):
        return pl.ds(pl.multiple_of(b * BR, BR), BR)

    nw = rows_n // WR

    def wide(b):
        return pl.ds(pl.multiple_of(b * WR, WR), WR)

    def lanes(p):
        return pl.ds(pl.multiple_of(p * pw, pw), pw)

    low_lane = iota((BR, pw), 1) < hw
    low_row = iota((pw, feat_n), 0) < hw
    row_id = iota((pw, feat_n), 0)

    loads["feats"].wait()
    featx[...] = jnp.zeros_like(featx)
    for p in range(pairs):
        for o in range(2):
            featx[p, o * hw : (o + 1) * hw, o * feat_n : (o + 1) * feat_n] = feats[2 * p + o]
            for rep in (1, 2):
                featx[
                    p, rep * pw + o * hw : rep * pw + (o + 1) * hw, o * feat_n : (o + 1) * feat_n
                ] = jnp.full((hw, feat_n), -0.5, BF16)
    ri, ci = iota((2 * pw, pw), 0), iota((2 * pw, pw), 1)
    swap = (lax.rem(ri, pw) < hw) != (ci < hw)
    bsw[...] = jnp.where(swap, 1.0, 0.0).astype(BF16)

    def build_mask(b, _):
        seg_i = seg_array((BR, BR), 0, first + b * BR)
        seg_j = seg_array((BR, BR), 1, first + b * BR)
        same = seg_i == seg_j
        i, j = iota((BR, BR), 0), iota((BR, BR), 1)
        mask[b] = jnp.where(same & (i >= j), 1.0, 0.0).astype(BF16)
        maskt[b] = jnp.where(same & (j >= i), 1.0, 0.0).astype(BF16)
        return 0

    lax.fori_loop(0, nb, build_mask, 0)
    lst[0] = jnp.zeros(lst.shape[1:], F32)
    vec[...] = jnp.zeros_like(vec)

    @pl.when(t == 0)
    def _():
        chf_in[...] = jnp.zeros_like(chf_in)

    @pl.when(t == tn - 1)
    def _():
        chb_in[...] = jnp.zeros_like(chb_in)

    loads["win"].wait()
    loads["wdn"].wait()
    pl.semaphore_wait(bar, len(targets))
    bfull[0] = jnp.broadcast_to(biases[1:2], bfull.shape[1:])
    for k in range(1, tn):
        bz_copy(k).start()
    wz_copy(1).start()
    wz_copy(2).start()

    def features_of(x, p):
        wide = x.astype(F32)
        square = wide * wide
        high = square.astype(BF16)
        rest = (square - high.astype(F32)).astype(BF16)
        arg = dot(jnp.concatenate([x, high, rest], 1), featx[p])
        return (jnp.exp(arg) * featscale).astype(BF16)

    def normalized(x):
        centre = jnp.mean(x, -1, keepdims=True)
        shifted = x - centre
        inverse = lax.rsqrt(jnp.mean(shifted * shifted, -1, keepdims=True) + EPSILON)
        return shifted * inverse, inverse

    def values_of(p, b):
        wide = vs[p, block(b)].astype(F32)
        return jnp.where(low_lane, wide, 1.0), jnp.where(low_lane, 1.0, wide)

    def keys_block(b, _):
        scaled, _inv = normalized(tok[wide(b)].astype(F32))
        normed = (scaled * g1[...]).astype(BF16)
        n1s[wide(b)] = normed
        key = (dot(normed, wqkv[:, width : 2 * width]) * shrink).astype(BF16)
        val = dot(normed, wqkv[:, 2 * width :]).astype(BF16)
        for p in range(pairs):
            ks[p, wide(b)] = key[:, p * pw : (p + 1) * pw]
            vs[p, wide(b)] = val[:, p * pw : (p + 1) * pw]

        return 0

    loads["tok"].wait()
    loads["wqkv"].wait()
    lax.fori_loop(0, nw, keys_block, 0)

    def state_pair(p, _):
        for b in range(nb):
            feat = features_of(ks[p, block(b)], p)
            phk[p, block(b)] = feat
            end = ending(b)
            ve, vo = values_of(p, b)
            ue = dot_lt(jnp.where(end, ve, 0.0).astype(BF16), feat[:, :feat_n])
            uo = dot_lt(jnp.where(end, vo, 0.0).astype(BF16), feat[:, feat_n:])
            keep = keep_of(b)
            lst[b + 1, p, :pw] = keep * lst[b, p, :pw] + jnp.where(low_row, ue, uo)
            lst[b + 1, p, pw : pw + 8] = keep * lst[b, p, pw : pw + 8] + ue[hw : hw + 8]
            lst[b + 1, p, pw + 8 :] = keep * lst[b, p, pw + 8 :] + uo[:8]

        @pl.when(t == 0)
        def _():
            up_handle(p)


        @pl.when(p == 1)
        def _():
            w_spread(1)

        return 0

    lax.fori_loop(0, pairs, state_pair, 0)

    def queries_block(b, _):
        up_slots(b, 0, nw)
        query = (dot(n1s[wide(b)], wqkv[:, :width]) * shrink).astype(BF16)
        for p in range(pairs):
            qs[p, wide(b)] = query[:, p * pw : (p + 1) * pw]

        @pl.when(b == 0)
        def _():
            for k in range(3, tn):
                wz_copy(k).start()

        return 0

    lax.fori_loop(0, nw, queries_block, 0)

    def features_pair(p, _):
        up_slots(nw + p, nw, nw + pairs)
        for b in range(nw):
            phq[p, wide(b)] = features_of(qs[p, wide(b)], p)
        return 0

    lax.fori_loop(0, pairs, features_pair, 0)

    def state_halves(state):
        top = state[:pw]
        even = jnp.where(low_row, top, jnp.broadcast_to(state[pw : pw + 1], top.shape)).astype(BF16)
        odd = jnp.where(low_row, jnp.broadcast_to(state[pw + 8 : pw + 9], top.shape), top).astype(BF16)
        return even, odd

    slot = nw + pairs

    def inside_half(i, _):
        up_slots(slot + i, slot, slot + 2 * pairs)
        p, half = lax.div(i, 2), lax.rem(i, 2)

        @pl.when(i == 2)
        def _():
            w_swap(1)

        @pl.when(i == 6)
        def _():
            w_spread(2)

        for c in range(nb // 2):
            b = half * (nb // 2) + c
            for o, (val, part) in enumerate(zip(values_of(p, b), (facc, xh2))):
                fq = phq[p, block(b), o * feat_n : (o + 1) * feat_n]
                fk = phk[p, block(b), o * feat_n : (o + 1) * feat_n]
                scores = jnp.where(mask[b].astype(F32) > 0, dot_rt(fq, fk), 0.0).astype(BF16)
                part[block(b), lanes(p)] = dot(scores, val.astype(BF16))
        return 0

    lax.fori_loop(0, 2 * pairs, inside_half, 0)

    def attend_pair(p, _):
        up_slots(slot + 2 * pairs + p, slot + 2 * pairs, slot + 3 * pairs)

        @pl.when(t == tn - 1)
        def _():
            up_copy(p).wait_recv()

        incoming = chf_in[p].astype(F32)
        for b in range(nb):
            first_pass = jnp.where(before == prev_of(b), 1.0, 0.0)
            state = (lst[b, p] + first_pass * incoming).astype(BF16)
            sb[b, p] = state
            reach = reached(b)
            outs = []
            for o, (st, part) in enumerate(zip(state_halves(state.astype(F32)), (facc, xh2))):
                fq = phq[p, block(b), o * feat_n : (o + 1) * feat_n]
                outs.append(part[block(b), lanes(p)] + jnp.where(reach, dot_rt(fq, st), 0.0))
            inverse = 1.0 / jnp.where(low_lane, outs[1], outs[0])
            rsw_s[block(b), lanes(p)] = inverse
            num = jnp.where(low_lane, outs[0], outs[1])
            attn[block(b), lanes(p)] = (num * pltpu.roll(inverse, hw, 1)).astype(BF16)
        return 0

    lax.fori_loop(0, pairs, attend_pair, 0)

    def hidden_block(b, _):
        h1 = tok[wide(b)].astype(F32) + (dot(attn[wide(b)], wout[...]) + biases[0:1])
        scaled, inverse = normalized(h1)
        xh2[wide(b)] = scaled
        rstd2[wide(b)] = inverse
        n2s[wide(b)] = (scaled * g2[...]).astype(BF16)
        facc[wide(b)] = h1 + biases[2:3]
        return 0

    loads["wout"].wait()
    lax.fori_loop(0, nw, hidden_block, 0)
    loads["cot"].wait()

    def feed_chunk(s, _):
        @pl.when(s > 0)
        def _():
            for k in range(1, tn):

                @pl.when(s == k)
                def _(k=k):
                    wc_copy(k).wait_send()
                    wc_recv(k).wait_recv()
                    bz_copy(k).wait()

        def rows_block(b, total):
            w_in = wfull[s, 0]
            w_dn = wfull[s, 1]
            u = dot(n2s[wide(b)], w_in) + bfull[s, 0:1]
            u2 = u * u
            th = jnp.tanh(u * (SQRT_2_OVER_PI + SQRT_2_OVER_PI * CUBIC * u2))
            half = 0.5 + 0.5 * th
            act = (u * half).astype(BF16)
            slope = half + (0.5 * u) * (1.0 - th * th) * (
                SQRT_2_OVER_PI + 3.0 * SQRT_2_OVER_PI * CUBIC * u2
            )
            ad[0, wide(b)] = act
            facc[wide(b)] += dot(act, w_dn)
            du = (slope * dot_rt(cot[wide(b)], w_dn)).astype(BF16)
            ad[1, wide(b)] = du
            back = dot_rt(du, w_in)

            @pl.when(s == 0)
            def _():
                igrad[wide(b)] = back

            @pl.when(s > 0)
            def _():
                igrad[wide(b)] += back

            @pl.when((s >= 1) & (b == 0))
            def _():
                a_finish(jnp.maximum(s - 1, 0))

            @pl.when((s == 0) & (b == 0))
            def _():
                w_swap(2)

            @pl.when((s == 0) & (b == nw - 1))
            def _():
                for k in range(3, tn):
                    w_spread(k)

            @pl.when((s == 2) & (b == nw - 1))
            def _():
                for k in range(3, tn):
                    w_swap(k)

            return total + jnp.sum(du.astype(F32), 0, keepdims=True)

        total = lax.fori_loop(0, nw, rows_block, jnp.zeros((1, wfull.shape[3]), F32))
        vec[pl.ds(4 + s, 1)] = total

        @pl.when(s >= 2)
        def _():
            b_finish(jnp.maximum(s - 2, 0))

        for k in range(1, tn - 2, 2):

            @pl.when(s == k + 2)
            def _(k=k):
                c_start(k)

        gbuf[s, 0] = dot_lt(n2s[...], ad[1]).astype(BF16)
        gbuf[s, 1] = dot_lt(cot[...], ad[0]).astype(BF16)
        a_start(s)
        return 0

    lax.fori_loop(0, tn, feed_chunk, 0)

    def norm_back(dn, gain, scaled, inverse):
        g = dn * gain
        inner = jnp.mean(g, -1, keepdims=True)
        cross = jnp.mean(g * scaled, -1, keepdims=True)
        return inverse * (g - inner - scaled * cross)

    lane_id = iota((BR, pw), 1)

    def branch_block(b, carry):
        gl2, gbo, gbd = carry
        layer_out[block(b)] = facc[block(b)].astype(BF16)
        dy = cot[block(b)].astype(F32)
        dn2 = igrad[block(b)]
        scaled = xh2[block(b)]
        dh1 = dy + norm_back(dn2, g2[...], scaled, rstd2[block(b)])
        igrad[block(b)] = dh1
        dob = dh1.astype(BF16)
        n2s[block(b)] = dob
        dattn = dot_rt(dob, wout[...])
        reach = reached(b)
        for p in range(pairs):
            da = dattn[:, p * pw : (p + 1) * pw]
            inverse = rsw_s[block(b), p * pw : (p + 1) * pw]
            dnum = da * pltpu.roll(inverse, hw, 1)
            prod = da * attn[block(b), p * pw : (p + 1) * pw].astype(F32)
            high = prod.astype(BF16)
            rest = (prod - high.astype(F32)).astype(BF16)
            dden = -dot(jnp.concatenate([high, rest], 1), bsw[...]) * inverse
            dhi = dden.astype(BF16).astype(F32)
            dlo = dden - dhi
            even = jnp.where(lane_id == hw, dhi, jnp.where(lane_id == hw + 1, dlo, 0.0))
            odd = jnp.where(lane_id == 0, dhi, jnp.where(lane_id == 1, dlo, 0.0))
            even = jnp.where(low_lane, dnum, even)
            odd = jnp.where(low_lane, odd, dnum)
            ad[0, block(b), p * pw : (p + 1) * pw] = even.astype(BF16)
            ad[1, block(b), p * pw : (p + 1) * pw] = odd.astype(BF16)
            ge = dot_lt(jnp.where(reach, even, 0.0).astype(BF16), phq[p, block(b), :feat_n])
            go = dot_lt(jnp.where(reach, odd, 0.0).astype(BF16), phq[p, block(b), feat_n:])
            lst[b, p, :pw] = jnp.where(low_row, ge, go)
            lst[b, p, pw : pw + 8] = jnp.broadcast_to(ge[hw : hw + 1] + ge[hw + 1 : hw + 2], (8, feat_n))
            lst[b, p, pw + 8 :] = jnp.broadcast_to(go[0:1] + go[1:2], (8, feat_n))

        @pl.when(b == 1)
        def _():
            a_finish(tn - 1)

        return (
            gl2 + jnp.sum(dn2 * scaled, 0, keepdims=True),
            gbo + jnp.sum(dob.astype(F32), 0, keepdims=True),
            gbd + jnp.sum(dy, 0, keepdims=True),
        )

    zero_row = jnp.zeros((1, width), F32)
    gl2, gbo, gbd = lax.fori_loop(0, nb, branch_block, (zero_row,) * 3)
    store_layer().start()
    vec[1:2] = gbo
    vec[2:3] = gl2
    vec[3:4] = gbd
    half_blocks = nb // 2

    def grad_at(j, b):
        if isinstance(b, int):
            return j, b // half_blocks, pl.ds((b % half_blocks) * BR, BR)
        rows = pl.ds(pl.multiple_of(lax.rem(b, half_blocks) * BR, BR), BR)
        return j, lax.div(b, half_blocks), rows

    half = rows_n // 2

    def weight_grad(ja, pa, jb, pb):
        total = 0.0
        for h in range(2):
            both = [wfull[j, h, :half, lanes(p)] for j, p in ((ja, pa), (jb, pb))]
            total = total + dot_lt(n1s[h * half : (h + 1) * half], jnp.concatenate(both, 1))
        return total

    def arg_back(darg, x, p):
        both = dot_rt(darg, featx[p, : 2 * pw])
        return (both[:, :pw] + (2.0 * x.astype(F32)) * both[:, pw:]) * shrink

    out_grad = dot_lt(attn[...], n2s[...])
    for i in range(2):
        k_a_start(i, out_grad[:, i * 2 * pw : (i + 1) * 2 * pw])

    def query_half(i, _):
        down_slots(i, 0, 2 * pairs)
        p, half = lax.div(i, 2), lax.rem(i, 2)
        for c in range(nb // 2):
            b = half * (nb // 2) + c
            se, so = state_halves(sb[b, p].astype(F32))
            reach = reached(b)
            ve, vo = values_of(p, b)
            dargs = []
            for o, (val, st) in enumerate(((ve, se), (vo, so))):
                dn = ad[o, block(b), lanes(p)]
                cdn = jnp.where(reach, dn.astype(F32), 0.0).astype(BF16)
                fq = phq[p, block(b), o * feat_n : (o + 1) * feat_n]
                fk = phk[p, block(b), o * feat_n : (o + 1) * feat_n]
                da = jnp.where(mask[b].astype(F32) > 0, dot_rt(dn, val.astype(BF16)), 0.0).astype(BF16)
                dfq = dot(da, fk) + dot(cdn, st)
                dargs.append((dfq * fq.astype(F32)).astype(BF16))
            wfull[grad_at(0, b) + (lanes(p),)] = arg_back(
                jnp.concatenate(dargs, 1), qs[p, block(b)], p
            ).astype(BF16)

        @pl.when(i == 1)
        def _():
            k_a_finish(0)
            k_a_finish(1)
            b_finish(tn - 2)

        @pl.when(i == 3)
        def _():
            k_a_start(2, weight_grad(0, 0, 0, 1))

        @pl.when(i == 5)
        def _():
            k_a_finish(2)
            b_finish(tn - 1)
            c_start(tn - 1)

        @pl.when(i == 7)
        def _():
            k_a_start(3, weight_grad(0, 2, 0, 3))
            s_b_finish(0)
            s_b_finish(1)

        return 0

    lax.fori_loop(0, 2 * pairs, query_half, 0)

    def key_pair(p, _):
        down_slots(2 * (pairs + p), 2 * pairs, 4 * pairs)

        @pl.when(t == 0)
        def _():
            down_copy(p).wait_recv()

        grad = chb_in[p].astype(F32)
        for b in range(nb - 1, -1, -1):
            top = grad[:pw]
            halves = []
            for o in range(2):
                dz = jnp.broadcast_to(grad[pw + 8 * o : pw + 8 * o + 1], top.shape)
                dz_hi = dz.astype(BF16).astype(F32)
                at = hw * (1 - o)
                filler = jnp.where(row_id == at, dz_hi, jnp.where(row_id == at + 1, dz - dz_hi, 0.0))
                halves.append(
                    (jnp.where(low_row, top, filler) if o == 0 else jnp.where(low_row, filler, top)).astype(BF16)
                )
            end = ending(b)
            ve, vo = values_of(p, b)
            dargs, dvs = [], []
            for o, (val, ds) in enumerate(((ve, halves[0]), (vo, halves[1]))):
                dn = ad[o, block(b), lanes(p)]
                fq = phq[p, block(b), o * feat_n : (o + 1) * feat_n]
                fk = phk[p, block(b), o * feat_n : (o + 1) * feat_n]
                at = jnp.where(maskt[b].astype(F32) > 0, dot_rt(fk, fq), 0.0).astype(BF16)
                dat = jnp.where(maskt[b].astype(F32) > 0, dot_rt(val.astype(BF16), dn), 0.0).astype(BF16)
                ev = jnp.where(end, val, 0.0).astype(BF16)
                dfk = dot(dat, fq) + dot(ev, ds)
                dargs.append((dfk * fk.astype(F32)).astype(BF16))
                dvs.append(dot(at, dn) + jnp.where(end, dot_rt(fk, ds), 0.0))
            wfull[grad_at(1, b) + (lanes(p),)] = arg_back(
                jnp.concatenate(dargs, 1), ks[p, block(b)], p
            ).astype(BF16)
            wfull[grad_at(2, b) + (lanes(p),)] = jnp.where(
                low_lane, dvs[0], dvs[1]
            ).astype(BF16)
            if b > 0:
                grad = keep_of(b) * grad + lst[b, p]

        k_a_start(4 + p, weight_grad(1, p, 2, p))

        @pl.when(p == 0)
        def _():
            k_a_finish(3)
            s_b_finish(2)
            for k in range(tn - 2, 0, -2):
                c_start(k)

        @pl.when(p >= 1)
        def _():
            k_a_finish(3 + p)

        @pl.when(p == 1)
        def _():
            s_middle(0)
            s_middle(1)
            s_b_finish(3)

        @pl.when(p == 2)
        def _():
            c_finish()
            s_middle(2)
            s_b_finish(4)

        @pl.when(p == 3)
        def _():
            s_c_finish(0)
            s_c_finish(1)
            s_middle(3)
            s_b_finish(5)

        return 0

    lax.fori_loop(0, pairs, key_pair, 0)

    @pl.when(t < tn - 1)
    def _():
        for p in range(pairs):
            up_copy(p).wait_send()

    @pl.when(t > 0)
    def _():
        for p in range(pairs):
            down_copy(p).wait_send()

    def input_block(b, gl1):
        dn1 = dot_rt(wfull[0, b, :WR], wqkv[:, :width])
        for j in range(1, 3):
            dn1 = dn1 + dot_rt(wfull[j, b, :WR], wqkv[:, j * width : (j + 1) * width])
        scaled, inverse = normalized(tok[wide(b)].astype(F32))
        igrad[wide(b)] += norm_back(dn1, g1[...], scaled, inverse)
        store_grad(b).start()

        @pl.when(b == 0)
        def _():
            k_a_finish(7)
            s_middle(4)
            s_c_finish(2)

        @pl.when(b == 1)
        def _():
            k_b_finish(6)
            d_finish()

        return gl1 + jnp.sum(dn1 * scaled, 0, keepdims=True)

    vec[0:1] = lax.fori_loop(0, nw, input_block, zero_row)
    va_copy = remote(vec, va, va_s, va_r, core_dev)
    va_copy.start()
    s_middle(5)
    s_c_finish(3)
    va_copy.wait()
    vb[0] = vec[...] + va[...]
    vb_copies = [remote(vb.at[0], vb.at[k], vb_s.at[k - 1], vb_r.at[k - 1], peer_dev(k)) for k in range(1, npeer)]
    for copy in vb_copies:
        copy.start()
    k_b_finish(7)
    k_d_finish(0)
    k_d_finish(1)
    k_d_finish(2)
    s_c_finish(4)
    for copy in vb_copies:
        copy.wait()
    total = vb[peers[0]]
    for j in range(1, npeer):
        total = total + vb[peers[j]]
    vc[0] = total
    vc_copies = [remote(vc.at[0], vc.at[k], vc_s.at[k - 1], vc_r.at[k - 1], z_dev(k)) for k in range(1, tn)]
    for copy in vc_copies:
        copy.start()
    s_c_finish(5)
    k_c_finish(6)
    k_d_finish(3)
    k_c_finish(7)
    k_d_finish(4)
    for copy in vc_copies:
        copy.wait()
    total = vc[zs[0]]
    for j in range(1, tn):
        total = total + vc[zs[j]]
    own = vc[0, 4:5]
    for k in range(1, tn):
        own = own + vc[k, 4 + k : 5 + k]
    vec_out[...] = total
    vec_out[4:5] = own
    k_d_finish(5)
    k_d_finish(6)
    e_finish()
    k_d_finish(7)
    for i in range(8):
        k_e_finish(i)
    store_layer().wait()
    for b in range(nw):
        store_grad(b).wait()


def finish_kernel(
    layer_in, igrad_in, fin_h, fink_h, vec, layer_out, igrad, gwq_h, gwo_h, gwi_h, gwd_h, gl1, gbo, gl2, gbi, gbd,
    layer_v, igrad_v, fin, fink, gwq, gwo, gwi, gwd, in_s, out_s,
):
    def move(i, src, dst, sems):
        copy = pltpu.make_async_copy(src, dst, sems.at[i])
        copy.start()
        return copy

    pairs = fink.shape[0] // 2
    width, pw = fink.shape[2:]
    kinds = ((fink_h, fink), (fin_h, fin), (layer_in, layer_v), (igrad_in, igrad_v))
    loads = [move(i, src, dst, in_s) for i, (src, dst) in enumerate(kinds)]
    for row, out in enumerate((gl1, gbo, gl2, gbd, gbi)):
        out[...] = vec[row : row + 1]
    loads[0].wait()
    for p in range(pairs):
        at = slice(p * pw, (p + 1) * pw)
        gwq[:, at] = fink[2 + p // 2, p % 2].astype(F32)
        gwq[:, width + p * pw : width + (p + 1) * pw] = fink[4 + p, 0].astype(F32)
        gwq[:, 2 * width + p * pw : 2 * width + (p + 1) * pw] = fink[4 + p, 1].astype(F32)
    stores = [move(0, gwq, gwq_h, out_s)]
    for p in range(pairs):
        gwo[:, p * pw : (p + 1) * pw] = fink[p // 2, p % 2].astype(F32)
    stores.append(move(1, gwo, gwo_h, out_s))
    loads[2].wait()
    stores.append(move(2, layer_v, layer_out, out_s))
    loads[3].wait()
    stores.append(move(3, igrad_v, igrad, out_s))
    loads[1].wait()
    gwi[...] = fin[0].astype(F32)
    stores.append(move(4, gwi, gwi_h, out_s))
    gwd[...] = fin[1].astype(F32).T
    stores.append(move(5, gwd, gwd_h, out_s))
    for copy in stores:
        copy.wait()


def local(
    tn,
    dpn,
    tokens,
    cotangent,
    seq_lengths,
    features,
    ln1_gain,
    w_qkv,
    w_out,
    b_out,
    ln2_gain,
    w_in,
    b_in,
    w_down,
    b_down,
):
    rows_n, width = tokens.shape
    heads, hw, feat_n = features.shape
    pairs, pw, nb = heads // 2, 2 * hw, rows_n // BR
    ffl = w_in.shape[1]
    npeer = dpn // 2
    rp = width // npeer
    vrows = -(-(4 + tn) // 8) * 8
    dma = pltpu.SemaphoreType.DMA
    vmem = pl.BlockSpec(memory_space=pltpu.VMEM)
    anywhere = pl.BlockSpec(memory_space=pl.ANY)

    def scratch(shape, dtype=BF16):
        return pltpu.VMEM(shape, dtype)

    out = pl.pallas_call(
        functools.partial(layer_kernel, tn, dpn),
        out_shape=(
            jax.ShapeDtypeStruct((rows_n, width), BF16),
            jax.ShapeDtypeStruct((rows_n, width), F32),
            jax.ShapeDtypeStruct((2, width, width), BF16),
            jax.ShapeDtypeStruct((8, 2, width, pw), BF16),
            jax.ShapeDtypeStruct((vrows, width), F32),
        ),
        in_specs=[pl.BlockSpec(memory_space=pltpu.SMEM)]
        + [anywhere, anywhere, anywhere, vmem, anywhere, anywhere, vmem, vmem, anywhere, anywhere],
        out_specs=(anywhere, anywhere, vmem, vmem, vmem),
        scratch_shapes=[
            scratch((rows_n, width)),
            scratch((rows_n, width)),
            scratch((heads, hw, feat_n)),
            scratch((width, 3 * width)),
            scratch((width, width)),
            scratch((rows_n, width)),
            scratch((rows_n, width), F32),
            scratch((tn, 2, width, ffl)),
            scratch((tn, 8, ffl), F32),
            scratch((rows_n, width)),
            scratch((pairs, rows_n, pw)),
            scratch((pairs, rows_n, pw)),
            scratch((pairs, rows_n, pw)),
            scratch((pairs, rows_n, 2 * feat_n)),
            scratch((pairs, rows_n, 2 * feat_n)),
            scratch((pairs, 3 * pw, 2 * feat_n)),
            scratch((2 * pw, pw)),
            scratch((nb, BR, BR)),
            scratch((nb, BR, BR)),
            scratch((nb + 1, pairs, pw + 16, feat_n), F32),
            scratch((nb, pairs, pw + 16, feat_n)),
            scratch((rows_n, width), F32),
            scratch((rows_n, width)),
            scratch((rows_n, width), F32),
            scratch((rows_n, width), F32),
            scratch((rows_n, 1), F32),
            scratch((rows_n, width)),
            scratch((2, rows_n, width)),
            scratch((pairs, pw + 16, feat_n)),
            scratch((pairs, pw + 16, feat_n)),
            scratch((pairs, pw + 16, feat_n)),
            scratch((pairs, pw + 16, feat_n)),
            scratch((tn, 2, width, width)),
            scratch((2, width, width)),
            scratch((4, npeer - 1, rp, width)),
            scratch((tn - 1, rp, width)),
            scratch((8, 2, width, pw)),
            scratch((4, width, pw)),
            scratch((8, npeer - 1, rp, pw)),
            scratch((8, max(tn, 2 * (tn - 1).bit_length()), rp, pw)),
            scratch((vrows, width), F32),
            scratch((vrows, width), F32),
            scratch((npeer, vrows, width), F32),
            scratch((tn, vrows, width), F32),
            dma((7,)),
            dma((1 + rows_n // WR,)),
            dma((tn - 1,)),
            dma((tn - 1,)),
            dma((tn - 1,)),
            dma((tn - 1,)),
            dma((tn - 1, npeer - 1)),
            dma((tn - 1, npeer - 1)),
            dma((tn - 1,)),
            dma((tn - 1,)),
            dma((pairs,)),
            dma((pairs,)),
            dma((pairs,)),
            dma((pairs,)),
            dma((tn,)),
            dma((tn,)),
            dma((tn, npeer - 1)),
            dma((tn, npeer - 1)),
            dma((tn - 1,)),
            dma((tn - 1,)),
            dma((npeer - 1,)),
            dma((npeer - 1,)),
            dma(()),
            dma(()),
            dma((8,)),
            dma((8,)),
            dma((8, npeer - 1)),
            dma((8, npeer - 1)),
            dma((8, tn - 1)),
            dma((8, tn - 1)),
            dma((8, npeer - 1)),
            dma((8, npeer - 1)),
            dma((8,)),
            dma((8,)),
            dma(()),
            dma(()),
            dma((npeer - 1,)),
            dma((npeer - 1,)),
            dma((tn - 1,)),
            dma((tn - 1,)),
        ],
        compiler_params=pltpu.CompilerParams(
            collective_id=0, has_side_effects=True, vmem_limit_bytes=63 * 1024 * 1024
        ),
    )(
        seq_lengths,
        tokens,
        cotangent,
        features,
        ln1_gain[None],
        w_qkv,
        w_out,
        jnp.stack([b_out, b_in, b_down]).astype(F32),
        ln2_gain[None],
        w_in,
        w_down,
    )
    row = jax.ShapeDtypeStruct((1, width), F32)

    def square(n):
        return jax.ShapeDtypeStruct((width, n * width), F32)

    done = pl.pallas_call(
        finish_kernel,
        out_shape=(out[0], out[1], square(3), square(1), square(1), square(1)) + (row,) * 5,
        in_specs=[anywhere] * 4 + [vmem],
        out_specs=(anywhere,) * 6 + (vmem,) * 5,
        scratch_shapes=[
            scratch((rows_n, width)),
            scratch((rows_n, width), F32),
            scratch((2, width, width)),
            scratch((8, 2, width, pw)),
            scratch((width, 3 * width), F32),
            scratch((width, width), F32),
            scratch((width, width), F32),
            scratch((width, width), F32),
            dma((4,)),
            dma((6,)),
        ],
        compiler_params=pltpu.CompilerParams(vmem_limit_bytes=63 * 1024 * 1024),
    )(*out)
    layer_out, input_grad, gwq, gwo, gwi, gwd, gl1, gbo, gl2, gbi, gbd = done
    return (
        layer_out,
        input_grad,
        gl1[0],
        gwq,
        gwo,
        gbo[0],
        gl2[0],
        gwi,
        gbi[0],
        gwd,
        gbd[0],
    )


def solution(mesh):
    tn, dpn = mesh.shape["tensor"], mesh.shape["dp"]
    rows = P(("dp", "tensor"), None)
    return jax.shard_map(
        functools.partial(local, tn, dpn),
        mesh=mesh,
        in_specs=(
            rows,
            rows,
            P("dp", None),
            P(),
            P(),
            P(),
            P(),
            P(),
            P(),
            P(None, "tensor"),
            P("tensor"),
            P("tensor", None),
            P(),
        ),
        out_specs=(
            rows,
            rows,
            P(),
            P(),
            P(),
            P(),
            P(),
            P(None, "tensor"),
            P("tensor"),
            P("tensor", None),
            P(),
        ),
        check_vma=False,
    )
```

```python
import functools

import jax
import jax.numpy as jnp
from jax import lax
from jax.experimental import pallas as pl
from jax.experimental.pallas import tpu as pltpu
from jax.sharding import PartitionSpec as P

MESH = pl.DeviceIdType.MESH
F32 = jnp.float32
BF16 = jnp.bfloat16
EPSILON = 1e-05
BR = 256
WR = 512
SQRT_2_OVER_PI = 0.7978845608028654
CUBIC = 0.044715


def dot(a, b):
    return jnp.dot(a, b, preferred_element_type=F32)


def dot_rt(a, b):
    return lax.dot_general(a, b, (((1,), (1,)), ((), ())), preferred_element_type=F32)


def dot_lt(a, b):
    return lax.dot_general(a, b, (((0,), (0,)), ((), ())), preferred_element_type=F32)


def xor(a, b, size):
    out, bit = 0, 1
    while bit < size:
        out = out + bit * lax.rem(lax.div(a, bit) + (b // bit if isinstance(b, int) else lax.div(b, bit)), 2)
        bit *= 2
    return out


def iota(shape, axis):
    return lax.broadcasted_iota(jnp.int32, shape, axis)


def layer_kernel(
    tn,
    dpn,
    lens,
    tok_h,
    cot_h,
    feats_h,
    g1_h,
    wqkv_h,
    wout_h,
    biases_h,
    g2_h,
    win_h,
    wdn_h,
    layer_h,
    igrad_h,
    fin_h,
    fink_h,
    vec_out,
    fin,
    fink,
    g1,
    g2,
    biases,
    tok,
    cot,
    feats,
    wqkv,
    wout,
    igrad,
    wfull,
    bfull,
    n1s,
    qs,
    ks,
    vs,
    phq,
    phk,
    featx,
    norms,
    bsw,
    mask,
    maskt,
    lst,
    sb,
    rsw_s,
    attn,
    facc,
    xh2,
    rstd2,
    n2s,
    ad,
    chf_in,
    chf_out,
    chb_in,
    chb_out,
    gbuf,
    ra,
    rb,
    rc,
    kbuf,
    kra,
    krb,
    krc,
    vec,
    va,
    vb,
    vc,
    in_s,
    out_s,
    bz_s,
    bz_r,
    wz_s,
    wz_r,
    wx_s,
    wx_r,
    wc_s,
    wc_r,
    chf_s,
    chf_r,
    chb_s,
    chb_r,
    a_s,
    a_r,
    b_s,
    b_r,
    c_s,
    c_r,
    d_s,
    d_r,
    e_s,
    e_r,
    ka_s,
    ka_r,
    kb_s,
    kb_r,
    kc_s,
    kc_r,
    kd_s,
    kd_r,
    ke_s,
    ke_r,
    va_s,
    va_r,
    vb_s,
    vb_r,
    vc_s,
    vc_r,
):
    rows_n, width = tok.shape
    heads, hw, feat_n = feats.shape
    pairs = heads // 2
    pw = 2 * hw
    nb = rows_n // BR
    seqs = lens.shape[1]
    shrink = hw ** (-0.25)
    featscale = feat_n ** (-0.5)
    npeer = dpn // 2
    rp = width // npeer

    dp = lax.axis_index("dp")
    t = lax.axis_index("tensor")
    cb = lax.rem(dp, 2)
    q = lax.div(dp, 2)
    core_dev = (dp + 1 - 2 * cb, t)

    peers = [xor(q, k, npeer) for k in range(npeer)]
    zs = [xor(t, k, tn) for k in range(tn)]

    def peer_dev(k):
        return (2 * peers[k] + cb, t)

    def z_dev(k):
        return (dp, zs[k])

    row_starts = [pl.multiple_of(peer * rp, rp) for peer in peers]

    def own_rows():
        return pl.ds(row_starts[0], rp)

    def peer_rows(k):
        return pl.ds(row_starts[k], rp)

    def load(i, src, dst):
        return pltpu.make_async_copy(src, dst, in_s.at[i])

    pairs_in = {
        "feats": (feats_h, feats),
        "g1": (g1_h, g1),
        "g2": (g2_h, g2),
        "biases": (biases_h, biases),
        "win": (win_h, wfull.at[0, 0]),
        "wdn": (wdn_h, wfull.at[0, 1]),
        "tok": (tok_h, tok),
        "wqkv": (wqkv_h, wqkv),
        "wout": (wout_h, wout),
        "cot": (cot_h, cot),
    }
    loads = {name: load(i, *pair) for i, (name, pair) in enumerate(pairs_in.items())}
    for copy in loads.values():
        copy.start()

    def store_layer():
        half = layer_h.shape[0] // 2
        for h in range(2):
            pltpu.make_async_copy(wfull.at[tn - 1, h], layer_h.at[pl.ds(h * half, half)], out_s.at[0]).start()

    def store_grad(b):
        rows = pl.ds(pl.multiple_of(b * WR, WR), WR)
        pltpu.make_async_copy(igrad.at[rows], igrad_h.at[rows], out_s.at[1]).start()

    def store_fin():
        return pltpu.make_async_copy(fin, fin_h, out_s.at[2])

    def store_fink(i):
        return pltpu.make_async_copy(fink.at[i], fink_h.at[i], out_s.at[3])

    bar = pltpu.get_barrier_semaphore()
    targets = [core_dev] + [peer_dev(k) for k in range(1, npeer)] + [z_dev(k) for k in range(1, tn)]
    for dev in targets:
        pl.semaphore_signal(bar, inc=1, device_id=dev, device_id_type=MESH)

    def remote(src, dst, ss, rs, dev):
        return pltpu.make_async_remote_copy(
            src_ref=src, dst_ref=dst, send_sem=ss, recv_sem=rs, device_id=dev, device_id_type=MESH
        )

    def arrived(ref, sem):
        remote(ref, ref, a_s, sem, core_dev).wait_recv()

    def sent(ref, sem):
        remote(ref, ref, sem, a_r.at[0], core_dev).wait_send()

    def bz_copy(k):
        return remote(bfull.at[0], bfull.at[k], bz_s, bz_r, z_dev(k))

    def wz_copy(k):
        source, via = (0, k) if k == 1 or k % 2 == 0 else (k - 1, 1)
        return remote(
            wfull.at[source, cb, own_rows()], wfull.at[k, cb, own_rows()], wz_s, wz_r.at[k - 1], z_dev(via)
        )

    def wx_copy(k, j):
        here = wfull.at[k, cb, own_rows()]
        return remote(here, here, wx_s, wx_r.at[k - 1], peer_dev(j))

    def wc_copy(k):
        return remote(wfull.at[k, cb], wfull.at[k, cb], wc_s, wc_r.at[k - 1], core_dev)

    def wc_recv(k):
        here = wfull.at[k, 1 - cb]
        return remote(here, here, wc_s, wc_r.at[k - 1], core_dev)

    def w_spread(k):
        wz_copy(k).wait_recv()
        if k > 1 and k % 2 == 0:
            wz_copy(k + 1).start()
        for j in range(1, npeer):
            wx_copy(k, j).start()

    def w_swap(k):
        arrived(wfull.at[k, cb, pl.ds(0, (npeer - 1) * rp)], wx_r.at[k - 1])
        wc_copy(k).start()

    levels = (tn - 1).bit_length()
    up_first = (1, 3, 5, 7), (8, 9, 10, 12)

    def up_due(at, p):
        return up_first[at - 1][p % 4] if at < 3 and p < 4 else 10 + p

    def down_due(hops, p):
        due = min(3 * hops + p, 8 + 2 * p)
        return due + due % 2 if due > 8 else due

    def up_copy(p):
        return remote(chf_out.at[p], chf_in.at[p], chf_s, chf_r.at[p], (dp, lax.rem(t + 1, tn)))

    def up_handle(p):
        @pl.when(t > 0)
        def _():
            up_copy(p).wait_recv()

        chf_out[p] = (lst[nb, p] + passing * chf_in[p].astype(F32)).astype(BF16)
        up_copy(p).start()

    def up_slots(k, low, high):
        for at in range(1, tn - 1):
            for p in range(pairs):
                if low <= up_due(at, p) < high:

                    @pl.when((t == at) & (k == up_due(at, p)))
                    def _(p=p):
                        up_handle(p)

    def down_copy(p):
        return remote(chb_out.at[p], chb_in.at[p], chb_s, chb_r.at[p], (dp, lax.rem(t + tn - 1, tn)))

    def down_handle(p):
        @pl.when(t < tn - 1)
        def _():
            down_copy(p).wait_recv()

        own = lst[nb - 1, p]
        for b in range(nb - 2, -1, -1):
            own = keep_of(b) * own + lst[b, p]
        chb_out[p] = (own + passing * chb_in[p].astype(F32)).astype(BF16)
        down_copy(p).start()

    def down_slots(k, low, high):
        for hops in range(tn - 1):
            for p in range(pairs):
                if low <= down_due(hops, p) < high:

                    @pl.when((t == tn - 1 - hops) & (k == down_due(hops, p)))
                    def _(p=p):
                        down_handle(p)

    def place_of(turn):
        return jnp.where(turn < tn // 2, 2 * turn + 1, 2 * (tn - 1 - turn))

    def a_copy(turn):
        turn = jnp.int32(turn)
        return remote(
            gbuf.at[place_of(turn), 1 - cb], ra.at[lax.rem(turn, 2)], a_s, a_r.at[lax.rem(turn, 2)], core_dev
        )

    def b_copy(s, k):
        s = jnp.int32(s)
        return remote(gbuf.at[s, cb, peer_rows(k)], rb.at[lax.rem(s, 4), k - 1], b_s, b_r.at[s], peer_dev(k))

    def c_copy(s):
        return remote(gbuf.at[s, cb, own_rows()], rc.at[s - 1], c_s, c_r.at[s - 1], z_dev(s & -s))

    def d_copy(k):
        here = fin.at[cb, own_rows()]
        return remote(here, here, d_s, d_r, peer_dev(k))

    def e_copy():
        return remote(fin.at[cb], fin.at[cb], e_s, e_r, core_dev)

    def e_recv():
        return remote(fin.at[1 - cb], fin.at[1 - cb], e_s, e_r, core_dev)

    def ka_copy(i):
        i = jnp.int32(i)
        return remote(kbuf.at[i, 1 - cb], kra.at[lax.rem(i, 4)], ka_s, ka_r.at[lax.rem(i, 4)], core_dev)

    def kb_copy(i, k):
        return remote(
            kbuf.at[i, cb, peer_rows(k)], krb.at[i, k - 1], kb_s, kb_r.at[i], peer_dev(k)
        )

    def kc_copy(i, k):
        return remote(krc.at[i, 0], krc.at[i, k], kc_s.at[0], kc_r.at[i, 0], z_dev(k))

    def ks_copy(i, l):
        return remote(
            krc.at[i, 2 * l], krc.at[i, 2 * l + 1], kc_s.at[1], kc_r.at[i, l], z_dev(1 << l)
        )

    def kd_copy(i, k):
        here = fink.at[i, cb, own_rows()]
        return remote(here, here, kd_s, kd_r.at[i], peer_dev(k))

    def ke_copy(i):
        return remote(fink.at[i, cb], fink.at[i, cb], ke_s, ke_r.at[i], core_dev)

    def ke_recv(i):
        return remote(fink.at[i, 1 - cb], fink.at[i, 1 - cb], ke_s, ke_r.at[i], core_dev)

    def a_start(turn):
        a_copy(turn).start()

    def a_finish(turn):
        turn = jnp.int32(turn)
        a_copy(turn).wait_recv()
        s = place_of(turn)
        gbuf[s, cb] = (gbuf[s, cb].astype(F32) + ra[lax.rem(turn, 2)].astype(F32)).astype(BF16)
        for k in range(1, npeer):
            b_copy(s, k).start()

    def b_sum(s):
        s = jnp.int32(s)
        arrived(rb.at[lax.rem(s, 4)], b_r.at[s])
        total = gbuf[s, cb, own_rows()].astype(F32)
        for k in range(1, npeer):
            total = total + rb[lax.rem(s, 4), k - 1].astype(F32)
        return total.astype(BF16)

    def b_finish(s):
        gbuf[s, cb, own_rows()] = b_sum(s)

    def c_add(s):
        step = 1
        while step < (s & -s if s else tn):
            c_copy(s + step).wait_recv()
            gbuf[s, cb, own_rows()] = (
                gbuf[s, cb, own_rows()].astype(F32) + rc[s + step - 1].astype(F32)
            ).astype(BF16)
            step *= 2

    def c_start(s):
        c_add(s)
        c_copy(s).start()

    def c_finish():
        total = gbuf[0, cb, own_rows()].astype(F32)
        step = 1
        while step < tn:
            c_copy(step).wait_recv()
            total = total + rc[step - 1].astype(F32)
            step *= 2
        fin[cb, own_rows()] = total.astype(BF16)
        for k in range(1, npeer):
            d_copy(k).start()

    def d_finish():
        arrived(fin.at[0, pl.ds(0, (npeer - 1) * rp)], d_r)
        e_copy().start()

    def e_finish():
        e_recv().wait_recv()

    def k_a_start(i, both):
        kbuf[i, 0] = both[:, :pw].astype(BF16)
        kbuf[i, 1] = both[:, pw:].astype(BF16)
        ka_copy(i).start()

    def k_a_finish(i):
        i = jnp.int32(i)
        ka_copy(i).wait_recv()
        kbuf[i, cb] = (kbuf[i, cb].astype(F32) + kra[lax.rem(i, 4)].astype(F32)).astype(BF16)
        for k in range(1, npeer):
            kb_copy(i, k).start()

    def k_b_sum(i):
        arrived(krb.at[i], kb_r.at[i])
        total = kbuf[i, cb, own_rows()].astype(F32)
        for k in range(1, npeer):
            total = total + krb[i, k - 1].astype(F32)
        krc[i, 0] = total.astype(BF16)

    def k_spread(i, total):
        fink[i, cb, own_rows()] = total.astype(BF16)
        for k in range(1, npeer):
            kd_copy(i, k).start()

    def k_b_finish(i):
        k_b_sum(i)
        for k in range(1, tn):
            kc_copy(i, k).start()

    def k_c_finish(i):
        arrived(krc.at[i, pl.ds(1, tn - 1)], kc_r.at[i, 0])
        total = krc[i, zs[0]].astype(F32)
        for j in range(1, tn):
            total = total + krc[i, zs[j]].astype(F32)
        k_spread(i, total)

    def s_b_finish(i):
        k_b_sum(i)
        ks_copy(i, 0).start()

    def s_sum(i, l):
        ks_copy(i, l).wait_recv()
        return krc[i, 2 * l].astype(F32) + krc[i, 2 * l + 1].astype(F32)

    def s_middle(i):
        for l in range(levels - 1):
            krc[i, 2 * l + 2] = s_sum(i, l).astype(BF16)
            ks_copy(i, l + 1).start()

    def s_c_finish(i):
        k_spread(i, s_sum(i, levels - 1))

    def k_d_finish(i):
        arrived(fink.at[i, 0, pl.ds(0, (npeer - 1) * rp)], kd_r.at[i])
        ke_copy(i).start()

    def k_e_finish(i):
        ke_recv(i).wait_recv()

    offsets = [jnp.int32(0)]
    for c in range(1, seqs):
        offsets.append(offsets[-1] + lens[0, c - 1])
    first = t * rows_n

    def seg_at(r):
        seg = -1
        for off in offsets:
            seg = seg + jnp.where(r >= off, 1, 0)
        return seg

    def seg_array(shape, axis, start):
        places = iota(shape, axis) + start
        seg = jnp.full(shape, -1, jnp.int32)
        for off in offsets:
            seg = seg + jnp.where(places >= off, 1, 0)
        return seg

    before = seg_at(first - 1)
    closing = seg_at(first + rows_n - 1)
    passing = jnp.where(before == closing, 1.0, 0.0)

    def prev_of(b):
        return seg_at(first + b * BR - 1)

    def last_of(b):
        return seg_at(first + b * BR + BR - 1)

    def keep_of(b):
        return jnp.where(prev_of(b) == last_of(b), 1.0, 0.0)

    def ending(b):
        return seg_array((BR, pw), 0, first + b * BR) == last_of(b)

    def reached(b):
        return seg_array((BR, pw), 0, first + b * BR) == prev_of(b)

    def block(b):
        return pl.ds(pl.multiple_of(b * BR, BR), BR)

    nw = rows_n // WR

    def wide(b):
        return pl.ds(pl.multiple_of(b * WR, WR), WR)

    def lanes(p):
        return pl.ds(pl.multiple_of(p * pw, pw), pw)

    low_lane = iota((BR, pw), 1) < hw
    low_row = iota((pw, feat_n), 0) < hw
    row_id = iota((pw, feat_n), 0)

    for name in ("feats", "g1", "g2", "biases"):
        loads[name].wait()
    featx[...] = jnp.zeros_like(featx)
    for p in range(pairs):
        for o in range(2):
            featx[p, o * hw : (o + 1) * hw, o * feat_n : (o + 1) * feat_n] = feats[2 * p + o]
            featx[p, pw + o * hw : pw + (o + 1) * hw, o * feat_n : (o + 1) * feat_n] = jnp.full(
                (hw, feat_n), -0.5, BF16
            )
    ri, ci = iota((2 * pw, pw), 0), iota((2 * pw, pw), 1)
    ro, co = iota((2 * pw, 2 * pw), 0), iota((2 * pw, 2 * pw), 1)
    norms[...] = jnp.where((lax.rem(ro, pw) < hw) == (co < pw), -0.5, 0.0).astype(BF16)
    swap = (lax.rem(ri, pw) < hw) != (ci < hw)
    bsw[...] = jnp.where(swap, 1.0, 0.0).astype(BF16)

    def build_mask(b, _):
        seg_i = seg_array((BR, BR), 0, first + b * BR)
        seg_j = seg_array((BR, BR), 1, first + b * BR)
        same = seg_i == seg_j
        i, j = iota((BR, BR), 0), iota((BR, BR), 1)
        mask[b] = jnp.where(same & (i >= j), 1.0, 0.0).astype(BF16)
        maskt[b] = jnp.where(same & (j >= i), 1.0, 0.0).astype(BF16)
        return 0

    lax.fori_loop(0, nb, build_mask, 0)
    lst[0] = jnp.zeros(lst.shape[1:], F32)
    vec[...] = jnp.zeros_like(vec)

    @pl.when(t == 0)
    def _():
        chf_in[...] = jnp.zeros_like(chf_in)

    @pl.when(t == tn - 1)
    def _():
        chb_in[...] = jnp.zeros_like(chb_in)

    loads["win"].wait()
    loads["wdn"].wait()
    pl.semaphore_wait(bar, len(targets))
    bfull[0] = jnp.broadcast_to(biases[:, width : width + bfull.shape[2]], bfull.shape[1:])
    for k in range(1, tn):
        bz_copy(k).start()
    wz_copy(1).start()
    wz_copy(2).start()

    def features_of(x, p):
        wide = x.astype(F32)
        square = wide * wide
        high = square.astype(BF16)
        rest = (square - high.astype(F32)).astype(BF16)
        norm = dot(jnp.concatenate([high, rest], 1), norms[...])
        repeats = [norm[:, :pw]] * (feat_n // pw) + [norm[:, pw:]] * (feat_n // pw)
        arg = dot(x, featx[p, :pw]) + jnp.concatenate(repeats, 1)
        return (jnp.exp(arg) * featscale).astype(BF16)

    def normalized(x):
        centre = jnp.mean(x, -1, keepdims=True)
        shifted = x - centre
        inverse = lax.rsqrt(jnp.mean(shifted * shifted, -1, keepdims=True) + EPSILON)
        return shifted * inverse, inverse

    def values_of(p, b):
        wide = vs[p, block(b)].astype(F32)
        return jnp.where(low_lane, wide, 1.0), jnp.where(low_lane, 1.0, wide)

    def keys_block(b, _):
        scaled, _inv = normalized(tok[wide(b)].astype(F32))
        normed = (scaled * g1[...]).astype(BF16)
        n1s[wide(b)] = normed
        key = (dot(normed, wqkv[:, width : 2 * width]) * shrink).astype(BF16)
        val = dot(normed, wqkv[:, 2 * width :]).astype(BF16)
        for p in range(pairs):
            ks[p, wide(b)] = key[:, p * pw : (p + 1) * pw]
            vs[p, wide(b)] = val[:, p * pw : (p + 1) * pw]

        return 0

    loads["tok"].wait()
    loads["wqkv"].wait()
    lax.fori_loop(0, nw, keys_block, 0)

    def state_pair(p, _):
        for c in range(nw):
            phk[p, wide(c)] = features_of(ks[p, wide(c)], p)
        for b in range(nb):
            feat = phk[p, block(b)]
            end = ending(b)
            ve, vo = values_of(p, b)
            ue = dot_lt(jnp.where(end, ve, 0.0).astype(BF16), feat[:, :feat_n])
            uo = dot_lt(jnp.where(end, vo, 0.0).astype(BF16), feat[:, feat_n:])
            keep = keep_of(b)
            lst[b + 1, p, :pw] = keep * lst[b, p, :pw] + jnp.where(low_row, ue, uo)
            lst[b + 1, p, pw : pw + 8] = keep * lst[b, p, pw : pw + 8] + ue[hw : hw + 8]
            lst[b + 1, p, pw + 8 :] = keep * lst[b, p, pw + 8 :] + uo[:8]

        @pl.when(t == 0)
        def _():
            up_handle(p)


        @pl.when(p == 3)
        def _():
            w_spread(1)

        return 0

    lax.fori_loop(0, pairs, state_pair, 0)

    def queries_block(b, _):
        up_slots(b, 0, nw)
        query = (dot(n1s[wide(b)], wqkv[:, :width]) * shrink).astype(BF16)
        for p in range(pairs):
            qs[p, wide(b)] = query[:, p * pw : (p + 1) * pw]

        @pl.when(b == nw - 1)
        def _():
            w_spread(2)

        return 0

    lax.fori_loop(0, nw, queries_block, 0)

    def features_pair(p, _):
        up_slots(nw + p, nw, nw + pairs)
        for b in range(nw):
            phq[p, wide(b)] = features_of(qs[p, wide(b)], p)
        return 0

    lax.fori_loop(0, pairs, features_pair, 0)

    def state_halves(state):
        top = state[:pw]
        even = jnp.where(low_row, top, jnp.broadcast_to(state[pw : pw + 1], top.shape)).astype(BF16)
        odd = jnp.where(low_row, jnp.broadcast_to(state[pw + 8 : pw + 9], top.shape), top).astype(BF16)
        return even, odd

    slot = nw + pairs

    def inside_pair(p, _):
        up_slots(slot + p, slot, slot + pairs)

        @pl.when(p == 3)
        def _():
            w_spread(3)

        for b in range(nb):
            for o, (val, part) in enumerate(zip(values_of(p, b), (facc, xh2))):
                fq = phq[p, block(b), o * feat_n : (o + 1) * feat_n]
                fk = phk[p, block(b), o * feat_n : (o + 1) * feat_n]
                scores = jnp.where(mask[b].astype(F32) > 0, dot_rt(fq, fk), 0.0).astype(BF16)
                part[block(b), lanes(p)] = dot(scores, val.astype(BF16))
        return 0

    lax.fori_loop(0, pairs, inside_pair, 0)

    def attend_pair(p, _):
        up_slots(slot + pairs + p, slot + pairs, slot + 2 * pairs)

        @pl.when(p == 2)
        def _():
            w_swap(1)

        @pl.when(t == tn - 1)
        def _():
            up_copy(p).wait_recv()

        incoming = chf_in[p].astype(F32)
        for b in range(nb):
            first_pass = jnp.where(before == prev_of(b), 1.0, 0.0)
            state = (lst[b, p] + first_pass * incoming).astype(BF16)
            sb[b, p] = state
            reach = reached(b)
            outs = []
            for o, (st, part) in enumerate(zip(state_halves(state.astype(F32)), (facc, xh2))):
                fq = phq[p, block(b), o * feat_n : (o + 1) * feat_n]
                outs.append(part[block(b), lanes(p)] + jnp.where(reach, dot_rt(fq, st), 0.0))
            inverse = 1.0 / jnp.where(low_lane, outs[1], outs[0])
            rsw_s[block(b), lanes(p)] = inverse
            num = jnp.where(low_lane, outs[0], outs[1])
            attn[block(b), lanes(p)] = (num * pltpu.roll(inverse, hw, 1)).astype(BF16)
        return 0

    lax.fori_loop(0, pairs, attend_pair, 0)

    def hidden_block(b, _):
        h1 = tok[wide(b)].astype(F32) + (dot(attn[wide(b)], wout[...]) + biases[:, :width])
        scaled, inverse = normalized(h1)
        xh2[wide(b)] = scaled
        rstd2[wide(b)] = inverse
        n2s[wide(b)] = (scaled * g2[...]).astype(BF16)
        facc[wide(b)] = h1 + biases[:, width + bfull.shape[2] :]
        return 0

    loads["wout"].wait()
    lax.fori_loop(0, nw, hidden_block, 0)
    loads["cot"].wait()

    def feed_chunk(turn, _):
        s = place_of(turn)

        @pl.when(s > 0)
        def _():
            for k in range(1, tn):

                @pl.when(s == k)
                def _(k=k):
                    wc_recv(k).wait_recv()

        def rows_block(b, total):
            w_in = wfull[s, 0]
            w_dn = wfull[s, 1]
            u = dot(n2s[wide(b)], w_in) + bfull[s, 0:1]
            u2 = u * u
            th = jnp.tanh(u * (SQRT_2_OVER_PI + SQRT_2_OVER_PI * CUBIC * u2))
            half = 0.5 + 0.5 * th
            act = (u * half).astype(BF16)
            slope = half + (0.5 * u) * (1.0 - th * th) * (
                SQRT_2_OVER_PI + 3.0 * SQRT_2_OVER_PI * CUBIC * u2
            )
            ad[0, wide(b)] = act
            facc[wide(b)] += dot(act, w_dn)
            du = (slope * dot_rt(cot[wide(b)], w_dn)).astype(BF16)
            ad[1, wide(b)] = du
            back = dot_rt(du, w_in)

            @pl.when(turn == 0)
            def _():
                igrad[wide(b)] = back

            @pl.when(turn > 0)
            def _():
                igrad[wide(b)] += back

            @pl.when((turn >= 1) & (b == 0))
            def _():
                a_finish(jnp.maximum(turn - 1, 0))

            @pl.when((turn == 0) & (b == 0))
            def _():
                w_swap(2)

            @pl.when((turn == 0) & (b == nw - 1))
            def _():
                w_swap(3)

            return total + jnp.sum(du.astype(F32), 0, keepdims=True)

        total = lax.fori_loop(0, nw, rows_block, jnp.zeros((1, wfull.shape[3]), F32))
        vec[pl.ds(4 + s, 1)] = total

        @pl.when(turn == tn - 1)
        def _():
            b_finish(1)
            c_start(1)

        gbuf[s, 0] = dot_lt(n2s[...], ad[1]).astype(BF16)
        gbuf[s, 1] = dot_lt(cot[...], ad[0]).astype(BF16)
        a_start(turn)
        return 0

    arrived(bfull.at[pl.ds(1, tn - 1)], bz_r)
    lax.fori_loop(0, tn, feed_chunk, 0)
    sent(bfull.at[pl.ds(1, tn - 1)], bz_s)
    sent(wfull.at[pl.ds(0, tn - 1), 0, pl.ds(0, rp)], wz_s)
    sent(wfull.at[pl.ds(0, tn - 1), 0, pl.ds(0, (npeer - 1) * rp)], wx_s)
    sent(wfull.at[pl.ds(0, tn - 1), 0], wc_s)

    def norm_back(dn, gain, scaled, inverse):
        g = dn * gain
        inner = jnp.mean(g, -1, keepdims=True)
        cross = jnp.mean(g * scaled, -1, keepdims=True)
        return inverse * (g - inner - scaled * cross)


    def branch_block(b, carry):
        gl2, gbo, gbd = carry
        wfull[tn - 1, b] = facc[wide(b)].astype(BF16)
        dy = cot[wide(b)].astype(F32)
        dn2 = igrad[wide(b)]
        scaled = xh2[wide(b)]
        dh1 = dy + norm_back(dn2, g2[...], scaled, rstd2[wide(b)])
        igrad[wide(b)] = dh1
        dob = dh1.astype(BF16)
        n2s[wide(b)] = dob
        dattn = dot_rt(dob, wout[...])
        lane_id = iota((WR, pw), 1)
        low_half = lane_id < hw
        for p in range(pairs):
            da = dattn[:, p * pw : (p + 1) * pw]
            inverse = rsw_s[wide(b), p * pw : (p + 1) * pw]
            dnum = da * pltpu.roll(inverse, hw, 1)
            prod = da * attn[wide(b), p * pw : (p + 1) * pw].astype(F32)
            high = prod.astype(BF16)
            rest = (prod - high.astype(F32)).astype(BF16)
            dden = -dot(jnp.concatenate([high, rest], 1), bsw[...]) * inverse
            dhi = dden.astype(BF16).astype(F32)
            dlo = dden - dhi
            even = jnp.where(lane_id == hw, dhi, jnp.where(lane_id == hw + 1, dlo, 0.0))
            odd = jnp.where(lane_id == 0, dhi, jnp.where(lane_id == 1, dlo, 0.0))
            ad[0, wide(b), p * pw : (p + 1) * pw] = jnp.where(low_half, dnum, even).astype(BF16)
            ad[1, wide(b), p * pw : (p + 1) * pw] = jnp.where(low_half, odd, dnum).astype(BF16)
        for c in range(nb // nw):
            at = b * (nb // nw) + c
            reach = reached(at)
            for p in range(pairs):
                ge, go = (
                    dot_lt(
                        jnp.where(reach, ad[o, block(at), p * pw : (p + 1) * pw].astype(F32), 0.0).astype(BF16),
                        phq[p, block(at), o * feat_n : (o + 1) * feat_n],
                    )
                    for o in range(2)
                )
                lst[at, p, :pw] = jnp.where(low_row, ge, go)
                lst[at, p, pw : pw + 8] = jnp.broadcast_to(ge[hw : hw + 1] + ge[hw + 1 : hw + 2], (8, feat_n))
                lst[at, p, pw + 8 :] = jnp.broadcast_to(go[0:1] + go[1:2], (8, feat_n))

        @pl.when(b == 0)
        def _():
            a_finish(tn - 1)
            b_finish(3)
            c_start(3)

        return (
            gl2 + jnp.sum(dn2 * scaled, 0, keepdims=True),
            gbo + jnp.sum(dob.astype(F32), 0, keepdims=True),
            gbd + jnp.sum(dy, 0, keepdims=True),
        )

    zero_row = jnp.zeros((1, width), F32)
    gl2, gbo, gbd = lax.fori_loop(0, nw, branch_block, (zero_row,) * 3)
    store_layer()
    vec[1:2] = gbo
    vec[2:3] = gl2
    vec[3:4] = gbd
    half_blocks = nb // 2

    def grad_at(j, b):
        if isinstance(b, int):
            return j, b // half_blocks, pl.ds((b % half_blocks) * BR, BR)
        rows = pl.ds(pl.multiple_of(lax.rem(b, half_blocks) * BR, BR), BR)
        return j, lax.div(b, half_blocks), rows

    half = rows_n // 2

    def weight_grad(ja, pa, jb, pb):
        total = 0.0
        for h in range(2):
            both = [wfull[j, h, :half, lanes(p)] for j, p in ((ja, pa), (jb, pb))]
            total = total + dot_lt(n1s[h * half : (h + 1) * half], jnp.concatenate(both, 1))
        return total

    def arg_back(darg, x, p):
        both = dot_rt(darg, featx[p])
        return (both[:, :pw] + (2.0 * x.astype(F32)) * both[:, pw:]) * shrink

    out_grad = dot_lt(attn[...], n2s[...])
    for i in range(2):
        k_a_start(i, out_grad[:, i * 2 * pw : (i + 1) * 2 * pw])

    def query_half(i, _):
        down_slots(i, 0, 2 * pairs)
        p, half = lax.div(i, 2), lax.rem(i, 2)
        for c in range(nb // 2):
            b = half * (nb // 2) + c
            se, so = state_halves(sb[b, p].astype(F32))
            reach = reached(b)
            ve, vo = values_of(p, b)
            dargs = []
            for o, (val, st) in enumerate(((ve, se), (vo, so))):
                dn = ad[o, block(b), lanes(p)]
                cdn = jnp.where(reach, dn.astype(F32), 0.0).astype(BF16)
                fq = phq[p, block(b), o * feat_n : (o + 1) * feat_n]
                fk = phk[p, block(b), o * feat_n : (o + 1) * feat_n]
                da = jnp.where(mask[b].astype(F32) > 0, dot_rt(dn, val.astype(BF16)), 0.0).astype(BF16)
                dfq = dot(da, fk) + dot(cdn, st)
                dargs.append((dfq * fq.astype(F32)).astype(BF16))
            wfull[grad_at(0, b) + (lanes(p),)] = arg_back(
                jnp.concatenate(dargs, 1), qs[p, block(b)], p
            ).astype(BF16)

        @pl.when(i == 1)
        def _():
            k_a_finish(0)
            k_a_finish(1)
            b_finish(2)

        @pl.when(i == 3)
        def _():
            k_a_start(2, weight_grad(0, 0, 0, 1))

        @pl.when(i == 5)
        def _():
            k_a_finish(2)
            b_finish(0)

        @pl.when(i == 7)
        def _():
            k_a_start(3, weight_grad(0, 2, 0, 3))
            c_start(2)

        return 0

    lax.fori_loop(0, 2 * pairs, query_half, 0)

    def key_pair(p, _):
        down_slots(2 * (pairs + p), 2 * pairs, 4 * pairs)

        @pl.when(t == 0)
        def _():
            down_copy(p).wait_recv()

        grad = chb_in[p].astype(F32)
        for b in range(nb - 1, -1, -1):
            top = grad[:pw]
            halves = []
            for o in range(2):
                dz = jnp.broadcast_to(grad[pw + 8 * o : pw + 8 * o + 1], top.shape)
                dz_hi = dz.astype(BF16).astype(F32)
                at = hw * (1 - o)
                filler = jnp.where(row_id == at, dz_hi, jnp.where(row_id == at + 1, dz - dz_hi, 0.0))
                halves.append(
                    (jnp.where(low_row, top, filler) if o == 0 else jnp.where(low_row, filler, top)).astype(BF16)
                )
            end = ending(b)
            ve, vo = values_of(p, b)
            dargs, dvs = [], []
            for o, (val, ds) in enumerate(((ve, halves[0]), (vo, halves[1]))):
                dn = ad[o, block(b), lanes(p)]
                fq = phq[p, block(b), o * feat_n : (o + 1) * feat_n]
                fk = phk[p, block(b), o * feat_n : (o + 1) * feat_n]
                at = jnp.where(maskt[b].astype(F32) > 0, dot_rt(fk, fq), 0.0).astype(BF16)
                dat = jnp.where(maskt[b].astype(F32) > 0, dot_rt(val.astype(BF16), dn), 0.0).astype(BF16)
                ev = jnp.where(end, val, 0.0).astype(BF16)
                dfk = dot(dat, fq) + dot(ev, ds)
                dargs.append((dfk * fk.astype(F32)).astype(BF16))
                dvs.append(dot(at, dn) + jnp.where(end, dot_rt(fk, ds), 0.0))
            wfull[grad_at(1, b) + (lanes(p),)] = arg_back(
                jnp.concatenate(dargs, 1), ks[p, block(b)], p
            ).astype(BF16)
            wfull[grad_at(2, b) + (lanes(p),)] = jnp.where(
                low_lane, dvs[0], dvs[1]
            ).astype(BF16)
            if b > 0:
                grad = keep_of(b) * grad + lst[b, p]

        k_a_start(4 + p, weight_grad(1, p, 2, p))

        @pl.when(p == 0)
        def _():
            k_a_finish(3)
            s_b_finish(0)
            s_b_finish(1)

        @pl.when(p >= 1)
        def _():
            k_a_finish(3 + p)

        @pl.when(p == 1)
        def _():
            s_b_finish(2)

        @pl.when(p == 2)
        def _():
            c_finish()
            s_b_finish(3)
            s_middle(0)
            s_middle(1)

        @pl.when(p == 3)
        def _():
            s_b_finish(4)
            s_middle(2)

        return 0

    lax.fori_loop(0, pairs, key_pair, 0)

    def input_block(b, gl1):
        dn1 = dot_rt(wfull[0, b, :WR], wqkv[:, :width])
        for j in range(1, 3):
            dn1 = dn1 + dot_rt(wfull[j, b, :WR], wqkv[:, j * width : (j + 1) * width])
        scaled, inverse = normalized(tok[wide(b)].astype(F32))
        igrad[wide(b)] += norm_back(dn1, g1[...], scaled, inverse)
        store_grad(b)

        @pl.when(b == 0)
        def _():
            k_a_finish(7)
            s_middle(3)

        @pl.when(b == 1)
        def _():
            s_b_finish(5)
            s_middle(4)

        return gl1 + jnp.sum(dn1 * scaled, 0, keepdims=True)

    vec[0:1] = lax.fori_loop(0, nw, input_block, zero_row)
    va_copy = remote(vec, va, va_s, va_r, core_dev)
    va_copy.start()
    k_b_finish(6)
    va_copy.wait_recv()
    vb[0] = vec[...] + va[...]
    vb_copies = [remote(vb.at[0], vb.at[k], vb_s, vb_r, peer_dev(k)) for k in range(1, npeer)]
    for copy in vb_copies:
        copy.start()
    k_b_finish(7)
    s_c_finish(0)
    s_c_finish(1)
    s_c_finish(2)
    s_middle(5)
    s_c_finish(3)
    s_c_finish(4)
    arrived(vb.at[pl.ds(1, npeer - 1)], vb_r)
    total = vb[peers[0]]
    for j in range(1, npeer):
        total = total + vb[peers[j]]
    vc[0] = total
    vc_copies = [remote(vc.at[0], vc.at[k], vc_s, vc_r, z_dev(k)) for k in range(1, tn)]
    for copy in vc_copies:
        copy.start()
    k_c_finish(6)
    k_c_finish(7)
    s_c_finish(5)
    d_finish()
    for i in range(4):
        k_d_finish(i)
    arrived(vc.at[pl.ds(1, tn - 1)], vc_r)
    total = vc[zs[0]]
    for j in range(1, tn):
        total = total + vc[zs[j]]
    own = vc[0, 4:5]
    for k in range(1, tn):
        own = own + vc[k, 4 + k : 5 + k]
    vec_out[...] = total
    vec_out[4:5] = own
    k_d_finish(4)
    k_d_finish(6)
    k_d_finish(7)
    k_d_finish(5)
    e_finish()
    store_fin().start()
    for i in (0, 1, 2, 3, 4, 6, 7, 5):
        k_e_finish(i)
        store_fink(i).start()
    sent(vec, va_s)
    sent(vb.at[pl.ds(1, npeer - 1)], vb_s)
    sent(vc.at[pl.ds(1, tn - 1)], vc_s)
    sent(gbuf.at[:, 0], a_s)
    sent(rb, b_s)
    sent(rc, c_s)
    sent(fin.at[0, pl.ds(0, (npeer - 1) * rp)], d_s)
    sent(fin.at[0], e_s)
    sent(kbuf.at[:, 0], ka_s)
    sent(krb, kb_s)
    sent(krc.at[pl.ds(0, 2), pl.ds(1, tn - 1)], kc_s.at[0])
    sent(krc.at[pl.ds(0, 6), pl.ds(0, levels)], kc_s.at[1])
    sent(fink.at[:, 0, pl.ds(0, (npeer - 1) * rp)], kd_s)
    sent(fink.at[:, 0], ke_s)

    @pl.when(t < tn - 1)
    def _():
        sent(chf_out, chf_s)

    @pl.when(t > 0)
    def _():
        sent(chb_out, chb_s)

    pltpu.make_async_copy(layer_h, layer_h, out_s.at[0]).wait()
    pltpu.make_async_copy(igrad, igrad_h, out_s.at[1]).wait()
    store_fin().wait()
    pltpu.make_async_copy(fink, fink_h, out_s.at[3]).wait()


def finish_kernel(
    layer_in, igrad_in, fin_h, fink_h, vec, layer_out, igrad, gwq_h, gwo_h, gwi_h, gwd_h, gl1, gbo, gl2, gbi, gbd,
    layer_v, igrad_v, fin, fink, gwq, gwo, gwi, gwd, in_s, out_s,
):
    used = [0, 0]

    def move(src, dst, out, parts):
        sems, copies = (in_s, out_s)[out], []
        size = src.shape[0] // parts
        for k in range(parts):
            at = pl.ds(k * size, size)
            copies.append(pltpu.make_async_copy(src.at[at], dst.at[at], sems.at[used[out]]))
            used[out] += 1
            copies[-1].start()
        return copies

    def wait(copies):
        for copy in copies:
            copy.wait()

    pairs = fink.shape[0] // 2
    width, pw = fink.shape[2:]
    a, b, c, d = (
        move(src, dst, 0, parts)
        for src, dst, parts in ((fink_h, fink, 8), (fin_h, fin, 2), (layer_in, layer_v, 4), (igrad_in, igrad_v, 4))
    )
    for row, out in enumerate((gl1, gbo, gl2, gbd, gbi)):
        out[...] = vec[row : row + 1]
    wait(a)
    stores = []
    quarter = width // 4
    for k in range(4):
        rows = pl.ds(k * quarter, quarter)
        for p in range(pairs):
            at = slice(p * pw, (p + 1) * pw)
            gwq[rows, at] = fink[2 + p // 2, p % 2, rows].astype(F32)
            gwq[rows, width + p * pw : width + (p + 1) * pw] = fink[4 + p, 0, rows].astype(F32)
            gwq[rows, 2 * width + p * pw : 2 * width + (p + 1) * pw] = fink[4 + p, 1, rows].astype(F32)
            gwo[rows, at] = fink[p // 2, p % 2, rows].astype(F32)
        stores += move(gwq.at[rows], gwq_h.at[rows], 1, 1)
        stores += move(gwo.at[rows], gwo_h.at[rows], 1, 1)
    wait(b)
    gwi[...] = fin[0].astype(F32)
    stores += move(gwi, gwi_h, 1, 2)
    wait(c)
    stores += move(layer_v, layer_out, 1, 2)
    wait(d)
    stores += move(igrad_v, igrad, 1, 4)
    gwd[...] = fin[1].astype(F32).T
    stores += move(gwd, gwd_h, 1, 2)
    wait(stores)


def local(
    tn,
    dpn,
    tokens,
    cotangent,
    seq_lengths,
    features,
    ln1_gain,
    w_qkv,
    w_out,
    b_out,
    ln2_gain,
    w_in,
    b_in,
    w_down,
    b_down,
):
    rows_n, width = tokens.shape
    heads, hw, feat_n = features.shape
    pairs, pw, nb = heads // 2, 2 * hw, rows_n // BR
    ffl = w_in.shape[1]
    npeer = dpn // 2
    rp = width // npeer
    vrows = -(-(4 + tn) // 8) * 8
    dma = pltpu.SemaphoreType.DMA
    vmem = pl.BlockSpec(memory_space=pltpu.VMEM)
    anywhere = pl.BlockSpec(memory_space=pl.ANY)

    def scratch(shape, dtype=BF16):
        return pltpu.VMEM(shape, dtype)

    out = pl.pallas_call(
        functools.partial(layer_kernel, tn, dpn),
        out_shape=(
            jax.ShapeDtypeStruct((rows_n, width), BF16),
            jax.ShapeDtypeStruct((rows_n, width), F32),
            jax.ShapeDtypeStruct((2, width, width), BF16),
            jax.ShapeDtypeStruct((8, 2, width, pw), BF16),
            jax.ShapeDtypeStruct((vrows, width), F32),
        ),
        in_specs=[pl.BlockSpec(memory_space=pltpu.SMEM)]
        + [anywhere] * 10,
        out_specs=(anywhere,) * 4 + (vmem,),
        scratch_shapes=[
            scratch((2, width, width)),
            scratch((8, 2, width, pw)),
            scratch((1, width), F32),
            scratch((1, width), F32),
            scratch((1, 2 * width + ffl), F32),
            scratch((rows_n, width)),
            scratch((rows_n, width)),
            scratch((heads, hw, feat_n)),
            scratch((width, 3 * width)),
            scratch((width, width)),
            scratch((rows_n, width), F32),
            scratch((tn, 2, width, ffl)),
            scratch((tn, 8, ffl), F32),
            scratch((rows_n, width)),
            scratch((pairs, rows_n, pw)),
            scratch((pairs, rows_n, pw)),
            scratch((pairs, rows_n, pw)),
            scratch((pairs, rows_n, 2 * feat_n)),
            scratch((pairs, rows_n, 2 * feat_n)),
            scratch((pairs, 2 * pw, 2 * feat_n)),
            scratch((2 * pw, 2 * pw)),
            scratch((2 * pw, pw)),
            scratch((nb, BR, BR)),
            scratch((nb, BR, BR)),
            scratch((nb + 1, pairs, pw + 16, feat_n), F32),
            scratch((nb, pairs, pw + 16, feat_n)),
            scratch((rows_n, width), F32),
            scratch((rows_n, width)),
            scratch((rows_n, width), F32),
            scratch((rows_n, width), F32),
            scratch((rows_n, 1), F32),
            scratch((rows_n, width)),
            scratch((2, rows_n, width)),
            scratch((pairs, pw + 16, feat_n)),
            scratch((pairs, pw + 16, feat_n)),
            scratch((pairs, pw + 16, feat_n)),
            scratch((pairs, pw + 16, feat_n)),
            scratch((tn, 2, width, width)),
            scratch((2, width, width)),
            scratch((4, npeer - 1, rp, width)),
            scratch((tn - 1, rp, width)),
            scratch((8, 2, width, pw)),
            scratch((4, width, pw)),
            scratch((8, npeer - 1, rp, pw)),
            scratch((8, max(tn, 2 * (tn - 1).bit_length()), rp, pw)),
            scratch((vrows, width), F32),
            scratch((vrows, width), F32),
            scratch((npeer, vrows, width), F32),
            scratch((tn, vrows, width), F32),
            dma((10,)),
            dma((4,)),
            dma(()),
            dma(()),
            dma(()),
            dma((tn - 1,)),
            dma(()),
            dma((tn - 1,)),
            dma(()),
            dma((tn - 1,)),
            dma(()),
            dma((pairs,)),
            dma(()),
            dma((pairs,)),
            dma(()),
            dma((2,)),
            dma(()),
            dma((tn,)),
            dma(()),
            dma((tn - 1,)),
            dma(()),
            dma(()),
            dma(()),
            dma(()),
            dma(()),
            dma((4,)),
            dma(()),
            dma((8,)),
            dma((2,)),
            dma((8, (tn - 1).bit_length())),
            dma(()),
            dma((8,)),
            dma(()),
            dma((8,)),
            dma(()),
            dma(()),
            dma(()),
            dma(()),
            dma(()),
            dma(()),
        ],
        compiler_params=pltpu.CompilerParams(
            collective_id=0, has_side_effects=True, vmem_limit_bytes=63 * 1024 * 1024
        ),
    )(
        seq_lengths,
        tokens,
        cotangent,
        features,
        ln1_gain[None],
        w_qkv,
        w_out,
        lax.optimization_barrier(jnp.concatenate([b_out, b_in, b_down]).astype(F32))[None],
        ln2_gain[None],
        w_in,
        w_down,
    )
    row = jax.ShapeDtypeStruct((1, width), F32)

    def square(n):
        return jax.ShapeDtypeStruct((width, n * width), F32)

    done = pl.pallas_call(
        finish_kernel,
        out_shape=(out[0], out[1], square(3), square(1), square(1), square(1)) + (row,) * 5,
        in_specs=[anywhere] * 4 + [vmem],
        out_specs=(anywhere,) * 6 + (vmem,) * 5,
        scratch_shapes=[
            scratch((rows_n, width)),
            scratch((rows_n, width), F32),
            scratch((2, width, width)),
            scratch((8, 2, width, pw)),
            scratch((width, 3 * width), F32),
            scratch((width, width), F32),
            scratch((width, width), F32),
            scratch((width, width), F32),
            dma((18,)),
            dma((18,)),
        ],
        compiler_params=pltpu.CompilerParams(vmem_limit_bytes=63 * 1024 * 1024),
    )(*out)
    layer_out, input_grad, gwq, gwo, gwi, gwd, gl1, gbo, gl2, gbi, gbd = done
    return (
        layer_out,
        input_grad,
        gl1[0],
        gwq,
        gwo,
        gbo[0],
        gl2[0],
        gwi,
        gbi[0],
        gwd,
        gbd[0],
    )


def solution(mesh):
    tn, dpn = mesh.shape["tensor"], mesh.shape["dp"]
    rows = P(("dp", "tensor"), None)
    return jax.shard_map(
        functools.partial(local, tn, dpn),
        mesh=mesh,
        in_specs=(
            rows,
            rows,
            P("dp", None),
            P(),
            P(),
            P(),
            P(),
            P(),
            P(),
            P(None, "tensor"),
            P("tensor"),
            P("tensor", None),
            P(),
        ),
        out_specs=(
            rows,
            rows,
            P(),
            P(),
            P(),
            P(),
            P(),
            P(None, "tensor"),
            P("tensor"),
            P("tensor", None),
            P(),
        ),
        check_vma=False,
    )
```

```python
import functools

import jax
import jax.numpy as jnp
from jax import lax
from jax.experimental import pallas as pl
from jax.experimental.pallas import tpu as pltpu
from jax.sharding import PartitionSpec as P

MESH = pl.DeviceIdType.MESH
F32 = jnp.float32
BF16 = jnp.bfloat16
EPSILON = 1e-05
BR = 256
WR = 512
SQRT_2_OVER_PI = 0.7978845608028654
CUBIC = 0.044715


def dot(a, b):
    return jnp.dot(a, b, preferred_element_type=F32)


def dot_rt(a, b):
    return lax.dot_general(a, b, (((1,), (1,)), ((), ())), preferred_element_type=F32)


def dot_lt(a, b):
    return lax.dot_general(a, b, (((0,), (0,)), ((), ())), preferred_element_type=F32)


def xor(a, b, size):
    out, bit = 0, 1
    while bit < size:
        out = out + bit * lax.rem(lax.div(a, bit) + (b // bit if isinstance(b, int) else lax.div(b, bit)), 2)
        bit *= 2
    return out


def iota(shape, axis):
    return lax.broadcasted_iota(jnp.int32, shape, axis)


def layer_kernel(
    tn,
    dpn,
    lens,
    tok_h,
    cot_h,
    feats_h,
    g1_h,
    wqkv_h,
    wout_h,
    bout_h,
    g2_h,
    win_h,
    bin_h,
    wdn_h,
    bdn_h,
    layer_h,
    igrad_h,
    fin_h,
    fink_h,
    vec_out,
    fin,
    fink,
    g1,
    g2,
    bout,
    bin_,
    bdn,
    tok,
    cot,
    feats,
    wqkv,
    wout,
    igrad,
    wfull,
    bfull,
    n1s,
    qs,
    ks,
    vs,
    phq,
    phk,
    featx,
    norms,
    bsw,
    mask,
    maskt,
    lst,
    sb,
    rsw_s,
    attn,
    facc,
    xh2,
    rstd2,
    n2s,
    ad,
    chf_in,
    chf_out,
    chb_in,
    chb_out,
    gbuf,
    ra,
    rb,
    rc,
    kbuf,
    kra,
    krb,
    krc,
    vec,
    va,
    vb,
    vc,
    in_s,
    out_s,
    bz_s,
    bz_r,
    wz_s,
    wz_r,
    wx_s,
    wx_r,
    wc_s,
    wc_r,
    chf_s,
    chf_r,
    chb_s,
    chb_r,
    a_s,
    a_r,
    b_s,
    b_r,
    c_s,
    c_r,
    d_s,
    d_r,
    e_s,
    e_r,
    ka_s,
    ka_r,
    kb_s,
    kb_r,
    kc_s,
    kc_r,
    kd_s,
    kd_r,
    ke_s,
    ke_r,
    va_s,
    va_r,
    vb_s,
    vb_r,
    vc_s,
    vc_r,
):
    rows_n, width = tok.shape
    heads, hw, feat_n = feats.shape
    pairs = heads // 2
    pw = 2 * hw
    nb = rows_n // BR
    seqs = lens.shape[1]
    shrink = hw ** (-0.25)
    featscale = feat_n ** (-0.5)
    npeer = dpn // 2
    rp = width // npeer

    dp = lax.axis_index("dp")
    t = lax.axis_index("tensor")
    cb = lax.rem(dp, 2)
    q = lax.div(dp, 2)
    core_dev = (dp + 1 - 2 * cb, t)

    peers = [xor(q, k, npeer) for k in range(npeer)]
    zs = [xor(t, k, tn) for k in range(tn)]

    def peer_dev(k):
        return (2 * peers[k] + cb, t)

    def z_dev(k):
        return (dp, zs[k])

    row_starts = [pl.multiple_of(peer * rp, rp) for peer in peers]

    def own_rows():
        return pl.ds(row_starts[0], rp)

    def peer_rows(k):
        return pl.ds(row_starts[k], rp)

    def load(i, src, dst):
        return pltpu.make_async_copy(src, dst, in_s.at[i])

    pairs_in = {
        "feats": (feats_h, feats),
        "g1": (g1_h, g1),
        "g2": (g2_h, g2),
        "bout": (bout_h, bout),
        "bin": (bin_h, bin_),
        "bdn": (bdn_h, bdn),
        "win": (win_h, wfull.at[0, 0]),
        "wdn": (wdn_h, wfull.at[0, 1]),
        "tok": (tok_h, tok),
        "wqkv": (wqkv_h, wqkv),
        "wout": (wout_h, wout),
        "cot": (cot_h, cot),
    }
    loads = {name: load(i, *pair) for i, (name, pair) in enumerate(pairs_in.items())}
    for copy in loads.values():
        copy.start()

    def store_layer():
        half = layer_h.shape[0] // 2
        for h in range(2):
            pltpu.make_async_copy(wfull.at[tn - 1, h], layer_h.at[pl.ds(h * half, half)], out_s.at[0]).start()

    def store_grad(b):
        rows = pl.ds(pl.multiple_of(b * WR, WR), WR)
        pltpu.make_async_copy(igrad.at[rows], igrad_h.at[rows], out_s.at[1]).start()

    def store_fin():
        return pltpu.make_async_copy(fin, fin_h, out_s.at[2])

    def store_fink(i):
        return pltpu.make_async_copy(fink.at[i], fink_h.at[i], out_s.at[3])

    bar = pltpu.get_barrier_semaphore()
    targets = [core_dev] + [peer_dev(k) for k in range(1, npeer)] + [z_dev(k) for k in range(1, tn)]
    for dev in targets:
        pl.semaphore_signal(bar, inc=1, device_id=dev, device_id_type=MESH)

    def remote(src, dst, ss, rs, dev):
        return pltpu.make_async_remote_copy(
            src_ref=src, dst_ref=dst, send_sem=ss, recv_sem=rs, device_id=dev, device_id_type=MESH
        )

    def arrived(ref, sem):
        remote(ref, ref, a_s, sem, core_dev).wait_recv()

    def sent(ref, sem):
        remote(ref, ref, sem, a_r.at[0], core_dev).wait_send()

    def bz_copy(k):
        return remote(bfull.at[0], bfull.at[k], bz_s, bz_r, z_dev(k))

    def wz_copy(k):
        source, via = (0, k) if k == 1 or k % 2 == 0 else (k - 1, 1)
        return remote(
            wfull.at[source, cb, own_rows()], wfull.at[k, cb, own_rows()], wz_s, wz_r.at[k - 1], z_dev(via)
        )

    def wx_copy(k, j):
        here = wfull.at[k, cb, own_rows()]
        return remote(here, here, wx_s, wx_r.at[k - 1], peer_dev(j))

    def wc_copy(k):
        return remote(wfull.at[k, cb], wfull.at[k, cb], wc_s, wc_r.at[k - 1], core_dev)

    def wc_recv(k):
        here = wfull.at[k, 1 - cb]
        return remote(here, here, wc_s, wc_r.at[k - 1], core_dev)

    def w_spread(k):
        wz_copy(k).wait_recv()
        if k > 1 and k % 2 == 0:
            wz_copy(k + 1).start()
        for j in range(1, npeer):
            wx_copy(k, j).start()

    def w_swap(k):
        arrived(wfull.at[k, cb, pl.ds(0, (npeer - 1) * rp)], wx_r.at[k - 1])
        wc_copy(k).start()

    levels = (tn - 1).bit_length()
    up_first = (1, 3, 5, 7), (8, 9, 10, 12)

    def up_due(at, p):
        return up_first[at - 1][p % 4] if at < 3 and p < 4 else 10 + p

    def down_due(hops, p):
        due = min(3 * hops + p, 8 + 2 * p)
        return due + due % 2 if due > 8 else due

    def up_copy(p):
        return remote(chf_out.at[p], chf_in.at[p], chf_s, chf_r.at[p], (dp, lax.rem(t + 1, tn)))

    def up_handle(p):
        @pl.when(t > 0)
        def _():
            up_copy(p).wait_recv()

        chf_out[p] = (lst[nb, p] + passing * chf_in[p].astype(F32)).astype(BF16)
        up_copy(p).start()

    def up_slots(k, low, high):
        for at in range(1, tn - 1):
            for p in range(pairs):
                if low <= up_due(at, p) < high:

                    @pl.when((t == at) & (k == up_due(at, p)))
                    def _(p=p):
                        up_handle(p)

    def down_copy(p):
        return remote(chb_out.at[p], chb_in.at[p], chb_s, chb_r.at[p], (dp, lax.rem(t + tn - 1, tn)))

    def down_handle(p):
        @pl.when(t < tn - 1)
        def _():
            down_copy(p).wait_recv()

        own = lst[nb - 1, p]
        for b in range(nb - 2, -1, -1):
            own = keep_of(b) * own + lst[b, p]
        chb_out[p] = (own + passing * chb_in[p].astype(F32)).astype(BF16)
        down_copy(p).start()

    def down_slots(k, low, high):
        for hops in range(tn - 1):
            for p in range(pairs):
                if low <= down_due(hops, p) < high:

                    @pl.when((t == tn - 1 - hops) & (k == down_due(hops, p)))
                    def _(p=p):
                        down_handle(p)

    def place_of(turn):
        return jnp.where(turn < tn // 2, 2 * turn + 1, 2 * (tn - 1 - turn))

    def a_copy(turn):
        turn = jnp.int32(turn)
        return remote(
            gbuf.at[place_of(turn), 1 - cb], ra.at[lax.rem(turn, 2)], a_s, a_r.at[lax.rem(turn, 2)], core_dev
        )

    def b_copy(s, k):
        s = jnp.int32(s)
        return remote(gbuf.at[s, cb, peer_rows(k)], rb.at[lax.rem(s, 4), k - 1], b_s, b_r.at[s], peer_dev(k))

    def c_copy(s):
        return remote(gbuf.at[s, cb, own_rows()], rc.at[s - 1], c_s, c_r.at[s - 1], z_dev(s & -s))

    def d_copy(k):
        here = fin.at[cb, own_rows()]
        return remote(here, here, d_s, d_r, peer_dev(k))

    def e_copy():
        return remote(fin.at[cb], fin.at[cb], e_s, e_r, core_dev)

    def e_recv():
        return remote(fin.at[1 - cb], fin.at[1 - cb], e_s, e_r, core_dev)

    def ka_copy(i):
        i = jnp.int32(i)
        return remote(kbuf.at[i, 1 - cb], kra.at[lax.rem(i, 4)], ka_s, ka_r.at[lax.rem(i, 4)], core_dev)

    def kb_copy(i, k):
        return remote(
            kbuf.at[i, cb, peer_rows(k)], krb.at[i, k - 1], kb_s, kb_r.at[i], peer_dev(k)
        )

    def kc_copy(i, k):
        return remote(krc.at[i, 0], krc.at[i, k], kc_s.at[0], kc_r.at[i, 0], z_dev(k))

    def ks_copy(i, l):
        return remote(
            krc.at[i, 2 * l], krc.at[i, 2 * l + 1], kc_s.at[1], kc_r.at[i, l], z_dev(1 << l)
        )

    def kd_copy(i, k):
        here = fink.at[i, cb, own_rows()]
        return remote(here, here, kd_s, kd_r.at[i], peer_dev(k))

    def ke_copy(i):
        return remote(fink.at[i, cb], fink.at[i, cb], ke_s, ke_r.at[i], core_dev)

    def ke_recv(i):
        return remote(fink.at[i, 1 - cb], fink.at[i, 1 - cb], ke_s, ke_r.at[i], core_dev)

    def a_start(turn):
        a_copy(turn).start()

    def a_finish(turn):
        turn = jnp.int32(turn)
        a_copy(turn).wait_recv()
        s = place_of(turn)
        gbuf[s, cb] = (gbuf[s, cb].astype(F32) + ra[lax.rem(turn, 2)].astype(F32)).astype(BF16)
        for k in range(1, npeer):
            b_copy(s, k).start()

    def b_sum(s):
        s = jnp.int32(s)
        arrived(rb.at[lax.rem(s, 4)], b_r.at[s])
        total = gbuf[s, cb, own_rows()].astype(F32)
        for k in range(1, npeer):
            total = total + rb[lax.rem(s, 4), k - 1].astype(F32)
        return total.astype(BF16)

    def b_finish(s):
        gbuf[s, cb, own_rows()] = b_sum(s)

    def c_add(s):
        step = 1
        while step < (s & -s if s else tn):
            c_copy(s + step).wait_recv()
            gbuf[s, cb, own_rows()] = (
                gbuf[s, cb, own_rows()].astype(F32) + rc[s + step - 1].astype(F32)
            ).astype(BF16)
            step *= 2

    def c_start(s):
        c_add(s)
        c_copy(s).start()

    def c_finish():
        total = gbuf[0, cb, own_rows()].astype(F32)
        step = 1
        while step < tn:
            c_copy(step).wait_recv()
            total = total + rc[step - 1].astype(F32)
            step *= 2
        fin[cb, own_rows()] = total.astype(BF16)
        for k in range(1, npeer):
            d_copy(k).start()

    def d_finish():
        arrived(fin.at[0, pl.ds(0, (npeer - 1) * rp)], d_r)
        e_copy().start()

    def e_finish():
        e_recv().wait_recv()

    def k_a_start(i, both):
        kbuf[i, 0] = both[:, :pw].astype(BF16)
        kbuf[i, 1] = both[:, pw:].astype(BF16)
        ka_copy(i).start()

    def k_a_finish(i):
        i = jnp.int32(i)
        ka_copy(i).wait_recv()
        kbuf[i, cb] = (kbuf[i, cb].astype(F32) + kra[lax.rem(i, 4)].astype(F32)).astype(BF16)
        for k in range(1, npeer):
            kb_copy(i, k).start()

    def k_b_sum(i):
        arrived(krb.at[i], kb_r.at[i])
        total = kbuf[i, cb, own_rows()].astype(F32)
        for k in range(1, npeer):
            total = total + krb[i, k - 1].astype(F32)
        krc[i, 0] = total.astype(BF16)

    def k_spread(i, total):
        fink[i, cb, own_rows()] = total.astype(BF16)
        for k in range(1, npeer):
            kd_copy(i, k).start()

    def k_b_finish(i):
        k_b_sum(i)
        for k in range(1, tn):
            kc_copy(i, k).start()

    def k_c_finish(i):
        arrived(krc.at[i, pl.ds(1, tn - 1)], kc_r.at[i, 0])
        total = krc[i, zs[0]].astype(F32)
        for j in range(1, tn):
            total = total + krc[i, zs[j]].astype(F32)
        k_spread(i, total)

    def s_b_finish(i):
        k_b_sum(i)
        ks_copy(i, 0).start()

    def s_sum(i, l):
        ks_copy(i, l).wait_recv()
        return krc[i, 2 * l].astype(F32) + krc[i, 2 * l + 1].astype(F32)

    def s_middle(i):
        for l in range(levels - 1):
            krc[i, 2 * l + 2] = s_sum(i, l).astype(BF16)
            ks_copy(i, l + 1).start()

    def s_c_finish(i):
        k_spread(i, s_sum(i, levels - 1))

    def k_d_finish(i):
        arrived(fink.at[i, 0, pl.ds(0, (npeer - 1) * rp)], kd_r.at[i])
        ke_copy(i).start()

    def k_e_finish(i):
        ke_recv(i).wait_recv()

    offsets = [jnp.int32(0)]
    for c in range(1, seqs):
        offsets.append(offsets[-1] + lens[0, c - 1])
    first = t * rows_n

    def seg_at(r):
        seg = -1
        for off in offsets:
            seg = seg + jnp.where(r >= off, 1, 0)
        return seg

    def seg_array(shape, axis, start):
        places = iota(shape, axis) + start
        seg = jnp.full(shape, -1, jnp.int32)
        for off in offsets:
            seg = seg + jnp.where(places >= off, 1, 0)
        return seg

    before = seg_at(first - 1)
    closing = seg_at(first + rows_n - 1)
    passing = jnp.where(before == closing, 1.0, 0.0)

    def prev_of(b):
        return seg_at(first + b * BR - 1)

    def last_of(b):
        return seg_at(first + b * BR + BR - 1)

    def keep_of(b):
        return jnp.where(prev_of(b) == last_of(b), 1.0, 0.0)

    def ending(b):
        return seg_array((BR, pw), 0, first + b * BR) == last_of(b)

    def reached(b):
        return seg_array((BR, pw), 0, first + b * BR) == prev_of(b)

    def block(b):
        return pl.ds(pl.multiple_of(b * BR, BR), BR)

    nw = rows_n // WR

    def wide(b):
        return pl.ds(pl.multiple_of(b * WR, WR), WR)

    def lanes(p):
        return pl.ds(pl.multiple_of(p * pw, pw), pw)

    def as_row(ref):
        return ref[...].astype(F32).reshape(1, ref.shape[0])

    low_lane = iota((BR, pw), 1) < hw
    low_row = iota((pw, feat_n), 0) < hw
    row_id = iota((pw, feat_n), 0)

    for name in ("feats", "g1", "g2", "bout", "bin", "bdn"):
        loads[name].wait()
    featx[...] = jnp.zeros_like(featx)
    for p in range(pairs):
        for o in range(2):
            featx[p, o * hw : (o + 1) * hw, o * feat_n : (o + 1) * feat_n] = feats[2 * p + o]
            featx[p, pw + o * hw : pw + (o + 1) * hw, o * feat_n : (o + 1) * feat_n] = jnp.full(
                (hw, feat_n), -0.5, BF16
            )
    ri, ci = iota((2 * pw, pw), 0), iota((2 * pw, pw), 1)
    ro, co = iota((2 * pw, 2 * pw), 0), iota((2 * pw, 2 * pw), 1)
    norms[...] = jnp.where((lax.rem(ro, pw) < hw) == (co < pw), -0.5, 0.0).astype(BF16)
    swap = (lax.rem(ri, pw) < hw) != (ci < hw)
    bsw[...] = jnp.where(swap, 1.0, 0.0).astype(BF16)

    def build_mask(b, _):
        seg_i = seg_array((BR, BR), 0, first + b * BR)
        seg_j = seg_array((BR, BR), 1, first + b * BR)
        same = seg_i == seg_j
        i, j = iota((BR, BR), 0), iota((BR, BR), 1)
        mask[b] = jnp.where(same & (i >= j), 1.0, 0.0).astype(BF16)
        maskt[b] = jnp.where(same & (j >= i), 1.0, 0.0).astype(BF16)
        return 0

    lax.fori_loop(0, nb, build_mask, 0)
    lst[0] = jnp.zeros(lst.shape[1:], F32)
    vec[...] = jnp.zeros_like(vec)

    @pl.when(t == 0)
    def _():
        chf_in[...] = jnp.zeros_like(chf_in)

    @pl.when(t == tn - 1)
    def _():
        chb_in[...] = jnp.zeros_like(chb_in)

    loads["win"].wait()
    loads["wdn"].wait()
    pl.semaphore_wait(bar, len(targets))
    bfull[0] = jnp.broadcast_to(as_row(bin_), bfull.shape[1:])
    for k in range(1, tn):
        bz_copy(k).start()
    wz_copy(1).start()
    wz_copy(2).start()

    def features_of(x, p):
        wide = x.astype(F32)
        square = wide * wide
        high = square.astype(BF16)
        rest = (square - high.astype(F32)).astype(BF16)
        norm = dot(jnp.concatenate([high, rest], 1), norms[...])
        repeats = [norm[:, :pw]] * (feat_n // pw) + [norm[:, pw:]] * (feat_n // pw)
        arg = dot(x, featx[p, :pw]) + jnp.concatenate(repeats, 1)
        return (jnp.exp(arg) * featscale).astype(BF16)

    def normalized(x):
        centre = jnp.mean(x, -1, keepdims=True)
        shifted = x - centre
        inverse = lax.rsqrt(jnp.mean(shifted * shifted, -1, keepdims=True) + EPSILON)
        return shifted * inverse, inverse

    def values_of(p, b):
        wide = vs[p, block(b)].astype(F32)
        return jnp.where(low_lane, wide, 1.0), jnp.where(low_lane, 1.0, wide)

    def keys_block(b, _):
        scaled, _inv = normalized(tok[wide(b)].astype(F32))
        normed = (scaled * g1[...]).astype(BF16)
        n1s[wide(b)] = normed
        key = (dot(normed, wqkv[:, width : 2 * width]) * shrink).astype(BF16)
        val = dot(normed, wqkv[:, 2 * width :]).astype(BF16)
        for p in range(pairs):
            ks[p, wide(b)] = key[:, p * pw : (p + 1) * pw]
            vs[p, wide(b)] = val[:, p * pw : (p + 1) * pw]

        return 0

    loads["tok"].wait()
    loads["wqkv"].wait()
    lax.fori_loop(0, nw, keys_block, 0)

    def state_pair(p, _):
        for c in range(nw):
            phk[p, wide(c)] = features_of(ks[p, wide(c)], p)
        for b in range(nb):
            feat = phk[p, block(b)]
            end = ending(b)
            ve, vo = values_of(p, b)
            ue = dot_lt(jnp.where(end, ve, 0.0).astype(BF16), feat[:, :feat_n])
            uo = dot_lt(jnp.where(end, vo, 0.0).astype(BF16), feat[:, feat_n:])
            keep = keep_of(b)
            lst[b + 1, p, :pw] = keep * lst[b, p, :pw] + jnp.where(low_row, ue, uo)
            lst[b + 1, p, pw : pw + 8] = keep * lst[b, p, pw : pw + 8] + ue[hw : hw + 8]
            lst[b + 1, p, pw + 8 :] = keep * lst[b, p, pw + 8 :] + uo[:8]

        @pl.when(t == 0)
        def _():
            up_handle(p)


        @pl.when(p == 3)
        def _():
            w_spread(1)

        return 0

    lax.fori_loop(0, pairs, state_pair, 0)

    def queries_block(b, _):
        up_slots(b, 0, nw)
        query = (dot(n1s[wide(b)], wqkv[:, :width]) * shrink).astype(BF16)
        for p in range(pairs):
            qs[p, wide(b)] = query[:, p * pw : (p + 1) * pw]

        @pl.when(b == nw - 1)
        def _():
            w_spread(2)

        return 0

    lax.fori_loop(0, nw, queries_block, 0)

    def features_pair(p, _):
        up_slots(nw + p, nw, nw + pairs)
        for b in range(nw):
            phq[p, wide(b)] = features_of(qs[p, wide(b)], p)
        return 0

    lax.fori_loop(0, pairs, features_pair, 0)

    def state_halves(state):
        top = state[:pw]
        even = jnp.where(low_row, top, jnp.broadcast_to(state[pw : pw + 1], top.shape)).astype(BF16)
        odd = jnp.where(low_row, jnp.broadcast_to(state[pw + 8 : pw + 9], top.shape), top).astype(BF16)
        return even, odd

    slot = nw + pairs

    def inside_pair(p, _):
        up_slots(slot + p, slot, slot + pairs)

        @pl.when(p == 3)
        def _():
            w_spread(3)

        for b in range(nb):
            for o, (val, part) in enumerate(zip(values_of(p, b), (facc, xh2))):
                fq = phq[p, block(b), o * feat_n : (o + 1) * feat_n]
                fk = phk[p, block(b), o * feat_n : (o + 1) * feat_n]
                scores = jnp.where(mask[b].astype(F32) > 0, dot_rt(fq, fk), 0.0).astype(BF16)
                part[block(b), lanes(p)] = dot(scores, val.astype(BF16))
        return 0

    lax.fori_loop(0, pairs, inside_pair, 0)

    def attend_pair(p, _):
        up_slots(slot + pairs + p, slot + pairs, slot + 2 * pairs)

        @pl.when(p == 2)
        def _():
            w_swap(1)

        @pl.when(t == tn - 1)
        def _():
            up_copy(p).wait_recv()

        incoming = chf_in[p].astype(F32)
        for b in range(nb):
            first_pass = jnp.where(before == prev_of(b), 1.0, 0.0)
            state = (lst[b, p] + first_pass * incoming).astype(BF16)
            sb[b, p] = state
            reach = reached(b)
            outs = []
            for o, (st, part) in enumerate(zip(state_halves(state.astype(F32)), (facc, xh2))):
                fq = phq[p, block(b), o * feat_n : (o + 1) * feat_n]
                outs.append(part[block(b), lanes(p)] + jnp.where(reach, dot_rt(fq, st), 0.0))
            inverse = 1.0 / jnp.where(low_lane, outs[1], outs[0])
            rsw_s[block(b), lanes(p)] = inverse
            num = jnp.where(low_lane, outs[0], outs[1])
            attn[block(b), lanes(p)] = (num * pltpu.roll(inverse, hw, 1)).astype(BF16)
        return 0

    lax.fori_loop(0, pairs, attend_pair, 0)

    def hidden_block(b, _):
        h1 = tok[wide(b)].astype(F32) + (dot(attn[wide(b)], wout[...]) + as_row(bout))
        scaled, inverse = normalized(h1)
        xh2[wide(b)] = scaled
        rstd2[wide(b)] = inverse
        n2s[wide(b)] = (scaled * g2[...]).astype(BF16)
        facc[wide(b)] = h1 + as_row(bdn)
        return 0

    loads["wout"].wait()
    lax.fori_loop(0, nw, hidden_block, 0)
    loads["cot"].wait()

    def feed_chunk(turn, _):
        s = place_of(turn)

        @pl.when(s > 0)
        def _():
            for k in range(1, tn):

                @pl.when(s == k)
                def _(k=k):
                    wc_recv(k).wait_recv()

        def rows_block(b, total):
            w_in = wfull[s, 0]
            w_dn = wfull[s, 1]
            u = dot(n2s[wide(b)], w_in) + bfull[s, 0:1]
            u2 = u * u
            th = jnp.tanh(u * (SQRT_2_OVER_PI + SQRT_2_OVER_PI * CUBIC * u2))
            half = 0.5 + 0.5 * th
            act = (u * half).astype(BF16)
            slope = half + (0.5 * u) * (1.0 - th * th) * (
                SQRT_2_OVER_PI + 3.0 * SQRT_2_OVER_PI * CUBIC * u2
            )
            ad[0, wide(b)] = act
            facc[wide(b)] += dot(act, w_dn)
            du = (slope * dot_rt(cot[wide(b)], w_dn)).astype(BF16)
            ad[1, wide(b)] = du
            back = dot_rt(du, w_in)

            @pl.when(turn == 0)
            def _():
                igrad[wide(b)] = back

            @pl.when(turn > 0)
            def _():
                igrad[wide(b)] += back

            @pl.when((turn >= 1) & (b == 0))
            def _():
                a_finish(jnp.maximum(turn - 1, 0))

            @pl.when((turn == 0) & (b == 0))
            def _():
                w_swap(2)

            @pl.when((turn == 0) & (b == nw - 1))
            def _():
                w_swap(3)

            return total + jnp.sum(du.astype(F32), 0, keepdims=True)

        total = lax.fori_loop(0, nw, rows_block, jnp.zeros((1, wfull.shape[3]), F32))
        vec[pl.ds(4 + s, 1)] = total

        @pl.when(turn == tn - 1)
        def _():
            b_finish(1)
            c_start(1)

        gbuf[s, 0] = dot_lt(n2s[...], ad[1]).astype(BF16)
        gbuf[s, 1] = dot_lt(cot[...], ad[0]).astype(BF16)
        a_start(turn)
        return 0

    arrived(bfull.at[pl.ds(1, tn - 1)], bz_r)
    lax.fori_loop(0, tn, feed_chunk, 0)
    sent(bfull.at[pl.ds(1, tn - 1)], bz_s)
    sent(wfull.at[pl.ds(0, tn - 1), 0, pl.ds(0, rp)], wz_s)
    sent(wfull.at[pl.ds(0, tn - 1), 0, pl.ds(0, (npeer - 1) * rp)], wx_s)
    sent(wfull.at[pl.ds(0, tn - 1), 0], wc_s)

    def norm_back(dn, gain, scaled, inverse):
        g = dn * gain
        inner = jnp.mean(g, -1, keepdims=True)
        cross = jnp.mean(g * scaled, -1, keepdims=True)
        return inverse * (g - inner - scaled * cross)


    def branch_block(b, carry):
        gl2, gbo, gbd = carry
        wfull[tn - 1, b] = facc[wide(b)].astype(BF16)
        dy = cot[wide(b)].astype(F32)
        dn2 = igrad[wide(b)]
        scaled = xh2[wide(b)]
        dh1 = dy + norm_back(dn2, g2[...], scaled, rstd2[wide(b)])
        igrad[wide(b)] = dh1
        dob = dh1.astype(BF16)
        n2s[wide(b)] = dob
        dattn = dot_rt(dob, wout[...])
        lane_id = iota((WR, pw), 1)
        low_half = lane_id < hw
        for p in range(pairs):
            da = dattn[:, p * pw : (p + 1) * pw]
            inverse = rsw_s[wide(b), p * pw : (p + 1) * pw]
            dnum = da * pltpu.roll(inverse, hw, 1)
            prod = da * attn[wide(b), p * pw : (p + 1) * pw].astype(F32)
            high = prod.astype(BF16)
            rest = (prod - high.astype(F32)).astype(BF16)
            dden = -dot(jnp.concatenate([high, rest], 1), bsw[...]) * inverse
            dhi = dden.astype(BF16).astype(F32)
            dlo = dden - dhi
            even = jnp.where(lane_id == hw, dhi, jnp.where(lane_id == hw + 1, dlo, 0.0))
            odd = jnp.where(lane_id == 0, dhi, jnp.where(lane_id == 1, dlo, 0.0))
            ad[0, wide(b), p * pw : (p + 1) * pw] = jnp.where(low_half, dnum, even).astype(BF16)
            ad[1, wide(b), p * pw : (p + 1) * pw] = jnp.where(low_half, odd, dnum).astype(BF16)
        for c in range(nb // nw):
            at = b * (nb // nw) + c
            reach = reached(at)
            for p in range(pairs):
                ge, go = (
                    dot_lt(
                        jnp.where(reach, ad[o, block(at), p * pw : (p + 1) * pw].astype(F32), 0.0).astype(BF16),
                        phq[p, block(at), o * feat_n : (o + 1) * feat_n],
                    )
                    for o in range(2)
                )
                lst[at, p, :pw] = jnp.where(low_row, ge, go)
                lst[at, p, pw : pw + 8] = jnp.broadcast_to(ge[hw : hw + 1] + ge[hw + 1 : hw + 2], (8, feat_n))
                lst[at, p, pw + 8 :] = jnp.broadcast_to(go[0:1] + go[1:2], (8, feat_n))

        @pl.when(b == 0)
        def _():
            a_finish(tn - 1)
            b_finish(3)
            c_start(3)

        return (
            gl2 + jnp.sum(dn2 * scaled, 0, keepdims=True),
            gbo + jnp.sum(dob.astype(F32), 0, keepdims=True),
            gbd + jnp.sum(dy, 0, keepdims=True),
        )

    zero_row = jnp.zeros((1, width), F32)
    gl2, gbo, gbd = lax.fori_loop(0, nw, branch_block, (zero_row,) * 3)
    store_layer()
    vec[1:2] = gbo
    vec[2:3] = gl2
    vec[3:4] = gbd
    half_blocks = nb // 2

    def grad_at(j, b):
        if isinstance(b, int):
            return j, b // half_blocks, pl.ds((b % half_blocks) * BR, BR)
        rows = pl.ds(pl.multiple_of(lax.rem(b, half_blocks) * BR, BR), BR)
        return j, lax.div(b, half_blocks), rows

    half = rows_n // 2

    def weight_grad(ja, pa, jb, pb):
        total = 0.0
        for h in range(2):
            both = [wfull[j, h, :half, lanes(p)] for j, p in ((ja, pa), (jb, pb))]
            total = total + dot_lt(n1s[h * half : (h + 1) * half], jnp.concatenate(both, 1))
        return total

    def arg_back(darg, x, p):
        both = dot_rt(darg, featx[p])
        return (both[:, :pw] + (2.0 * x.astype(F32)) * both[:, pw:]) * shrink

    out_grad = dot_lt(attn[...], n2s[...])
    for i in range(2):
        k_a_start(i, out_grad[:, i * 2 * pw : (i + 1) * 2 * pw])

    def query_half(i, _):
        down_slots(i, 0, 2 * pairs)
        p, half = lax.div(i, 2), lax.rem(i, 2)
        for c in range(nb // 2):
            b = half * (nb // 2) + c
            se, so = state_halves(sb[b, p].astype(F32))
            reach = reached(b)
            ve, vo = values_of(p, b)
            dargs = []
            for o, (val, st) in enumerate(((ve, se), (vo, so))):
                dn = ad[o, block(b), lanes(p)]
                cdn = jnp.where(reach, dn.astype(F32), 0.0).astype(BF16)
                fq = phq[p, block(b), o * feat_n : (o + 1) * feat_n]
                fk = phk[p, block(b), o * feat_n : (o + 1) * feat_n]
                da = jnp.where(mask[b].astype(F32) > 0, dot_rt(dn, val.astype(BF16)), 0.0).astype(BF16)
                dfq = dot(da, fk) + dot(cdn, st)
                dargs.append((dfq * fq.astype(F32)).astype(BF16))
            wfull[grad_at(0, b) + (lanes(p),)] = arg_back(
                jnp.concatenate(dargs, 1), qs[p, block(b)], p
            ).astype(BF16)

        @pl.when(i == 1)
        def _():
            k_a_finish(0)
            k_a_finish(1)
            b_finish(2)

        @pl.when(i == 3)
        def _():
            k_a_start(2, weight_grad(0, 0, 0, 1))

        @pl.when(i == 5)
        def _():
            k_a_finish(2)
            b_finish(0)

        @pl.when(i == 7)
        def _():
            k_a_start(3, weight_grad(0, 2, 0, 3))
            c_start(2)

        return 0

    lax.fori_loop(0, 2 * pairs, query_half, 0)

    def key_pair(p, _):
        down_slots(2 * (pairs + p), 2 * pairs, 4 * pairs)

        @pl.when(t == 0)
        def _():
            down_copy(p).wait_recv()

        grad = chb_in[p].astype(F32)
        for b in range(nb - 1, -1, -1):
            top = grad[:pw]
            halves = []
            for o in range(2):
                dz = jnp.broadcast_to(grad[pw + 8 * o : pw + 8 * o + 1], top.shape)
                dz_hi = dz.astype(BF16).astype(F32)
                at = hw * (1 - o)
                filler = jnp.where(row_id == at, dz_hi, jnp.where(row_id == at + 1, dz - dz_hi, 0.0))
                halves.append(
                    (jnp.where(low_row, top, filler) if o == 0 else jnp.where(low_row, filler, top)).astype(BF16)
                )
            end = ending(b)
            ve, vo = values_of(p, b)
            dargs, dvs = [], []
            for o, (val, ds) in enumerate(((ve, halves[0]), (vo, halves[1]))):
                dn = ad[o, block(b), lanes(p)]
                fq = phq[p, block(b), o * feat_n : (o + 1) * feat_n]
                fk = phk[p, block(b), o * feat_n : (o + 1) * feat_n]
                at = jnp.where(maskt[b].astype(F32) > 0, dot_rt(fk, fq), 0.0).astype(BF16)
                dat = jnp.where(maskt[b].astype(F32) > 0, dot_rt(val.astype(BF16), dn), 0.0).astype(BF16)
                ev = jnp.where(end, val, 0.0).astype(BF16)
                dfk = dot(dat, fq) + dot(ev, ds)
                dargs.append((dfk * fk.astype(F32)).astype(BF16))
                dvs.append(dot(at, dn) + jnp.where(end, dot_rt(fk, ds), 0.0))
            wfull[grad_at(1, b) + (lanes(p),)] = arg_back(
                jnp.concatenate(dargs, 1), ks[p, block(b)], p
            ).astype(BF16)
            wfull[grad_at(2, b) + (lanes(p),)] = jnp.where(
                low_lane, dvs[0], dvs[1]
            ).astype(BF16)
            if b > 0:
                grad = keep_of(b) * grad + lst[b, p]

        k_a_start(4 + p, weight_grad(1, p, 2, p))

        @pl.when(p == 0)
        def _():
            k_a_finish(3)
            s_b_finish(0)
            s_b_finish(1)

        @pl.when(p >= 1)
        def _():
            k_a_finish(3 + p)

        @pl.when(p == 1)
        def _():
            s_b_finish(2)

        @pl.when(p == 2)
        def _():
            c_finish()
            s_b_finish(3)
            s_middle(0)
            s_middle(1)

        @pl.when(p == 3)
        def _():
            s_b_finish(4)
            s_middle(2)

        return 0

    lax.fori_loop(0, pairs, key_pair, 0)

    def input_block(b, gl1):
        dn1 = dot_rt(wfull[0, b, :WR], wqkv[:, :width])
        for j in range(1, 3):
            dn1 = dn1 + dot_rt(wfull[j, b, :WR], wqkv[:, j * width : (j + 1) * width])
        scaled, inverse = normalized(tok[wide(b)].astype(F32))
        igrad[wide(b)] += norm_back(dn1, g1[...], scaled, inverse)
        store_grad(b)

        @pl.when(b == 0)
        def _():
            k_a_finish(7)
            s_middle(3)

        @pl.when(b == 1)
        def _():
            s_b_finish(5)
            s_middle(4)

        return gl1 + jnp.sum(dn1 * scaled, 0, keepdims=True)

    vec[0:1] = lax.fori_loop(0, nw, input_block, zero_row)
    va_copy = remote(vec, va, va_s, va_r, core_dev)
    va_copy.start()
    k_b_finish(6)
    va_copy.wait_recv()
    vb[0] = vec[...] + va[...]
    vb_copies = [remote(vb.at[0], vb.at[k], vb_s, vb_r, peer_dev(k)) for k in range(1, npeer)]
    for copy in vb_copies:
        copy.start()
    k_b_finish(7)
    s_c_finish(0)
    s_c_finish(1)
    s_c_finish(2)
    s_middle(5)
    s_c_finish(3)
    s_c_finish(4)
    arrived(vb.at[pl.ds(1, npeer - 1)], vb_r)
    total = vb[peers[0]]
    for j in range(1, npeer):
        total = total + vb[peers[j]]
    vc[0] = total
    vc_copies = [remote(vc.at[0], vc.at[k], vc_s, vc_r, z_dev(k)) for k in range(1, tn)]
    for copy in vc_copies:
        copy.start()
    k_c_finish(6)
    k_c_finish(7)
    s_c_finish(5)
    d_finish()
    for i in range(4):
        k_d_finish(i)
    arrived(vc.at[pl.ds(1, tn - 1)], vc_r)
    total = vc[zs[0]]
    for j in range(1, tn):
        total = total + vc[zs[j]]
    own = vc[0, 4:5]
    for k in range(1, tn):
        own = own + vc[k, 4 + k : 5 + k]
    vec_out[...] = total
    vec_out[4:5] = own
    k_d_finish(4)
    k_d_finish(6)
    k_d_finish(7)
    k_d_finish(5)
    e_finish()
    store_fin().start()
    for i in (0, 1, 2, 3, 4, 6, 7, 5):
        k_e_finish(i)
        store_fink(i).start()
    sent(vec, va_s)
    sent(vb.at[pl.ds(1, npeer - 1)], vb_s)
    sent(vc.at[pl.ds(1, tn - 1)], vc_s)
    sent(gbuf.at[:, 0], a_s)
    sent(rb, b_s)
    sent(rc, c_s)
    sent(fin.at[0, pl.ds(0, (npeer - 1) * rp)], d_s)
    sent(fin.at[0], e_s)
    sent(kbuf.at[:, 0], ka_s)
    sent(krb, kb_s)
    sent(krc.at[pl.ds(0, 2), pl.ds(1, tn - 1)], kc_s.at[0])
    sent(krc.at[pl.ds(0, 6), pl.ds(0, levels)], kc_s.at[1])
    sent(fink.at[:, 0, pl.ds(0, (npeer - 1) * rp)], kd_s)
    sent(fink.at[:, 0], ke_s)

    @pl.when(t < tn - 1)
    def _():
        sent(chf_out, chf_s)

    @pl.when(t > 0)
    def _():
        sent(chb_out, chb_s)

    pltpu.make_async_copy(layer_h, layer_h, out_s.at[0]).wait()
    pltpu.make_async_copy(igrad, igrad_h, out_s.at[1]).wait()
    store_fin().wait()
    pltpu.make_async_copy(fink, fink_h, out_s.at[3]).wait()


def finish_kernel(
    layer_in, igrad_in, fin_h, fink_h, vec, layer_out, igrad, gwq_h, gwo_h, gwi_h, gwd_h, gl1, gbo, gl2, gbi, gbd,
    layer_v, igrad_v, fin, fink, gwq, gwo, gwi, gwd, in_s, out_s,
):
    used = [0, 0]

    def move(src, dst, out, parts):
        sems, copies = (in_s, out_s)[out], []
        size = src.shape[0] // parts
        for k in range(parts):
            at = pl.ds(k * size, size)
            copies.append(pltpu.make_async_copy(src.at[at], dst.at[at], sems.at[used[out]]))
            used[out] += 1
            copies[-1].start()
        return copies

    def wait(copies):
        for copy in copies:
            copy.wait()

    pairs = fink.shape[0] // 2
    width, pw = fink.shape[2:]
    a, b, c, d = (
        move(src, dst, 0, parts)
        for src, dst, parts in ((fink_h, fink, 8), (fin_h, fin, 2), (layer_in, layer_v, 4), (igrad_in, igrad_v, 4))
    )
    for row, out in enumerate((gl1, gbo, gl2, gbd, gbi)):
        out[...] = vec[row : row + 1]
    wait(a)
    stores = []
    quarter = width // 4
    for k in range(4):
        rows = pl.ds(k * quarter, quarter)
        for p in range(pairs):
            at = slice(p * pw, (p + 1) * pw)
            gwq[rows, at] = fink[2 + p // 2, p % 2, rows].astype(F32)
            gwq[rows, width + p * pw : width + (p + 1) * pw] = fink[4 + p, 0, rows].astype(F32)
            gwq[rows, 2 * width + p * pw : 2 * width + (p + 1) * pw] = fink[4 + p, 1, rows].astype(F32)
            gwo[rows, at] = fink[p // 2, p % 2, rows].astype(F32)
        stores += move(gwq.at[rows], gwq_h.at[rows], 1, 1)
        stores += move(gwo.at[rows], gwo_h.at[rows], 1, 1)
    wait(b)
    gwi[...] = fin[0].astype(F32)
    stores += move(gwi, gwi_h, 1, 2)
    wait(c)
    stores += move(layer_v, layer_out, 1, 2)
    wait(d)
    stores += move(igrad_v, igrad, 1, 4)
    gwd[...] = fin[1].astype(F32).T
    stores += move(gwd, gwd_h, 1, 2)
    wait(stores)


def local(
    tn,
    dpn,
    tokens,
    cotangent,
    seq_lengths,
    features,
    ln1_gain,
    w_qkv,
    w_out,
    b_out,
    ln2_gain,
    w_in,
    b_in,
    w_down,
    b_down,
):
    rows_n, width = tokens.shape
    heads, hw, feat_n = features.shape
    pairs, pw, nb = heads // 2, 2 * hw, rows_n // BR
    ffl = w_in.shape[1]
    npeer = dpn // 2
    rp = width // npeer
    vrows = -(-(4 + tn) // 8) * 8
    dma = pltpu.SemaphoreType.DMA
    vmem = pl.BlockSpec(memory_space=pltpu.VMEM)
    anywhere = pl.BlockSpec(memory_space=pl.ANY)

    def scratch(shape, dtype=BF16):
        return pltpu.VMEM(shape, dtype)

    out = pl.pallas_call(
        functools.partial(layer_kernel, tn, dpn),
        out_shape=(
            jax.ShapeDtypeStruct((rows_n, width), BF16),
            jax.ShapeDtypeStruct((rows_n, width), F32),
            jax.ShapeDtypeStruct((2, width, width), BF16),
            jax.ShapeDtypeStruct((8, 2, width, pw), BF16),
            jax.ShapeDtypeStruct((vrows, width), F32),
        ),
        in_specs=[pl.BlockSpec(memory_space=pltpu.SMEM)]
        + [anywhere] * 12,
        out_specs=(anywhere,) * 4 + (vmem,),
        scratch_shapes=[
            scratch((2, width, width)),
            scratch((8, 2, width, pw)),
            scratch((1, width), F32),
            scratch((1, width), F32),
            scratch((width,)),
            scratch((ffl,)),
            scratch((width,)),
            scratch((rows_n, width)),
            scratch((rows_n, width)),
            scratch((heads, hw, feat_n)),
            scratch((width, 3 * width)),
            scratch((width, width)),
            scratch((rows_n, width), F32),
            scratch((tn, 2, width, ffl)),
            scratch((tn, 8, ffl), F32),
            scratch((rows_n, width)),
            scratch((pairs, rows_n, pw)),
            scratch((pairs, rows_n, pw)),
            scratch((pairs, rows_n, pw)),
            scratch((pairs, rows_n, 2 * feat_n)),
            scratch((pairs, rows_n, 2 * feat_n)),
            scratch((pairs, 2 * pw, 2 * feat_n)),
            scratch((2 * pw, 2 * pw)),
            scratch((2 * pw, pw)),
            scratch((nb, BR, BR)),
            scratch((nb, BR, BR)),
            scratch((nb + 1, pairs, pw + 16, feat_n), F32),
            scratch((nb, pairs, pw + 16, feat_n)),
            scratch((rows_n, width), F32),
            scratch((rows_n, width)),
            scratch((rows_n, width), F32),
            scratch((rows_n, width), F32),
            scratch((rows_n, 1), F32),
            scratch((rows_n, width)),
            scratch((2, rows_n, width)),
            scratch((pairs, pw + 16, feat_n)),
            scratch((pairs, pw + 16, feat_n)),
            scratch((pairs, pw + 16, feat_n)),
            scratch((pairs, pw + 16, feat_n)),
            scratch((tn, 2, width, width)),
            scratch((2, width, width)),
            scratch((4, npeer - 1, rp, width)),
            scratch((tn - 1, rp, width)),
            scratch((8, 2, width, pw)),
            scratch((4, width, pw)),
            scratch((8, npeer - 1, rp, pw)),
            scratch((8, max(tn, 2 * (tn - 1).bit_length()), rp, pw)),
            scratch((vrows, width), F32),
            scratch((vrows, width), F32),
            scratch((npeer, vrows, width), F32),
            scratch((tn, vrows, width), F32),
            dma((12,)),
            dma((4,)),
            dma(()),
            dma(()),
            dma(()),
            dma((tn - 1,)),
            dma(()),
            dma((tn - 1,)),
            dma(()),
            dma((tn - 1,)),
            dma(()),
            dma((pairs,)),
            dma(()),
            dma((pairs,)),
            dma(()),
            dma((2,)),
            dma(()),
            dma((tn,)),
            dma(()),
            dma((tn - 1,)),
            dma(()),
            dma(()),
            dma(()),
            dma(()),
            dma(()),
            dma((4,)),
            dma(()),
            dma((8,)),
            dma((2,)),
            dma((8, (tn - 1).bit_length())),
            dma(()),
            dma((8,)),
            dma(()),
            dma((8,)),
            dma(()),
            dma(()),
            dma(()),
            dma(()),
            dma(()),
            dma(()),
        ],
        compiler_params=pltpu.CompilerParams(
            collective_id=0, has_side_effects=True, vmem_limit_bytes=63 * 1024 * 1024
        ),
    )(
        seq_lengths,
        tokens,
        cotangent,
        features,
        ln1_gain[None],
        w_qkv,
        w_out,
        b_out,
        ln2_gain[None],
        w_in,
        b_in,
        w_down,
        b_down,
    )
    row = jax.ShapeDtypeStruct((1, width), F32)

    def square(n):
        return jax.ShapeDtypeStruct((width, n * width), F32)

    done = pl.pallas_call(
        finish_kernel,
        out_shape=(out[0], out[1], square(3), square(1), square(1), square(1)) + (row,) * 5,
        in_specs=[anywhere] * 4 + [vmem],
        out_specs=(anywhere,) * 6 + (vmem,) * 5,
        scratch_shapes=[
            scratch((rows_n, width)),
            scratch((rows_n, width), F32),
            scratch((2, width, width)),
            scratch((8, 2, width, pw)),
            scratch((width, 3 * width), F32),
            scratch((width, width), F32),
            scratch((width, width), F32),
            scratch((width, width), F32),
            dma((18,)),
            dma((18,)),
        ],
        compiler_params=pltpu.CompilerParams(vmem_limit_bytes=63 * 1024 * 1024),
    )(*out)
    layer_out, input_grad, gwq, gwo, gwi, gwd, gl1, gbo, gl2, gbi, gbd = done
    return (
        layer_out,
        input_grad,
        gl1[0],
        gwq,
        gwo,
        gbo[0],
        gl2[0],
        gwi,
        gbi[0],
        gwd,
        gbd[0],
    )


def solution(mesh):
    tn, dpn = mesh.shape["tensor"], mesh.shape["dp"]
    rows = P(("dp", "tensor"), None)
    return jax.shard_map(
        functools.partial(local, tn, dpn),
        mesh=mesh,
        in_specs=(
            rows,
            rows,
            P("dp", None),
            P(),
            P(),
            P(),
            P(),
            P(),
            P(),
            P(None, "tensor"),
            P("tensor"),
            P("tensor", None),
            P(),
        ),
        out_specs=(
            rows,
            rows,
            P(),
            P(),
            P(),
            P(),
            P(),
            P(None, "tensor"),
            P("tensor"),
            P("tensor", None),
            P(),
        ),
        check_vma=False,
    )
```

```python
import functools

import jax
import jax.numpy as jnp
from jax import lax
from jax.experimental import pallas as pl
from jax.experimental.pallas import tpu as pltpu
from jax.sharding import PartitionSpec as P

MESH = pl.DeviceIdType.MESH
F32 = jnp.float32
BF16 = jnp.bfloat16
EPSILON = 1e-05
BR = 256
WR = 512
SQRT_2_OVER_PI = 0.7978845608028654
CUBIC = 0.044715


def dot(a, b):
    return jnp.dot(a, b, preferred_element_type=F32)


def dot_rt(a, b):
    return lax.dot_general(a, b, (((1,), (1,)), ((), ())), preferred_element_type=F32)


def dot_lt(a, b):
    return lax.dot_general(a, b, (((0,), (0,)), ((), ())), preferred_element_type=F32)


def xor(a, b, size):
    out, bit = 0, 1
    while bit < size:
        out = out + bit * lax.rem(lax.div(a, bit) + (b // bit if isinstance(b, int) else lax.div(b, bit)), 2)
        bit *= 2
    return out


def iota(shape, axis):
    return lax.broadcasted_iota(jnp.int32, shape, axis)


def layer_kernel(
    tn,
    dpn,
    lens,
    tok_h,
    cot_h,
    feats_h,
    g1_h,
    wqkv_h,
    wout_h,
    bout_h,
    g2_h,
    win_h,
    bin_h,
    wdn_h,
    bdn_h,
    layer_h,
    igrad_h,
    fin_h,
    fink_h,
    vec_h,
    vec_out,
    fin,
    fink,
    g1,
    g2,
    bout,
    bin_,
    bdn,
    tok,
    cot,
    feats,
    wqkv,
    wout,
    igrad,
    wfull,
    bfull,
    n1s,
    qs,
    ks,
    vs,
    phq,
    phk,
    featx,
    norms,
    bsw,
    mask,
    maskt,
    lst,
    sb,
    rsw_s,
    attn,
    facc,
    xh2,
    rstd2,
    n2s,
    ad,
    chf_in,
    chf_out,
    chb_in,
    chb_out,
    gbuf,
    ra,
    rb,
    rc,
    kbuf,
    kra,
    krb,
    krc,
    vec,
    va,
    vb,
    vc,
    in_s,
    out_s,
    bz_s,
    bz_r,
    wz_s,
    wz_r,
    wx_s,
    wx_r,
    wc_s,
    wc_r,
    chf_s,
    chf_r,
    chb_s,
    chb_r,
    a_s,
    a_r,
    b_s,
    b_r,
    c_s,
    c_r,
    d_s,
    d_r,
    e_s,
    e_r,
    ka_s,
    ka_r,
    kb_s,
    kb_r,
    kc_s,
    kc_r,
    kd_s,
    kd_r,
    ke_s,
    ke_r,
    va_s,
    va_r,
    vb_s,
    vb_r,
    vc_s,
    vc_r,
):
    rows_n, width = tok.shape
    heads, hw, feat_n = feats.shape
    pairs = heads // 2
    pw = 2 * hw
    nb = rows_n // BR
    seqs = lens.shape[1]
    shrink = hw ** (-0.25)
    featscale = feat_n ** (-0.5)
    npeer = dpn // 2
    rp = width // npeer

    dp = lax.axis_index("dp")
    t = lax.axis_index("tensor")
    cb = lax.rem(dp, 2)
    q = lax.div(dp, 2)
    core_dev = (dp + 1 - 2 * cb, t)

    peers = [xor(q, k, npeer) for k in range(npeer)]
    zs = [xor(t, k, tn) for k in range(tn)]

    def peer_dev(k):
        return (2 * peers[k] + cb, t)

    def z_dev(k):
        return (dp, zs[k])

    row_starts = [pl.multiple_of(peer * rp, rp) for peer in peers]

    def own_rows():
        return pl.ds(row_starts[0], rp)

    def peer_rows(k):
        return pl.ds(row_starts[k], rp)

    def load(i, src, dst):
        return pltpu.make_async_copy(src, dst, in_s.at[i])

    pairs_in = {
        "feats": (feats_h, feats),
        "g1": (g1_h, g1),
        "g2": (g2_h, g2),
        "bout": (bout_h, bout),
        "bin": (bin_h, bin_),
        "bdn": (bdn_h, bdn),
        "win": (win_h, wfull.at[0, 0]),
        "wdn": (wdn_h, wfull.at[0, 1]),
        "tok": (tok_h, tok),
        "wqkv": (wqkv_h, wqkv),
        "wout": (wout_h, wout),
        "cot": (cot_h, cot),
    }
    loads = {name: load(i, *pair) for i, (name, pair) in enumerate(pairs_in.items())}
    for copy in loads.values():
        copy.start()

    def store_layer():
        half = layer_h.shape[0] // 2
        for h in range(2):
            pltpu.make_async_copy(wfull.at[tn - 1, h], layer_h.at[pl.ds(h * half, half)], out_s.at[0]).start()

    def store_grad(b):
        rows = pl.ds(pl.multiple_of(b * WR, WR), WR)
        pltpu.make_async_copy(igrad.at[rows], igrad_h.at[rows], out_s.at[1]).start()

    def store_fin():
        return pltpu.make_async_copy(fin, fin_h, out_s.at[2])

    def store_fink(i):
        return pltpu.make_async_copy(fink.at[i], fink_h.at[i], out_s.at[3])

    bar = pltpu.get_barrier_semaphore()
    targets = [core_dev] + [peer_dev(k) for k in range(1, npeer)] + [z_dev(k) for k in range(1, tn)]
    for dev in targets:
        pl.semaphore_signal(bar, inc=1, device_id=dev, device_id_type=MESH)

    def remote(src, dst, ss, rs, dev):
        return pltpu.make_async_remote_copy(
            src_ref=src, dst_ref=dst, send_sem=ss, recv_sem=rs, device_id=dev, device_id_type=MESH
        )

    def arrived(ref, sem):
        remote(ref, ref, a_s, sem, core_dev).wait_recv()

    def sent(ref, sem):
        remote(ref, ref, sem, a_r.at[0], core_dev).wait_send()

    def bz_copy(k):
        return remote(bfull.at[0], bfull.at[k], bz_s, bz_r, z_dev(k))

    def wz_copy(k):
        source, via = (0, k) if k == 1 or k % 2 == 0 else (k - 1, 1)
        return remote(
            wfull.at[source, cb, own_rows()], wfull.at[k, cb, own_rows()], wz_s, wz_r.at[k - 1], z_dev(via)
        )

    def wx_copy(k, j):
        here = wfull.at[k, cb, own_rows()]
        return remote(here, here, wx_s, wx_r.at[k - 1], peer_dev(j))

    def wc_copy(k):
        return remote(wfull.at[k, cb], wfull.at[k, cb], wc_s, wc_r.at[k - 1], core_dev)

    def wc_recv(k):
        here = wfull.at[k, 1 - cb]
        return remote(here, here, wc_s, wc_r.at[k - 1], core_dev)

    def w_spread(k):
        wz_copy(k).wait_recv()
        if k > 1 and k % 2 == 0:
            wz_copy(k + 1).start()
        for j in range(1, npeer):
            wx_copy(k, j).start()

    def w_swap(k):
        arrived(wfull.at[k, cb, pl.ds(0, (npeer - 1) * rp)], wx_r.at[k - 1])
        wc_copy(k).start()

    levels = (tn - 1).bit_length()
    up_first = (1, 3, 5, 7), (8, 9, 10, 12)

    def up_due(at, p):
        return up_first[at - 1][p % 4] if at < 3 and p < 4 else 10 + p

    def down_due(hops, p):
        due = min(3 * hops + p, 8 + 2 * p)
        return due + due % 2 if due > 8 else due

    def up_copy(p):
        return remote(chf_out.at[p], chf_in.at[p], chf_s, chf_r.at[p], (dp, lax.rem(t + 1, tn)))

    def up_handle(p):
        @pl.when(t > 0)
        def _():
            up_copy(p).wait_recv()

        chf_out[p] = (lst[nb, p] + passing * chf_in[p].astype(F32)).astype(BF16)
        up_copy(p).start()

    def up_slots(k, low, high):
        for at in range(1, tn - 1):
            for p in range(pairs):
                if low <= up_due(at, p) < high:

                    @pl.when((t == at) & (k == up_due(at, p)))
                    def _(p=p):
                        up_handle(p)

    def down_copy(p):
        return remote(chb_out.at[p], chb_in.at[p], chb_s, chb_r.at[p], (dp, lax.rem(t + tn - 1, tn)))

    def down_handle(p):
        @pl.when(t < tn - 1)
        def _():
            down_copy(p).wait_recv()

        own = lst[nb - 1, p]
        for b in range(nb - 2, -1, -1):
            own = keep_of(b) * own + lst[b, p]
        chb_out[p] = (own + passing * chb_in[p].astype(F32)).astype(BF16)
        down_copy(p).start()

    def down_slots(k, low, high):
        for hops in range(tn - 1):
            for p in range(pairs):
                if low <= down_due(hops, p) < high:

                    @pl.when((t == tn - 1 - hops) & (k == down_due(hops, p)))
                    def _(p=p):
                        down_handle(p)

    def place_of(turn):
        return jnp.where(turn < tn // 2, 2 * turn + 1, 2 * (tn - 1 - turn))

    def a_copy(turn):
        turn = jnp.int32(turn)
        return remote(
            gbuf.at[place_of(turn), 1 - cb], ra.at[lax.rem(turn, 2)], a_s, a_r.at[lax.rem(turn, 2)], core_dev
        )

    def b_copy(s, k):
        s = jnp.int32(s)
        return remote(gbuf.at[s, cb, peer_rows(k)], rb.at[lax.rem(s, 4), k - 1], b_s, b_r.at[s], peer_dev(k))

    def c_copy(s):
        return remote(gbuf.at[s, cb, own_rows()], rc.at[s - 1], c_s, c_r.at[s - 1], z_dev(s & -s))

    def d_copy(k):
        here = fin.at[cb, own_rows()]
        return remote(here, here, d_s, d_r, peer_dev(k))

    def e_copy():
        return remote(fin.at[cb], fin.at[cb], e_s, e_r, core_dev)

    def e_recv():
        return remote(fin.at[1 - cb], fin.at[1 - cb], e_s, e_r, core_dev)

    def ka_copy(i):
        i = jnp.int32(i)
        return remote(kbuf.at[i, 1 - cb], kra.at[lax.rem(i, 4)], ka_s, ka_r.at[lax.rem(i, 4)], core_dev)

    def kb_copy(i, k):
        return remote(
            kbuf.at[i, cb, peer_rows(k)], krb.at[i, k - 1], kb_s, kb_r.at[i], peer_dev(k)
        )

    def kc_copy(i, k):
        return remote(krc.at[i, 0], krc.at[i, k], kc_s.at[0], kc_r.at[i, 0], z_dev(k))

    def ks_copy(i, l):
        return remote(
            krc.at[i, 2 * l], krc.at[i, 2 * l + 1], kc_s.at[1], kc_r.at[i, l], z_dev(1 << l)
        )

    def kd_copy(i, k):
        here = fink.at[i, cb, own_rows()]
        return remote(here, here, kd_s, kd_r.at[i], peer_dev(k))

    def ke_copy(i):
        return remote(fink.at[i, cb], fink.at[i, cb], ke_s, ke_r.at[i], core_dev)

    def ke_recv(i):
        return remote(fink.at[i, 1 - cb], fink.at[i, 1 - cb], ke_s, ke_r.at[i], core_dev)

    def a_start(turn):
        a_copy(turn).start()

    def a_finish(turn):
        turn = jnp.int32(turn)
        a_copy(turn).wait_recv()
        s = place_of(turn)
        gbuf[s, cb] = (gbuf[s, cb].astype(F32) + ra[lax.rem(turn, 2)].astype(F32)).astype(BF16)
        for k in range(1, npeer):
            b_copy(s, k).start()

    def b_sum(s):
        s = jnp.int32(s)
        arrived(rb.at[lax.rem(s, 4)], b_r.at[s])
        total = gbuf[s, cb, own_rows()].astype(F32)
        for k in range(1, npeer):
            total = total + rb[lax.rem(s, 4), k - 1].astype(F32)
        return total.astype(BF16)

    def b_finish(s):
        gbuf[s, cb, own_rows()] = b_sum(s)

    def c_add(s):
        step = 1
        while step < (s & -s if s else tn):
            c_copy(s + step).wait_recv()
            gbuf[s, cb, own_rows()] = (
                gbuf[s, cb, own_rows()].astype(F32) + rc[s + step - 1].astype(F32)
            ).astype(BF16)
            step *= 2

    def c_start(s):
        c_add(s)
        c_copy(s).start()

    def c_finish():
        total = gbuf[0, cb, own_rows()].astype(F32)
        step = 1
        while step < tn:
            c_copy(step).wait_recv()
            total = total + rc[step - 1].astype(F32)
            step *= 2
        fin[cb, own_rows()] = total.astype(BF16)
        for k in range(1, npeer):
            d_copy(k).start()

    def d_finish():
        arrived(fin.at[0, pl.ds(0, (npeer - 1) * rp)], d_r)
        e_copy().start()

    def e_finish():
        e_recv().wait_recv()

    def k_a_start(i, both):
        kbuf[i, 0] = both[:, :pw].astype(BF16)
        kbuf[i, 1] = both[:, pw:].astype(BF16)
        ka_copy(i).start()

    def k_a_finish(i):
        i = jnp.int32(i)
        ka_copy(i).wait_recv()
        kbuf[i, cb] = (kbuf[i, cb].astype(F32) + kra[lax.rem(i, 4)].astype(F32)).astype(BF16)
        for k in range(1, npeer):
            kb_copy(i, k).start()

    def k_b_sum(i):
        arrived(krb.at[i], kb_r.at[i])
        total = kbuf[i, cb, own_rows()].astype(F32)
        for k in range(1, npeer):
            total = total + krb[i, k - 1].astype(F32)
        krc[i, 0] = total.astype(BF16)

    def k_spread(i, total):
        fink[i, cb, own_rows()] = total.astype(BF16)
        for k in range(1, npeer):
            kd_copy(i, k).start()

    def k_b_finish(i):
        k_b_sum(i)
        for k in range(1, tn):
            kc_copy(i, k).start()

    def k_c_finish(i):
        arrived(krc.at[i, pl.ds(1, tn - 1)], kc_r.at[i, 0])
        total = krc[i, zs[0]].astype(F32)
        for j in range(1, tn):
            total = total + krc[i, zs[j]].astype(F32)
        k_spread(i, total)

    def s_b_finish(i):
        k_b_sum(i)
        ks_copy(i, 0).start()

    def s_sum(i, l):
        ks_copy(i, l).wait_recv()
        return krc[i, 2 * l].astype(F32) + krc[i, 2 * l + 1].astype(F32)

    def s_middle(i):
        for l in range(levels - 1):
            krc[i, 2 * l + 2] = s_sum(i, l).astype(BF16)
            ks_copy(i, l + 1).start()

    def s_c_finish(i):
        k_spread(i, s_sum(i, levels - 1))

    def k_d_finish(i):
        arrived(fink.at[i, 0, pl.ds(0, (npeer - 1) * rp)], kd_r.at[i])
        ke_copy(i).start()

    def k_e_finish(i):
        ke_recv(i).wait_recv()

    offsets = [jnp.int32(0)]
    for c in range(1, seqs):
        offsets.append(offsets[-1] + lens[0, c - 1])
    first = t * rows_n

    def seg_at(r):
        seg = -1
        for off in offsets:
            seg = seg + jnp.where(r >= off, 1, 0)
        return seg

    def seg_array(shape, axis, start):
        places = iota(shape, axis) + start
        seg = jnp.full(shape, -1, jnp.int32)
        for off in offsets:
            seg = seg + jnp.where(places >= off, 1, 0)
        return seg

    before = seg_at(first - 1)
    closing = seg_at(first + rows_n - 1)
    passing = jnp.where(before == closing, 1.0, 0.0)

    def prev_of(b):
        return seg_at(first + b * BR - 1)

    def last_of(b):
        return seg_at(first + b * BR + BR - 1)

    def keep_of(b):
        return jnp.where(prev_of(b) == last_of(b), 1.0, 0.0)

    def ending(b):
        return seg_array((BR, pw), 0, first + b * BR) == last_of(b)

    def reached(b):
        return seg_array((BR, pw), 0, first + b * BR) == prev_of(b)

    def block(b):
        return pl.ds(pl.multiple_of(b * BR, BR), BR)

    nw = rows_n // WR

    def wide(b):
        return pl.ds(pl.multiple_of(b * WR, WR), WR)

    def lanes(p):
        return pl.ds(pl.multiple_of(p * pw, pw), pw)

    def as_row(ref):
        return ref[...].astype(F32).reshape(1, ref.shape[0])

    low_lane = iota((BR, pw), 1) < hw
    low_row = iota((pw, feat_n), 0) < hw
    row_id = iota((pw, feat_n), 0)

    for name in ("feats", "g1", "g2", "bout", "bin", "bdn"):
        loads[name].wait()
    featx[...] = jnp.zeros_like(featx)
    for p in range(pairs):
        for o in range(2):
            featx[p, o * hw : (o + 1) * hw, o * feat_n : (o + 1) * feat_n] = feats[2 * p + o]
            featx[p, pw + o * hw : pw + (o + 1) * hw, o * feat_n : (o + 1) * feat_n] = jnp.full(
                (hw, feat_n), -0.5, BF16
            )
    ri, ci = iota((2 * pw, pw), 0), iota((2 * pw, pw), 1)
    ro, co = iota((2 * pw, 2 * pw), 0), iota((2 * pw, 2 * pw), 1)
    norms[...] = jnp.where((lax.rem(ro, pw) < hw) == (co < pw), -0.5, 0.0).astype(BF16)
    swap = (lax.rem(ri, pw) < hw) != (ci < hw)
    bsw[...] = jnp.where(swap, 1.0, 0.0).astype(BF16)

    def build_mask(b, _):
        seg_i = seg_array((BR, BR), 0, first + b * BR)
        seg_j = seg_array((BR, BR), 1, first + b * BR)
        same = seg_i == seg_j
        i, j = iota((BR, BR), 0), iota((BR, BR), 1)
        mask[b] = jnp.where(same & (i >= j), 1.0, 0.0).astype(BF16)
        maskt[b] = jnp.where(same & (j >= i), 1.0, 0.0).astype(BF16)
        return 0

    lax.fori_loop(0, nb, build_mask, 0)
    lst[0] = jnp.zeros(lst.shape[1:], F32)
    vec[...] = jnp.zeros_like(vec)

    @pl.when(t == 0)
    def _():
        chf_in[...] = jnp.zeros_like(chf_in)

    @pl.when(t == tn - 1)
    def _():
        chb_in[...] = jnp.zeros_like(chb_in)

    loads["win"].wait()
    loads["wdn"].wait()
    pl.semaphore_wait(bar, len(targets))
    bfull[0] = jnp.broadcast_to(as_row(bin_), bfull.shape[1:])
    for k in range(1, tn):
        bz_copy(k).start()
    wz_copy(1).start()
    wz_copy(2).start()

    def features_of(x, p):
        wide = x.astype(F32)
        square = wide * wide
        high = square.astype(BF16)
        rest = (square - high.astype(F32)).astype(BF16)
        norm = dot(jnp.concatenate([high, rest], 1), norms[...])
        repeats = [norm[:, :pw]] * (feat_n // pw) + [norm[:, pw:]] * (feat_n // pw)
        arg = dot(x, featx[p, :pw]) + jnp.concatenate(repeats, 1)
        return (jnp.exp(arg) * featscale).astype(BF16)

    def normalized(x):
        centre = jnp.mean(x, -1, keepdims=True)
        shifted = x - centre
        inverse = lax.rsqrt(jnp.mean(shifted * shifted, -1, keepdims=True) + EPSILON)
        return shifted * inverse, inverse

    def values_of(p, b):
        wide = vs[p, block(b)].astype(F32)
        return jnp.where(low_lane, wide, 1.0), jnp.where(low_lane, 1.0, wide)

    def keys_block(b, _):
        scaled, _inv = normalized(tok[wide(b)].astype(F32))
        normed = (scaled * g1[...]).astype(BF16)
        n1s[wide(b)] = normed
        key = (dot(normed, wqkv[:, width : 2 * width]) * shrink).astype(BF16)
        val = dot(normed, wqkv[:, 2 * width :]).astype(BF16)
        for p in range(pairs):
            ks[p, wide(b)] = key[:, p * pw : (p + 1) * pw]
            vs[p, wide(b)] = val[:, p * pw : (p + 1) * pw]

        return 0

    loads["tok"].wait()
    loads["wqkv"].wait()
    lax.fori_loop(0, nw, keys_block, 0)

    def state_pair(p, _):
        for c in range(nw):
            phk[p, wide(c)] = features_of(ks[p, wide(c)], p)
        for b in range(nb):
            feat = phk[p, block(b)]
            end = ending(b)
            ve, vo = values_of(p, b)
            ue = dot_lt(jnp.where(end, ve, 0.0).astype(BF16), feat[:, :feat_n])
            uo = dot_lt(jnp.where(end, vo, 0.0).astype(BF16), feat[:, feat_n:])
            keep = keep_of(b)
            lst[b + 1, p, :pw] = keep * lst[b, p, :pw] + jnp.where(low_row, ue, uo)
            lst[b + 1, p, pw : pw + 8] = keep * lst[b, p, pw : pw + 8] + ue[hw : hw + 8]
            lst[b + 1, p, pw + 8 :] = keep * lst[b, p, pw + 8 :] + uo[:8]

        @pl.when(t == 0)
        def _():
            up_handle(p)


        @pl.when(p == 3)
        def _():
            w_spread(1)

        return 0

    lax.fori_loop(0, pairs, state_pair, 0)

    def queries_block(b, _):
        up_slots(b, 0, nw)
        query = (dot(n1s[wide(b)], wqkv[:, :width]) * shrink).astype(BF16)
        for p in range(pairs):
            qs[p, wide(b)] = query[:, p * pw : (p + 1) * pw]

        @pl.when(b == nw - 1)
        def _():
            w_spread(2)

        return 0

    lax.fori_loop(0, nw, queries_block, 0)

    def features_pair(p, _):
        up_slots(nw + p, nw, nw + pairs)
        for b in range(nw):
            phq[p, wide(b)] = features_of(qs[p, wide(b)], p)
        return 0

    lax.fori_loop(0, pairs, features_pair, 0)

    def state_halves(state):
        top = state[:pw]
        even = jnp.where(low_row, top, jnp.broadcast_to(state[pw : pw + 1], top.shape)).astype(BF16)
        odd = jnp.where(low_row, jnp.broadcast_to(state[pw + 8 : pw + 9], top.shape), top).astype(BF16)
        return even, odd

    slot = nw + pairs

    def inside_pair(p, _):
        up_slots(slot + p, slot, slot + pairs)

        @pl.when(p == 3)
        def _():
            w_spread(3)

        for b in range(nb):
            for o, (val, part) in enumerate(zip(values_of(p, b), (facc, xh2))):
                fq = phq[p, block(b), o * feat_n : (o + 1) * feat_n]
                fk = phk[p, block(b), o * feat_n : (o + 1) * feat_n]
                scores = jnp.where(mask[b].astype(F32) > 0, dot_rt(fq, fk), 0.0).astype(BF16)
                part[block(b), lanes(p)] = dot(scores, val.astype(BF16))
        return 0

    lax.fori_loop(0, pairs, inside_pair, 0)

    def attend_pair(p, _):
        up_slots(slot + pairs + p, slot + pairs, slot + 2 * pairs)

        @pl.when(p == 2)
        def _():
            w_swap(1)

        @pl.when(t == tn - 1)
        def _():
            up_copy(p).wait_recv()

        incoming = chf_in[p].astype(F32)
        for b in range(nb):
            first_pass = jnp.where(before == prev_of(b), 1.0, 0.0)
            state = (lst[b, p] + first_pass * incoming).astype(BF16)
            sb[b, p] = state
            reach = reached(b)
            outs = []
            for o, (st, part) in enumerate(zip(state_halves(state.astype(F32)), (facc, xh2))):
                fq = phq[p, block(b), o * feat_n : (o + 1) * feat_n]
                outs.append(part[block(b), lanes(p)] + jnp.where(reach, dot_rt(fq, st), 0.0))
            inverse = 1.0 / jnp.where(low_lane, outs[1], outs[0])
            rsw_s[block(b), lanes(p)] = inverse
            num = jnp.where(low_lane, outs[0], outs[1])
            attn[block(b), lanes(p)] = (num * pltpu.roll(inverse, hw, 1)).astype(BF16)
        return 0

    lax.fori_loop(0, pairs, attend_pair, 0)

    def hidden_block(b, _):
        h1 = tok[wide(b)].astype(F32) + (dot(attn[wide(b)], wout[...]) + as_row(bout))
        scaled, inverse = normalized(h1)
        xh2[wide(b)] = scaled
        rstd2[wide(b)] = inverse
        n2s[wide(b)] = (scaled * g2[...]).astype(BF16)
        facc[wide(b)] = h1 + as_row(bdn)
        return 0

    loads["wout"].wait()
    lax.fori_loop(0, nw, hidden_block, 0)
    loads["cot"].wait()

    def feed_chunk(turn, _):
        s = place_of(turn)

        @pl.when(s > 0)
        def _():
            for k in range(1, tn):

                @pl.when(s == k)
                def _(k=k):
                    wc_recv(k).wait_recv()

        def rows_block(b, total):
            w_in = wfull[s, 0]
            w_dn = wfull[s, 1]
            u = dot(n2s[wide(b)], w_in) + bfull[s, 0:1]
            u2 = u * u
            th = jnp.tanh(u * (SQRT_2_OVER_PI + SQRT_2_OVER_PI * CUBIC * u2))
            half = 0.5 + 0.5 * th
            act = (u * half).astype(BF16)
            slope = half + (0.5 * u) * (1.0 - th * th) * (
                SQRT_2_OVER_PI + 3.0 * SQRT_2_OVER_PI * CUBIC * u2
            )
            ad[0, wide(b)] = act
            facc[wide(b)] += dot(act, w_dn)
            du = (slope * dot_rt(cot[wide(b)], w_dn)).astype(BF16)
            ad[1, wide(b)] = du
            back = dot_rt(du, w_in)

            @pl.when(turn == 0)
            def _():
                igrad[wide(b)] = back

            @pl.when(turn > 0)
            def _():
                igrad[wide(b)] += back

            @pl.when((turn >= 1) & (b == 0))
            def _():
                a_finish(jnp.maximum(turn - 1, 0))

            @pl.when((turn == 0) & (b == 0))
            def _():
                w_swap(2)

            @pl.when((turn == 0) & (b == nw - 1))
            def _():
                w_swap(3)

            return total + jnp.sum(du.astype(F32), 0, keepdims=True)

        total = lax.fori_loop(0, nw, rows_block, jnp.zeros((1, wfull.shape[3]), F32))
        vec[pl.ds(4 + s, 1)] = total

        @pl.when(turn == tn - 1)
        def _():
            b_finish(1)
            c_start(1)

        gbuf[s, 0] = dot_lt(n2s[...], ad[1]).astype(BF16)
        gbuf[s, 1] = dot_lt(cot[...], ad[0]).astype(BF16)
        a_start(turn)
        return 0

    arrived(bfull.at[pl.ds(1, tn - 1)], bz_r)
    lax.fori_loop(0, tn, feed_chunk, 0)
    sent(bfull.at[pl.ds(1, tn - 1)], bz_s)
    sent(wfull.at[pl.ds(0, tn - 1), 0, pl.ds(0, rp)], wz_s)
    sent(wfull.at[pl.ds(0, tn - 1), 0, pl.ds(0, (npeer - 1) * rp)], wx_s)
    sent(wfull.at[pl.ds(0, tn - 1), 0], wc_s)

    def norm_back(dn, gain, scaled, inverse):
        g = dn * gain
        inner = jnp.mean(g, -1, keepdims=True)
        cross = jnp.mean(g * scaled, -1, keepdims=True)
        return inverse * (g - inner - scaled * cross)


    def branch_block(b, carry):
        gl2, gbo, gbd = carry
        wfull[tn - 1, b] = facc[wide(b)].astype(BF16)
        dy = cot[wide(b)].astype(F32)
        dn2 = igrad[wide(b)]
        scaled = xh2[wide(b)]
        dh1 = dy + norm_back(dn2, g2[...], scaled, rstd2[wide(b)])
        igrad[wide(b)] = dh1
        dob = dh1.astype(BF16)
        n2s[wide(b)] = dob
        dattn = dot_rt(dob, wout[...])
        lane_id = iota((WR, pw), 1)
        low_half = lane_id < hw
        for p in range(pairs):
            da = dattn[:, p * pw : (p + 1) * pw]
            inverse = rsw_s[wide(b), p * pw : (p + 1) * pw]
            dnum = da * pltpu.roll(inverse, hw, 1)
            prod = da * attn[wide(b), p * pw : (p + 1) * pw].astype(F32)
            high = prod.astype(BF16)
            rest = (prod - high.astype(F32)).astype(BF16)
            dden = -dot(jnp.concatenate([high, rest], 1), bsw[...]) * inverse
            dhi = dden.astype(BF16).astype(F32)
            dlo = dden - dhi
            even = jnp.where(lane_id == hw, dhi, jnp.where(lane_id == hw + 1, dlo, 0.0))
            odd = jnp.where(lane_id == 0, dhi, jnp.where(lane_id == 1, dlo, 0.0))
            ad[0, wide(b), p * pw : (p + 1) * pw] = jnp.where(low_half, dnum, even).astype(BF16)
            ad[1, wide(b), p * pw : (p + 1) * pw] = jnp.where(low_half, odd, dnum).astype(BF16)
        for c in range(nb // nw):
            at = b * (nb // nw) + c
            reach = reached(at)
            for p in range(pairs):
                ge, go = (
                    dot_lt(
                        jnp.where(reach, ad[o, block(at), p * pw : (p + 1) * pw].astype(F32), 0.0).astype(BF16),
                        phq[p, block(at), o * feat_n : (o + 1) * feat_n],
                    )
                    for o in range(2)
                )
                lst[at, p, :pw] = jnp.where(low_row, ge, go)
                lst[at, p, pw : pw + 8] = jnp.broadcast_to(ge[hw : hw + 1] + ge[hw + 1 : hw + 2], (8, feat_n))
                lst[at, p, pw + 8 :] = jnp.broadcast_to(go[0:1] + go[1:2], (8, feat_n))

        @pl.when(b == 0)
        def _():
            a_finish(tn - 1)
            b_finish(3)
            c_start(3)

        return (
            gl2 + jnp.sum(dn2 * scaled, 0, keepdims=True),
            gbo + jnp.sum(dob.astype(F32), 0, keepdims=True),
            gbd + jnp.sum(dy, 0, keepdims=True),
        )

    zero_row = jnp.zeros((1, width), F32)
    gl2, gbo, gbd = lax.fori_loop(0, nw, branch_block, (zero_row,) * 3)
    store_layer()
    vec[1:2] = gbo
    vec[2:3] = gl2
    vec[3:4] = gbd
    half_blocks = nb // 2

    def grad_at(j, b):
        if isinstance(b, int):
            return j, b // half_blocks, pl.ds((b % half_blocks) * BR, BR)
        rows = pl.ds(pl.multiple_of(lax.rem(b, half_blocks) * BR, BR), BR)
        return j, lax.div(b, half_blocks), rows

    half = rows_n // 2

    def weight_grad(ja, pa, jb, pb):
        total = 0.0
        for h in range(2):
            both = [wfull[j, h, :half, lanes(p)] for j, p in ((ja, pa), (jb, pb))]
            total = total + dot_lt(n1s[h * half : (h + 1) * half], jnp.concatenate(both, 1))
        return total

    def arg_back(darg, x, p):
        both = dot_rt(darg, featx[p])
        return (both[:, :pw] + (2.0 * x.astype(F32)) * both[:, pw:]) * shrink

    out_grad = dot_lt(attn[...], n2s[...])
    for i in range(2):
        k_a_start(i, out_grad[:, i * 2 * pw : (i + 1) * 2 * pw])

    def query_half(i, _):
        down_slots(i, 0, 2 * pairs)
        p, half = lax.div(i, 2), lax.rem(i, 2)
        for c in range(nb // 2):
            b = half * (nb // 2) + c
            se, so = state_halves(sb[b, p].astype(F32))
            reach = reached(b)
            ve, vo = values_of(p, b)
            dargs = []
            for o, (val, st) in enumerate(((ve, se), (vo, so))):
                dn = ad[o, block(b), lanes(p)]
                cdn = jnp.where(reach, dn.astype(F32), 0.0).astype(BF16)
                fq = phq[p, block(b), o * feat_n : (o + 1) * feat_n]
                fk = phk[p, block(b), o * feat_n : (o + 1) * feat_n]
                da = jnp.where(mask[b].astype(F32) > 0, dot_rt(dn, val.astype(BF16)), 0.0).astype(BF16)
                dfq = dot(da, fk) + dot(cdn, st)
                dargs.append((dfq * fq.astype(F32)).astype(BF16))
            wfull[grad_at(0, b) + (lanes(p),)] = arg_back(
                jnp.concatenate(dargs, 1), qs[p, block(b)], p
            ).astype(BF16)

        @pl.when(i == 1)
        def _():
            k_a_finish(0)
            k_a_finish(1)
            b_finish(2)

        @pl.when(i == 3)
        def _():
            k_a_start(2, weight_grad(0, 0, 0, 1))

        @pl.when(i == 5)
        def _():
            k_a_finish(2)
            b_finish(0)

        @pl.when(i == 7)
        def _():
            k_a_start(3, weight_grad(0, 2, 0, 3))
            c_start(2)

        return 0

    lax.fori_loop(0, 2 * pairs, query_half, 0)

    def key_pair(p, _):
        down_slots(2 * (pairs + p), 2 * pairs, 4 * pairs)

        @pl.when(t == 0)
        def _():
            down_copy(p).wait_recv()

        grad = chb_in[p].astype(F32)
        for b in range(nb - 1, -1, -1):
            top = grad[:pw]
            halves = []
            for o in range(2):
                dz = jnp.broadcast_to(grad[pw + 8 * o : pw + 8 * o + 1], top.shape)
                dz_hi = dz.astype(BF16).astype(F32)
                at = hw * (1 - o)
                filler = jnp.where(row_id == at, dz_hi, jnp.where(row_id == at + 1, dz - dz_hi, 0.0))
                halves.append(
                    (jnp.where(low_row, top, filler) if o == 0 else jnp.where(low_row, filler, top)).astype(BF16)
                )
            end = ending(b)
            ve, vo = values_of(p, b)
            dargs, dvs = [], []
            for o, (val, ds) in enumerate(((ve, halves[0]), (vo, halves[1]))):
                dn = ad[o, block(b), lanes(p)]
                fq = phq[p, block(b), o * feat_n : (o + 1) * feat_n]
                fk = phk[p, block(b), o * feat_n : (o + 1) * feat_n]
                at = jnp.where(maskt[b].astype(F32) > 0, dot_rt(fk, fq), 0.0).astype(BF16)
                dat = jnp.where(maskt[b].astype(F32) > 0, dot_rt(val.astype(BF16), dn), 0.0).astype(BF16)
                ev = jnp.where(end, val, 0.0).astype(BF16)
                dfk = dot(dat, fq) + dot(ev, ds)
                dargs.append((dfk * fk.astype(F32)).astype(BF16))
                dvs.append(dot(at, dn) + jnp.where(end, dot_rt(fk, ds), 0.0))
            wfull[grad_at(1, b) + (lanes(p),)] = arg_back(
                jnp.concatenate(dargs, 1), ks[p, block(b)], p
            ).astype(BF16)
            wfull[grad_at(2, b) + (lanes(p),)] = jnp.where(
                low_lane, dvs[0], dvs[1]
            ).astype(BF16)
            if b > 0:
                grad = keep_of(b) * grad + lst[b, p]

        k_a_start(4 + p, weight_grad(1, p, 2, p))

        @pl.when(p == 0)
        def _():
            k_a_finish(3)
            s_b_finish(0)
            s_b_finish(1)

        @pl.when(p >= 1)
        def _():
            k_a_finish(3 + p)

        @pl.when(p == 1)
        def _():
            s_b_finish(2)

        @pl.when(p == 2)
        def _():
            c_finish()
            s_b_finish(3)
            s_middle(0)
            s_middle(1)

        @pl.when(p == 3)
        def _():
            s_b_finish(4)
            s_middle(2)

        return 0

    lax.fori_loop(0, pairs, key_pair, 0)

    def input_block(b, gl1):
        dn1 = dot_rt(wfull[0, b, :WR], wqkv[:, :width])
        for j in range(1, 3):
            dn1 = dn1 + dot_rt(wfull[j, b, :WR], wqkv[:, j * width : (j + 1) * width])
        scaled, inverse = normalized(tok[wide(b)].astype(F32))
        igrad[wide(b)] += norm_back(dn1, g1[...], scaled, inverse)
        store_grad(b)

        @pl.when(b == 0)
        def _():
            k_a_finish(7)
            s_middle(3)

        @pl.when(b == 1)
        def _():
            s_b_finish(5)
            s_middle(4)

        return gl1 + jnp.sum(dn1 * scaled, 0, keepdims=True)

    vec[0:1] = lax.fori_loop(0, nw, input_block, zero_row)
    va_copy = remote(vec, va, va_s, va_r, core_dev)
    va_copy.start()
    k_b_finish(6)
    va_copy.wait_recv()
    vb[0] = vec[...] + va[...]
    vb_copies = [remote(vb.at[0], vb.at[k], vb_s, vb_r, peer_dev(k)) for k in range(1, npeer)]
    for copy in vb_copies:
        copy.start()
    k_b_finish(7)
    s_c_finish(0)
    s_c_finish(1)
    s_c_finish(2)
    s_middle(5)
    s_c_finish(3)
    s_c_finish(4)
    arrived(vb.at[pl.ds(1, npeer - 1)], vb_r)
    total = vb[peers[0]]
    for j in range(1, npeer):
        total = total + vb[peers[j]]
    vc[0] = total
    vc_copies = [remote(vc.at[0], vc.at[k], vc_s, vc_r, z_dev(k)) for k in range(1, tn)]
    for copy in vc_copies:
        copy.start()
    k_c_finish(6)
    k_c_finish(7)
    s_c_finish(5)
    d_finish()
    for i in range(4):
        k_d_finish(i)
    arrived(vc.at[pl.ds(1, tn - 1)], vc_r)
    total = vc[zs[0]]
    for j in range(1, tn):
        total = total + vc[zs[j]]
    own = vc[0, 4:5]
    for k in range(1, tn):
        own = own + vc[k, 4 + k : 5 + k]
    vec_out[...] = total
    vec_out[4:5] = own
    pltpu.make_async_copy(vec_out, vec_h, out_s.at[4]).start()
    k_d_finish(4)
    k_d_finish(6)
    k_d_finish(7)
    k_d_finish(5)
    e_finish()
    store_fin().start()
    for i in (0, 1, 2, 3, 4, 6, 7, 5):
        k_e_finish(i)
        store_fink(i).start()
    sent(vec, va_s)
    sent(vb.at[pl.ds(1, npeer - 1)], vb_s)
    sent(vc.at[pl.ds(1, tn - 1)], vc_s)
    sent(gbuf.at[:, 0], a_s)
    sent(rb, b_s)
    sent(rc, c_s)
    sent(fin.at[0, pl.ds(0, (npeer - 1) * rp)], d_s)
    sent(fin.at[0], e_s)
    sent(kbuf.at[:, 0], ka_s)
    sent(krb, kb_s)
    sent(krc.at[pl.ds(0, 2), pl.ds(1, tn - 1)], kc_s.at[0])
    sent(krc.at[pl.ds(0, 6), pl.ds(0, levels)], kc_s.at[1])
    sent(fink.at[:, 0, pl.ds(0, (npeer - 1) * rp)], kd_s)
    sent(fink.at[:, 0], ke_s)

    @pl.when(t < tn - 1)
    def _():
        sent(chf_out, chf_s)

    @pl.when(t > 0)
    def _():
        sent(chb_out, chb_s)

    pltpu.make_async_copy(vec_out, vec_h, out_s.at[4]).wait()
    pltpu.make_async_copy(layer_h, layer_h, out_s.at[0]).wait()
    pltpu.make_async_copy(igrad, igrad_h, out_s.at[1]).wait()
    store_fin().wait()
    pltpu.make_async_copy(fink, fink_h, out_s.at[3]).wait()


def finish_kernel(
    layer_in, igrad_in, fin_h, fink_h, vec_h, layer_out, igrad, gwq_h, gwo_h, gwi_h, gwd_h, gl1, gbo, gl2, gbi, gbd,
    layer_v, igrad_v, fin, fink, vec, rows_v, gwq, gwo, gwi, gwd, in_s, out_s,
):
    def move(src, dst, sem):
        copy = pltpu.make_async_copy(src, dst, sem)
        copy.start()
        return copy

    pairs = fink.shape[0] // 2
    width, pw = fink.shape[2:]
    kinds = ((fink_h, fink), (layer_in, layer_v), (igrad_in, igrad_v), (fin_h, fin), (vec_h, vec))
    a, b, c, d, e = (move(src, dst, in_s.at[n]) for n, (src, dst) in enumerate(kinds))
    stores = []
    a.wait()
    for k in range(2):
        rows = pl.ds(k * width // 2, width // 2)
        for p in range(pairs):
            at = slice(p * pw, (p + 1) * pw)
            gwq[rows, at] = fink[2 + p // 2, p % 2, rows].astype(F32)
            gwq[rows, width + p * pw : width + (p + 1) * pw] = fink[4 + p, 0, rows].astype(F32)
            gwq[rows, 2 * width + p * pw : 2 * width + (p + 1) * pw] = fink[4 + p, 1, rows].astype(F32)
        stores.append(move(gwq.at[rows], gwq_h.at[rows], out_s.at[k]))
    b.wait()
    stores.append(move(layer_v, layer_out, out_s.at[2]))
    c.wait()
    stores.append(move(igrad_v, igrad, out_s.at[3]))
    for p in range(pairs):
        gwo[:, p * pw : (p + 1) * pw] = fink[p // 2, p % 2].astype(F32)
    stores.append(move(gwo, gwo_h, out_s.at[4]))
    d.wait()
    gwi[...] = fin[0].astype(F32)
    stores.append(move(gwi, gwi_h, out_s.at[5]))
    gwd[...] = fin[1].astype(F32).T
    stores.append(move(gwd, gwd_h, out_s.at[6]))
    e.wait()
    for row, out in enumerate((gl1, gbo, gl2, gbd, gbi)):
        rows_v[row] = vec[row : row + 1]
        stores.append(move(rows_v.at[row], out, out_s.at[7 + row]))
    for copy in stores:
        copy.wait()


def local(
    tn,
    dpn,
    tokens,
    cotangent,
    seq_lengths,
    features,
    ln1_gain,
    w_qkv,
    w_out,
    b_out,
    ln2_gain,
    w_in,
    b_in,
    w_down,
    b_down,
):
    rows_n, width = tokens.shape
    heads, hw, feat_n = features.shape
    pairs, pw, nb = heads // 2, 2 * hw, rows_n // BR
    ffl = w_in.shape[1]
    npeer = dpn // 2
    rp = width // npeer
    vrows = -(-(4 + tn) // 8) * 8
    dma = pltpu.SemaphoreType.DMA
    anywhere = pl.BlockSpec(memory_space=pl.ANY)

    def scratch(shape, dtype=BF16):
        return pltpu.VMEM(shape, dtype)

    out = pl.pallas_call(
        functools.partial(layer_kernel, tn, dpn),
        out_shape=(
            jax.ShapeDtypeStruct((rows_n, width), BF16),
            jax.ShapeDtypeStruct((rows_n, width), F32),
            jax.ShapeDtypeStruct((2, width, width), BF16),
            jax.ShapeDtypeStruct((8, 2, width, pw), BF16),
            jax.ShapeDtypeStruct((vrows, width), F32),
        ),
        in_specs=[pl.BlockSpec(memory_space=pltpu.SMEM)]
        + [anywhere] * 12,
        out_specs=(anywhere,) * 5,
        scratch_shapes=[
            scratch((vrows, width), F32),
            scratch((2, width, width)),
            scratch((8, 2, width, pw)),
            scratch((1, width), F32),
            scratch((1, width), F32),
            scratch((width,)),
            scratch((ffl,)),
            scratch((width,)),
            scratch((rows_n, width)),
            scratch((rows_n, width)),
            scratch((heads, hw, feat_n)),
            scratch((width, 3 * width)),
            scratch((width, width)),
            scratch((rows_n, width), F32),
            scratch((tn, 2, width, ffl)),
            scratch((tn, 8, ffl), F32),
            scratch((rows_n, width)),
            scratch((pairs, rows_n, pw)),
            scratch((pairs, rows_n, pw)),
            scratch((pairs, rows_n, pw)),
            scratch((pairs, rows_n, 2 * feat_n)),
            scratch((pairs, rows_n, 2 * feat_n)),
            scratch((pairs, 2 * pw, 2 * feat_n)),
            scratch((2 * pw, 2 * pw)),
            scratch((2 * pw, pw)),
            scratch((nb, BR, BR)),
            scratch((nb, BR, BR)),
            scratch((nb + 1, pairs, pw + 16, feat_n), F32),
            scratch((nb, pairs, pw + 16, feat_n)),
            scratch((rows_n, width), F32),
            scratch((rows_n, width)),
            scratch((rows_n, width), F32),
            scratch((rows_n, width), F32),
            scratch((rows_n, 1), F32),
            scratch((rows_n, width)),
            scratch((2, rows_n, width)),
            scratch((pairs, pw + 16, feat_n)),
            scratch((pairs, pw + 16, feat_n)),
            scratch((pairs, pw + 16, feat_n)),
            scratch((pairs, pw + 16, feat_n)),
            scratch((tn, 2, width, width)),
            scratch((2, width, width)),
            scratch((4, npeer - 1, rp, width)),
            scratch((tn - 1, rp, width)),
            scratch((8, 2, width, pw)),
            scratch((4, width, pw)),
            scratch((8, npeer - 1, rp, pw)),
            scratch((8, max(tn, 2 * (tn - 1).bit_length()), rp, pw)),
            scratch((vrows, width), F32),
            scratch((vrows, width), F32),
            scratch((npeer, vrows, width), F32),
            scratch((tn, vrows, width), F32),
            dma((12,)),
            dma((5,)),
            dma(()),
            dma(()),
            dma(()),
            dma((tn - 1,)),
            dma(()),
            dma((tn - 1,)),
            dma(()),
            dma((tn - 1,)),
            dma(()),
            dma((pairs,)),
            dma(()),
            dma((pairs,)),
            dma(()),
            dma((2,)),
            dma(()),
            dma((tn,)),
            dma(()),
            dma((tn - 1,)),
            dma(()),
            dma(()),
            dma(()),
            dma(()),
            dma(()),
            dma((4,)),
            dma(()),
            dma((8,)),
            dma((2,)),
            dma((8, (tn - 1).bit_length())),
            dma(()),
            dma((8,)),
            dma(()),
            dma((8,)),
            dma(()),
            dma(()),
            dma(()),
            dma(()),
            dma(()),
            dma(()),
        ],
        compiler_params=pltpu.CompilerParams(
            collective_id=0, has_side_effects=True, vmem_limit_bytes=63 * 1024 * 1024
        ),
    )(
        seq_lengths,
        tokens,
        cotangent,
        features,
        ln1_gain[None],
        w_qkv,
        w_out,
        b_out,
        ln2_gain[None],
        w_in,
        b_in,
        w_down,
        b_down,
    )
    row = jax.ShapeDtypeStruct((1, width), F32)

    def square(n):
        return jax.ShapeDtypeStruct((width, n * width), F32)

    done = pl.pallas_call(
        finish_kernel,
        out_shape=(out[0], out[1], square(3), square(1), square(1), square(1)) + (row,) * 5,
        in_specs=[anywhere] * 5,
        out_specs=(anywhere,) * 11,
        scratch_shapes=[
            scratch((rows_n, width)),
            scratch((rows_n, width), F32),
            scratch((2, width, width)),
            scratch((8, 2, width, pw)),
            scratch((vrows, width), F32),
            scratch((5, 1, width), F32),
            scratch((width, 3 * width), F32),
            scratch((width, width), F32),
            scratch((width, width), F32),
            scratch((width, width), F32),
            dma((5,)),
            dma((12,)),
        ],
        compiler_params=pltpu.CompilerParams(vmem_limit_bytes=63 * 1024 * 1024),
    )(*out)
    layer_out, input_grad, gwq, gwo, gwi, gwd, gl1, gbo, gl2, gbi, gbd = done
    return (
        layer_out,
        input_grad,
        gl1[0],
        gwq,
        gwo,
        gbo[0],
        gl2[0],
        gwi,
        gbi[0],
        gwd,
        gbd[0],
    )


def solution(mesh):
    tn, dpn = mesh.shape["tensor"], mesh.shape["dp"]
    rows = P(("dp", "tensor"), None)
    return jax.shard_map(
        functools.partial(local, tn, dpn),
        mesh=mesh,
        in_specs=(
            rows,
            rows,
            P("dp", None),
            P(),
            P(),
            P(),
            P(),
            P(),
            P(),
            P(None, "tensor"),
            P("tensor"),
            P("tensor", None),
            P(),
        ),
        out_specs=(
            rows,
            rows,
            P(),
            P(),
            P(),
            P(),
            P(),
            P(None, "tensor"),
            P("tensor"),
            P("tensor", None),
            P(),
        ),
        check_vma=False,
    )
```

```python
import functools

import jax
import jax.numpy as jnp
from jax import lax
from jax.experimental import pallas as pl
from jax.experimental.pallas import tpu as pltpu
from jax.sharding import PartitionSpec as P

MESH = pl.DeviceIdType.MESH
F32 = jnp.float32
BF16 = jnp.bfloat16
EPSILON = 1e-05
BR = 256
WR = 512
SQRT_2_OVER_PI = 0.7978845608028654
CUBIC = 0.044715


def dot(a, b):
    return jnp.dot(a, b, preferred_element_type=F32)


def dot_rt(a, b):
    return lax.dot_general(a, b, (((1,), (1,)), ((), ())), preferred_element_type=F32)


def dot_lt(a, b):
    return lax.dot_general(a, b, (((0,), (0,)), ((), ())), preferred_element_type=F32)


def xor(a, b, size):
    out, bit = 0, 1
    while bit < size:
        out = out + bit * lax.rem(lax.div(a, bit) + (b // bit if isinstance(b, int) else lax.div(b, bit)), 2)
        bit *= 2
    return out


def iota(shape, axis):
    return lax.broadcasted_iota(jnp.int32, shape, axis)


def layer_kernel(
    tn,
    dpn,
    lens,
    tok_h,
    cot_h,
    feats_h,
    g1_h,
    wqkv_h,
    wout_h,
    bout_h,
    g2_h,
    win_h,
    bin_h,
    wdn_h,
    bdn_h,
    layer_h,
    igrad_h,
    fin_h,
    fink_h,
    vec_h,
    vec_out,
    fin,
    fink,
    g1,
    g2,
    bout,
    bin_,
    bdn,
    tok,
    cot,
    feats,
    wqkv,
    wout,
    igrad,
    wfull,
    bfull,
    n1s,
    qs,
    ks,
    vs,
    phq,
    phk,
    featx,
    norms,
    bsw,
    mask,
    maskt,
    lst,
    sb,
    rsw_s,
    attn,
    facc,
    xh2,
    rstd2,
    n2s,
    ad,
    chf_in,
    chf_out,
    chb_in,
    chb_out,
    gbuf,
    ra,
    rb,
    rc,
    kbuf,
    kra,
    krb,
    krc,
    vec,
    va,
    vb,
    vc,
    in_s,
    out_s,
    bz_s,
    bz_r,
    wz_s,
    wz_r,
    wx_s,
    wx_r,
    wc_s,
    wc_r,
    chf_s,
    chf_r,
    chb_s,
    chb_r,
    a_s,
    a_r,
    b_s,
    b_r,
    c_s,
    c_r,
    d_s,
    d_r,
    e_s,
    e_r,
    ka_s,
    ka_r,
    kb_s,
    kb_r,
    kc_s,
    kc_r,
    kd_s,
    kd_r,
    ke_s,
    ke_r,
    va_s,
    va_r,
    vb_s,
    vb_r,
    vc_s,
    vc_r,
):
    rows_n, width = tok.shape
    heads, hw, feat_n = feats.shape
    pairs = heads // 2
    pw = 2 * hw
    nb = rows_n // BR
    seqs = lens.shape[1]
    shrink = hw ** (-0.25)
    featscale = feat_n ** (-0.5)
    npeer = dpn // 2
    rp = width // npeer

    dp = lax.axis_index("dp")
    t = lax.axis_index("tensor")
    cb = lax.rem(dp, 2)
    q = lax.div(dp, 2)
    core_dev = (dp + 1 - 2 * cb, t)

    peers = [xor(q, k, npeer) for k in range(npeer)]
    zs = [xor(t, k, tn) for k in range(tn)]

    def peer_dev(k):
        return (2 * peers[k] + cb, t)

    def z_dev(k):
        return (dp, zs[k])

    row_starts = [pl.multiple_of(peer * rp, rp) for peer in peers]

    def own_rows():
        return pl.ds(row_starts[0], rp)

    def peer_rows(k):
        return pl.ds(row_starts[k], rp)

    def load(i, src, dst):
        return pltpu.make_async_copy(src, dst, in_s.at[i])

    pairs_in = {
        "feats": (feats_h, feats),
        "g1": (g1_h, g1),
        "g2": (g2_h, g2),
        "bout": (bout_h, bout),
        "bin": (bin_h, bin_),
        "bdn": (bdn_h, bdn),
        "tok": (tok_h, tok),
        "wqkv": (wqkv_h, wqkv),
        "win": (win_h, wfull.at[0, 0]),
        "wdn": (wdn_h, wfull.at[0, 1]),
        "wout": (wout_h, wout),
        "cot": (cot_h, cot),
    }
    loads = {name: load(i, *pair) for i, (name, pair) in enumerate(pairs_in.items())}
    for copy in loads.values():
        copy.start()

    def store_layer():
        half = layer_h.shape[0] // 2
        for h in range(2):
            pltpu.make_async_copy(wfull.at[tn - 1, h], layer_h.at[pl.ds(h * half, half)], out_s.at[0]).start()

    def store_grad(b):
        rows = pl.ds(pl.multiple_of(b * WR, WR), WR)
        pltpu.make_async_copy(igrad.at[rows], igrad_h.at[rows], out_s.at[1]).start()

    def store_fin():
        return pltpu.make_async_copy(fin, fin_h, out_s.at[2])

    def store_fink(i):
        return pltpu.make_async_copy(fink.at[i], fink_h.at[i], out_s.at[3])

    bar = pltpu.get_barrier_semaphore()
    targets = [core_dev] + [peer_dev(k) for k in range(1, npeer)] + [z_dev(k) for k in range(1, tn)]
    for dev in targets:
        pl.semaphore_signal(bar, inc=1, device_id=dev, device_id_type=MESH)

    def remote(src, dst, ss, rs, dev):
        return pltpu.make_async_remote_copy(
            src_ref=src, dst_ref=dst, send_sem=ss, recv_sem=rs, device_id=dev, device_id_type=MESH
        )

    def arrived(ref, sem):
        remote(ref, ref, a_s, sem, core_dev).wait_recv()

    def sent(ref, sem):
        remote(ref, ref, sem, a_r.at[0], core_dev).wait_send()

    def bz_copy(k):
        return remote(bfull.at[0], bfull.at[k], bz_s, bz_r, z_dev(k))

    def wz_copy(k):
        source, via = (0, k) if k == 1 or k % 2 == 0 else (k - 1, 1)
        return remote(
            wfull.at[source, cb, own_rows()], wfull.at[k, cb, own_rows()], wz_s, wz_r.at[k - 1], z_dev(via)
        )

    def wx_copy(k, j):
        here = wfull.at[k, cb, own_rows()]
        return remote(here, here, wx_s, wx_r.at[k - 1], peer_dev(j))

    def wc_copy(k):
        return remote(wfull.at[k, cb], wfull.at[k, cb], wc_s, wc_r.at[k - 1], core_dev)

    def wc_recv(k):
        here = wfull.at[k, 1 - cb]
        return remote(here, here, wc_s, wc_r.at[k - 1], core_dev)

    def w_spread(k):
        wz_copy(k).wait_recv()
        if k > 1 and k % 2 == 0:
            wz_copy(k + 1).start()
        for j in range(1, npeer):
            wx_copy(k, j).start()

    def w_swap(k):
        arrived(wfull.at[k, cb, pl.ds(0, (npeer - 1) * rp)], wx_r.at[k - 1])
        wc_copy(k).start()

    levels = (tn - 1).bit_length()
    up_first = (1, 3, 5, 7), (8, 9, 10, 12)

    def up_due(at, p):
        return up_first[at - 1][p % 4] if at < 3 and p < 4 else 10 + p

    def down_due(hops, p):
        due = min(3 * hops + p, 8 + 2 * p)
        return due + due % 2 if due > 8 else due

    def up_copy(p):
        return remote(chf_out.at[p], chf_in.at[p], chf_s, chf_r.at[p], (dp, lax.rem(t + 1, tn)))

    def up_handle(p):
        @pl.when(t > 0)
        def _():
            up_copy(p).wait_recv()

        chf_out[p] = (lst[nb, p] + passing * chf_in[p].astype(F32)).astype(BF16)
        up_copy(p).start()

    def up_slots(k, low, high):
        for at in range(1, tn - 1):
            for p in range(pairs):
                if low <= up_due(at, p) < high:

                    @pl.when((t == at) & (k == up_due(at, p)))
                    def _(p=p):
                        up_handle(p)

    def down_copy(p):
        return remote(chb_out.at[p], chb_in.at[p], chb_s, chb_r.at[p], (dp, lax.rem(t + tn - 1, tn)))

    def down_handle(p):
        @pl.when(t < tn - 1)
        def _():
            down_copy(p).wait_recv()

        own = lst[nb - 1, p]
        for b in range(nb - 2, -1, -1):
            own = keep_of(b) * own + lst[b, p]
        chb_out[p] = (own + passing * chb_in[p].astype(F32)).astype(BF16)
        down_copy(p).start()

    def down_slots(k, low, high):
        for hops in range(tn - 1):
            for p in range(pairs):
                if low <= down_due(hops, p) < high:

                    @pl.when((t == tn - 1 - hops) & (k == down_due(hops, p)))
                    def _(p=p):
                        down_handle(p)

    def place_of(turn):
        return jnp.where(turn < tn // 2, 2 * turn + 1, 2 * (tn - 1 - turn))

    def a_copy(turn):
        turn = jnp.int32(turn)
        return remote(
            gbuf.at[place_of(turn), 1 - cb], ra.at[lax.rem(turn, 2)], a_s, a_r.at[lax.rem(turn, 2)], core_dev
        )

    def b_copy(s, k):
        s = jnp.int32(s)
        return remote(gbuf.at[s, cb, peer_rows(k)], rb.at[lax.rem(s, 4), k - 1], b_s, b_r.at[s], peer_dev(k))

    def c_copy(s):
        return remote(gbuf.at[s, cb, own_rows()], rc.at[s - 1], c_s, c_r.at[s - 1], z_dev(s & -s))

    def d_copy(k):
        here = fin.at[cb, own_rows()]
        return remote(here, here, d_s, d_r, peer_dev(k))

    def e_copy():
        return remote(fin.at[cb], fin.at[cb], e_s, e_r, core_dev)

    def e_recv():
        return remote(fin.at[1 - cb], fin.at[1 - cb], e_s, e_r, core_dev)

    def ka_copy(i):
        i = jnp.int32(i)
        return remote(kbuf.at[i, 1 - cb], kra.at[lax.rem(i, 4)], ka_s, ka_r.at[lax.rem(i, 4)], core_dev)

    def kb_copy(i, k):
        return remote(
            kbuf.at[i, cb, peer_rows(k)], krb.at[i, k - 1], kb_s, kb_r.at[i], peer_dev(k)
        )

    def kc_copy(i, k):
        return remote(krc.at[i, 0], krc.at[i, k], kc_s.at[0], kc_r.at[i, 0], z_dev(k))

    def ks_copy(i, l):
        return remote(
            krc.at[i, 2 * l], krc.at[i, 2 * l + 1], kc_s.at[1], kc_r.at[i, l], z_dev(1 << l)
        )

    def kd_copy(i, k):
        here = fink.at[i, cb, own_rows()]
        return remote(here, here, kd_s, kd_r.at[i], peer_dev(k))

    def ke_copy(i):
        return remote(fink.at[i, cb], fink.at[i, cb], ke_s, ke_r.at[i], core_dev)

    def ke_recv(i):
        return remote(fink.at[i, 1 - cb], fink.at[i, 1 - cb], ke_s, ke_r.at[i], core_dev)

    def a_start(turn):
        a_copy(turn).start()

    def a_finish(turn):
        turn = jnp.int32(turn)
        a_copy(turn).wait_recv()
        s = place_of(turn)
        gbuf[s, cb] = (gbuf[s, cb].astype(F32) + ra[lax.rem(turn, 2)].astype(F32)).astype(BF16)
        for k in range(1, npeer):
            b_copy(s, k).start()

    def b_sum(s):
        s = jnp.int32(s)
        arrived(rb.at[lax.rem(s, 4)], b_r.at[s])
        total = gbuf[s, cb, own_rows()].astype(F32)
        for k in range(1, npeer):
            total = total + rb[lax.rem(s, 4), k - 1].astype(F32)
        return total.astype(BF16)

    def b_finish(s):
        gbuf[s, cb, own_rows()] = b_sum(s)

    def c_add(s):
        step = 1
        while step < (s & -s if s else tn):
            c_copy(s + step).wait_recv()
            gbuf[s, cb, own_rows()] = (
                gbuf[s, cb, own_rows()].astype(F32) + rc[s + step - 1].astype(F32)
            ).astype(BF16)
            step *= 2

    def c_start(s):
        c_add(s)
        c_copy(s).start()

    def c_finish():
        total = gbuf[0, cb, own_rows()].astype(F32)
        step = 1
        while step < tn:
            c_copy(step).wait_recv()
            total = total + rc[step - 1].astype(F32)
            step *= 2
        fin[cb, own_rows()] = total.astype(BF16)
        for k in range(1, npeer):
            d_copy(k).start()

    def d_finish():
        arrived(fin.at[0, pl.ds(0, (npeer - 1) * rp)], d_r)
        e_copy().start()

    def e_finish():
        e_recv().wait_recv()

    def k_a_start(i, both):
        kbuf[i, 0] = both[:, :pw].astype(BF16)
        kbuf[i, 1] = both[:, pw:].astype(BF16)
        ka_copy(i).start()

    def k_a_finish(i):
        i = jnp.int32(i)
        ka_copy(i).wait_recv()
        kbuf[i, cb] = (kbuf[i, cb].astype(F32) + kra[lax.rem(i, 4)].astype(F32)).astype(BF16)
        for k in range(1, npeer):
            kb_copy(i, k).start()

    def k_b_sum(i):
        arrived(krb.at[i], kb_r.at[i])
        total = kbuf[i, cb, own_rows()].astype(F32)
        for k in range(1, npeer):
            total = total + krb[i, k - 1].astype(F32)
        krc[i, 0] = total.astype(BF16)

    def k_spread(i, total):
        fink[i, cb, own_rows()] = total.astype(BF16)
        for k in range(1, npeer):
            kd_copy(i, k).start()

    def k_b_finish(i):
        k_b_sum(i)
        for k in range(1, tn):
            kc_copy(i, k).start()

    def k_c_finish(i):
        arrived(krc.at[i, pl.ds(1, tn - 1)], kc_r.at[i, 0])
        total = krc[i, zs[0]].astype(F32)
        for j in range(1, tn):
            total = total + krc[i, zs[j]].astype(F32)
        k_spread(i, total)

    def s_b_finish(i):
        k_b_sum(i)
        ks_copy(i, 0).start()

    def s_sum(i, l):
        ks_copy(i, l).wait_recv()
        return krc[i, 2 * l].astype(F32) + krc[i, 2 * l + 1].astype(F32)

    def s_middle(i):
        for l in range(levels - 1):
            krc[i, 2 * l + 2] = s_sum(i, l).astype(BF16)
            ks_copy(i, l + 1).start()

    def s_c_finish(i):
        k_spread(i, s_sum(i, levels - 1))

    def k_d_finish(i):
        arrived(fink.at[i, 0, pl.ds(0, (npeer - 1) * rp)], kd_r.at[i])
        ke_copy(i).start()

    def k_e_finish(i):
        ke_recv(i).wait_recv()

    offsets = [jnp.int32(0)]
    for c in range(1, seqs):
        offsets.append(offsets[-1] + lens[0, c - 1])
    first = t * rows_n

    def seg_at(r):
        seg = -1
        for off in offsets:
            seg = seg + jnp.where(r >= off, 1, 0)
        return seg

    def seg_array(shape, axis, start):
        places = iota(shape, axis) + start
        seg = jnp.full(shape, -1, jnp.int32)
        for off in offsets:
            seg = seg + jnp.where(places >= off, 1, 0)
        return seg

    before = seg_at(first - 1)
    closing = seg_at(first + rows_n - 1)
    passing = jnp.where(before == closing, 1.0, 0.0)

    def prev_of(b):
        return seg_at(first + b * BR - 1)

    def last_of(b):
        return seg_at(first + b * BR + BR - 1)

    def keep_of(b):
        return jnp.where(prev_of(b) == last_of(b), 1.0, 0.0)

    def ending(b):
        return seg_array((BR, pw), 0, first + b * BR) == last_of(b)

    def reached(b):
        return seg_array((BR, pw), 0, first + b * BR) == prev_of(b)

    def block(b):
        return pl.ds(pl.multiple_of(b * BR, BR), BR)

    nw = rows_n // WR

    def wide(b):
        return pl.ds(pl.multiple_of(b * WR, WR), WR)

    def lanes(p):
        return pl.ds(pl.multiple_of(p * pw, pw), pw)

    def as_row(ref):
        return ref[...].astype(F32).reshape(1, ref.shape[0])

    low_lane = iota((BR, pw), 1) < hw
    low_row = iota((pw, feat_n), 0) < hw
    row_id = iota((pw, feat_n), 0)

    for name in ("feats", "g1", "g2", "bout", "bin", "bdn"):
        loads[name].wait()
    featx[...] = jnp.zeros_like(featx)
    for p in range(pairs):
        for o in range(2):
            featx[p, o * hw : (o + 1) * hw, o * feat_n : (o + 1) * feat_n] = feats[2 * p + o]
            featx[p, pw + o * hw : pw + (o + 1) * hw, o * feat_n : (o + 1) * feat_n] = jnp.full(
                (hw, feat_n), -0.5, BF16
            )
    ro, co = iota((2 * pw, 2 * pw), 0), iota((2 * pw, 2 * pw), 1)
    norms[...] = jnp.where((lax.rem(ro, pw) < hw) == (co < pw), -0.5, 0.0).astype(BF16)

    def build_mask(b, _):
        seg_i = seg_array((BR, BR), 0, first + b * BR)
        seg_j = seg_array((BR, BR), 1, first + b * BR)
        same = seg_i == seg_j
        i, j = iota((BR, BR), 0), iota((BR, BR), 1)
        mask[b] = jnp.where(same & (i >= j), 1.0, 0.0).astype(BF16)
        return 0

    lax.fori_loop(0, nb, build_mask, 0)
    lst[0] = jnp.zeros(lst.shape[1:], F32)
    vec[...] = jnp.zeros_like(vec)

    @pl.when(t == 0)
    def _():
        chf_in[...] = jnp.zeros_like(chf_in)


    loads["win"].wait()
    loads["wdn"].wait()
    pl.semaphore_wait(bar, len(targets))
    bfull[0] = jnp.broadcast_to(as_row(bin_), bfull.shape[1:])
    wz_copy(1).start()
    wz_copy(2).start()
    for k in range(1, tn):
        bz_copy(k).start()

    def features_of(x, p):
        wide = x.astype(F32)
        square = wide * wide
        high = square.astype(BF16)
        rest = (square - high.astype(F32)).astype(BF16)
        norm = dot(jnp.concatenate([high, rest], 1), norms[...])
        repeats = [norm[:, :pw]] * (feat_n // pw) + [norm[:, pw:]] * (feat_n // pw)
        arg = dot(x, featx[p, :pw]) + jnp.concatenate(repeats, 1)
        return (jnp.exp(arg) * featscale).astype(BF16)

    def normalized(x):
        centre = jnp.mean(x, -1, keepdims=True)
        shifted = x - centre
        inverse = lax.rsqrt(jnp.mean(shifted * shifted, -1, keepdims=True) + EPSILON)
        return shifted * inverse, inverse

    def values_of(p, b):
        wide = vs[p, block(b)].astype(F32)
        return jnp.where(low_lane, wide, 1.0), jnp.where(low_lane, 1.0, wide)

    def keys_block(b, _):
        scaled, _inv = normalized(tok[wide(b)].astype(F32))
        normed = (scaled * g1[...]).astype(BF16)
        n1s[wide(b)] = normed
        key = (dot(normed, wqkv[:, width : 2 * width]) * shrink).astype(BF16)
        val = dot(normed, wqkv[:, 2 * width :]).astype(BF16)
        for p in range(pairs):
            ks[p, wide(b)] = key[:, p * pw : (p + 1) * pw]
            vs[p, wide(b)] = val[:, p * pw : (p + 1) * pw]

        return 0

    loads["tok"].wait()
    loads["wqkv"].wait()
    lax.fori_loop(0, nw, keys_block, 0)

    def state_pair(p, _):
        for c in range(nw):
            phk[p, wide(c)] = features_of(ks[p, wide(c)], p)
        for b in range(nb):
            feat = phk[p, block(b)]
            end = ending(b)
            ve, vo = values_of(p, b)
            ue = dot_lt(jnp.where(end, ve, 0.0).astype(BF16), feat[:, :feat_n])
            uo = dot_lt(jnp.where(end, vo, 0.0).astype(BF16), feat[:, feat_n:])
            keep = keep_of(b)
            lst[b + 1, p, :pw] = keep * lst[b, p, :pw] + jnp.where(low_row, ue, uo)
            lst[b + 1, p, pw : pw + 8] = keep * lst[b, p, pw : pw + 8] + ue[hw : hw + 8]
            lst[b + 1, p, pw + 8 :] = keep * lst[b, p, pw + 8 :] + uo[:8]

        @pl.when(t == 0)
        def _():
            up_handle(p)


        @pl.when(p == 3)
        def _():
            w_spread(1)

        return 0

    lax.fori_loop(0, pairs, state_pair, 0)

    def queries_block(b, _):
        up_slots(b, 0, nw)
        query = (dot(n1s[wide(b)], wqkv[:, :width]) * shrink).astype(BF16)
        for p in range(pairs):
            qs[p, wide(b)] = query[:, p * pw : (p + 1) * pw]

        @pl.when(b == nw - 1)
        def _():
            w_spread(2)

        return 0

    lax.fori_loop(0, nw, queries_block, 0)

    def features_pair(p, _):
        up_slots(nw + p, nw, nw + pairs)
        for b in range(nw):
            phq[p, wide(b)] = features_of(qs[p, wide(b)], p)
        return 0

    lax.fori_loop(0, pairs, features_pair, 0)

    def state_halves(state):
        top = state[:pw]
        even = jnp.where(low_row, top, jnp.broadcast_to(state[pw : pw + 1], top.shape)).astype(BF16)
        odd = jnp.where(low_row, jnp.broadcast_to(state[pw + 8 : pw + 9], top.shape), top).astype(BF16)
        return even, odd

    slot = nw + pairs

    def inside_pair(p, _):
        up_slots(slot + p, slot, slot + pairs)

        @pl.when(p == 3)
        def _():
            w_spread(3)

        for b in range(nb):
            for o, (val, part) in enumerate(zip(values_of(p, b), (facc, xh2))):
                fq = phq[p, block(b), o * feat_n : (o + 1) * feat_n]
                fk = phk[p, block(b), o * feat_n : (o + 1) * feat_n]
                scores = jnp.where(mask[b].astype(F32) > 0, dot_rt(fq, fk), 0.0).astype(BF16)
                part[block(b), lanes(p)] = dot(scores, val.astype(BF16))
        return 0

    lax.fori_loop(0, pairs, inside_pair, 0)

    ri, ci = iota((2 * pw, pw), 0), iota((2 * pw, pw), 1)
    swap = (lax.rem(ri, pw) < hw) != (ci < hw)
    bsw[...] = jnp.where(swap, 1.0, 0.0).astype(BF16)

    def build_turned(b, _):
        seg_i = seg_array((BR, BR), 0, first + b * BR)
        seg_j = seg_array((BR, BR), 1, first + b * BR)
        later = iota((BR, BR), 1) >= iota((BR, BR), 0)
        maskt[b] = jnp.where((seg_i == seg_j) & later, 1.0, 0.0).astype(BF16)
        return 0

    lax.fori_loop(0, nb, build_turned, 0)

    @pl.when(t == tn - 1)
    def _():
        chb_in[...] = jnp.zeros_like(chb_in)

    def attend_pair(p, _):
        up_slots(slot + pairs + p, slot + pairs, slot + 2 * pairs)

        @pl.when(p == 2)
        def _():
            w_swap(1)

        @pl.when(t == tn - 1)
        def _():
            up_copy(p).wait_recv()

        incoming = chf_in[p].astype(F32)
        for b in range(nb):
            first_pass = jnp.where(before == prev_of(b), 1.0, 0.0)
            state = (lst[b, p] + first_pass * incoming).astype(BF16)
            sb[b, p] = state
            reach = reached(b)
            outs = []
            for o, (st, part) in enumerate(zip(state_halves(state.astype(F32)), (facc, xh2))):
                fq = phq[p, block(b), o * feat_n : (o + 1) * feat_n]
                outs.append(part[block(b), lanes(p)] + jnp.where(reach, dot_rt(fq, st), 0.0))
            inverse = 1.0 / jnp.where(low_lane, outs[1], outs[0])
            rsw_s[block(b), lanes(p)] = inverse
            num = jnp.where(low_lane, outs[0], outs[1])
            attn[block(b), lanes(p)] = (num * pltpu.roll(inverse, hw, 1)).astype(BF16)
        return 0

    lax.fori_loop(0, pairs, attend_pair, 0)

    def hidden_block(b, _):
        h1 = tok[wide(b)].astype(F32) + (dot(attn[wide(b)], wout[...]) + as_row(bout))
        scaled, inverse = normalized(h1)
        xh2[wide(b)] = scaled
        rstd2[wide(b)] = inverse
        n2s[wide(b)] = (scaled * g2[...]).astype(BF16)
        facc[wide(b)] = h1 + as_row(bdn)
        return 0

    loads["wout"].wait()
    lax.fori_loop(0, nw, hidden_block, 0)
    loads["cot"].wait()

    def feed_chunk(turn, _):
        s = place_of(turn)

        @pl.when(s > 0)
        def _():
            for k in range(1, tn):

                @pl.when(s == k)
                def _(k=k):
                    wc_recv(k).wait_recv()

        def rows_block(b, total):
            w_in = wfull[s, 0]
            w_dn = wfull[s, 1]
            u = dot(n2s[wide(b)], w_in) + bfull[s, 0:1]
            u2 = u * u
            th = jnp.tanh(u * (SQRT_2_OVER_PI + SQRT_2_OVER_PI * CUBIC * u2))
            half = 0.5 + 0.5 * th
            act = (u * half).astype(BF16)
            slope = half + (0.5 * u) * (1.0 - th * th) * (
                SQRT_2_OVER_PI + 3.0 * SQRT_2_OVER_PI * CUBIC * u2
            )
            ad[0, wide(b)] = act
            facc[wide(b)] += dot(act, w_dn)
            du = (slope * dot_rt(cot[wide(b)], w_dn)).astype(BF16)
            ad[1, wide(b)] = du
            back = dot_rt(du, w_in)

            @pl.when(turn == 0)
            def _():
                igrad[wide(b)] = back

            @pl.when(turn > 0)
            def _():
                igrad[wide(b)] += back

            @pl.when((turn >= 1) & (b == 0))
            def _():
                a_finish(jnp.maximum(turn - 1, 0))

            @pl.when((turn == 0) & (b == nw - 1))
            def _():
                w_swap(3)

            @pl.when((turn == 1) & (b == 0))
            def _():
                w_swap(2)

            return total + jnp.sum(du.astype(F32), 0, keepdims=True)

        total = lax.fori_loop(0, nw, rows_block, jnp.zeros((1, wfull.shape[3]), F32))
        vec[pl.ds(4 + s, 1)] = total

        @pl.when(turn == tn - 1)
        def _():
            b_finish(1)
            c_start(1)

        gbuf[s, 0] = dot_lt(n2s[...], ad[1]).astype(BF16)
        gbuf[s, 1] = dot_lt(cot[...], ad[0]).astype(BF16)
        a_start(turn)
        return 0

    arrived(bfull.at[pl.ds(1, tn - 1)], bz_r)
    lax.fori_loop(0, tn, feed_chunk, 0)
    sent(bfull.at[pl.ds(1, tn - 1)], bz_s)
    sent(wfull.at[pl.ds(0, tn - 1), 0, pl.ds(0, rp)], wz_s)
    sent(wfull.at[pl.ds(0, tn - 1), 0, pl.ds(0, (npeer - 1) * rp)], wx_s)
    sent(wfull.at[pl.ds(0, tn - 1), 0], wc_s)

    def norm_back(dn, gain, scaled, inverse):
        g = dn * gain
        inner = jnp.mean(g, -1, keepdims=True)
        cross = jnp.mean(g * scaled, -1, keepdims=True)
        return inverse * (g - inner - scaled * cross)


    def branch_block(b, carry):
        gl2, gbo, gbd = carry
        wfull[tn - 1, b] = facc[wide(b)].astype(BF16)
        dy = cot[wide(b)].astype(F32)
        dn2 = igrad[wide(b)]
        scaled = xh2[wide(b)]
        dh1 = dy + norm_back(dn2, g2[...], scaled, rstd2[wide(b)])
        igrad[wide(b)] = dh1
        dob = dh1.astype(BF16)
        n2s[wide(b)] = dob
        dattn = dot_rt(dob, wout[...])
        lane_id = iota((WR, pw), 1)
        low_half = lane_id < hw
        for p in range(pairs):
            da = dattn[:, p * pw : (p + 1) * pw]
            inverse = rsw_s[wide(b), p * pw : (p + 1) * pw]
            dnum = da * pltpu.roll(inverse, hw, 1)
            prod = da * attn[wide(b), p * pw : (p + 1) * pw].astype(F32)
            high = prod.astype(BF16)
            rest = (prod - high.astype(F32)).astype(BF16)
            dden = -dot(jnp.concatenate([high, rest], 1), bsw[...]) * inverse
            dhi = dden.astype(BF16).astype(F32)
            dlo = dden - dhi
            even = jnp.where(lane_id == hw, dhi, jnp.where(lane_id == hw + 1, dlo, 0.0))
            odd = jnp.where(lane_id == 0, dhi, jnp.where(lane_id == 1, dlo, 0.0))
            ad[0, wide(b), p * pw : (p + 1) * pw] = jnp.where(low_half, dnum, even).astype(BF16)
            ad[1, wide(b), p * pw : (p + 1) * pw] = jnp.where(low_half, odd, dnum).astype(BF16)
        for c in range(nb // nw):
            at = b * (nb // nw) + c
            reach = reached(at)
            for p in range(pairs):
                ge, go = (
                    dot_lt(
                        jnp.where(reach, ad[o, block(at), p * pw : (p + 1) * pw].astype(F32), 0.0).astype(BF16),
                        phq[p, block(at), o * feat_n : (o + 1) * feat_n],
                    )
                    for o in range(2)
                )
                lst[at, p, :pw] = jnp.where(low_row, ge, go)
                lst[at, p, pw : pw + 8] = jnp.broadcast_to(ge[hw : hw + 1] + ge[hw + 1 : hw + 2], (8, feat_n))
                lst[at, p, pw + 8 :] = jnp.broadcast_to(go[0:1] + go[1:2], (8, feat_n))

        @pl.when(b == 0)
        def _():
            a_finish(tn - 1)
            b_finish(3)
            c_start(3)

        return (
            gl2 + jnp.sum(dn2 * scaled, 0, keepdims=True),
            gbo + jnp.sum(dob.astype(F32), 0, keepdims=True),
            gbd + jnp.sum(dy, 0, keepdims=True),
        )

    zero_row = jnp.zeros((1, width), F32)
    gl2, gbo, gbd = lax.fori_loop(0, nw, branch_block, (zero_row,) * 3)
    store_layer()
    vec[1:2] = gbo
    vec[2:3] = gl2
    vec[3:4] = gbd
    half_blocks = nb // 2

    def grad_at(j, b):
        if isinstance(b, int):
            return j, b // half_blocks, pl.ds((b % half_blocks) * BR, BR)
        rows = pl.ds(pl.multiple_of(lax.rem(b, half_blocks) * BR, BR), BR)
        return j, lax.div(b, half_blocks), rows

    half = rows_n // 2

    def weight_grad(ja, pa, jb, pb):
        total = 0.0
        for h in range(2):
            both = [wfull[j, h, :half, lanes(p)] for j, p in ((ja, pa), (jb, pb))]
            total = total + dot_lt(n1s[h * half : (h + 1) * half], jnp.concatenate(both, 1))
        return total

    def arg_back(darg, x, p):
        both = dot_rt(darg, featx[p])
        return (both[:, :pw] + (2.0 * x.astype(F32)) * both[:, pw:]) * shrink

    out_grad = dot_lt(attn[...], n2s[...])
    for i in range(2):
        k_a_start(i, out_grad[:, i * 2 * pw : (i + 1) * 2 * pw])

    def query_half(i, _):
        down_slots(i, 0, 2 * pairs)
        p, half = lax.div(i, 2), lax.rem(i, 2)
        for c in range(nb // 2):
            b = half * (nb // 2) + c
            se, so = state_halves(sb[b, p].astype(F32))
            reach = reached(b)
            ve, vo = values_of(p, b)
            dargs = []
            for o, (val, st) in enumerate(((ve, se), (vo, so))):
                dn = ad[o, block(b), lanes(p)]
                cdn = jnp.where(reach, dn.astype(F32), 0.0).astype(BF16)
                fq = phq[p, block(b), o * feat_n : (o + 1) * feat_n]
                fk = phk[p, block(b), o * feat_n : (o + 1) * feat_n]
                da = jnp.where(mask[b].astype(F32) > 0, dot_rt(dn, val.astype(BF16)), 0.0).astype(BF16)
                dfq = dot(da, fk) + dot(cdn, st)
                dargs.append((dfq * fq.astype(F32)).astype(BF16))
            wfull[grad_at(0, b) + (lanes(p),)] = arg_back(
                jnp.concatenate(dargs, 1), qs[p, block(b)], p
            ).astype(BF16)

        @pl.when(i == 1)
        def _():
            k_a_finish(0)
            k_a_finish(1)
            b_finish(2)

        @pl.when(i == 3)
        def _():
            k_a_start(2, weight_grad(0, 0, 0, 1))

        @pl.when(i == 5)
        def _():
            k_a_finish(2)
            b_finish(0)

        @pl.when(i == 7)
        def _():
            k_a_start(3, weight_grad(0, 2, 0, 3))
            c_start(2)

        return 0

    lax.fori_loop(0, 2 * pairs, query_half, 0)

    def key_pair(p, _):
        down_slots(2 * (pairs + p), 2 * pairs, 4 * pairs)

        @pl.when(t == 0)
        def _():
            down_copy(p).wait_recv()

        grad = chb_in[p].astype(F32)
        for b in range(nb - 1, -1, -1):
            top = grad[:pw]
            halves = []
            for o in range(2):
                dz = jnp.broadcast_to(grad[pw + 8 * o : pw + 8 * o + 1], top.shape)
                dz_hi = dz.astype(BF16).astype(F32)
                at = hw * (1 - o)
                filler = jnp.where(row_id == at, dz_hi, jnp.where(row_id == at + 1, dz - dz_hi, 0.0))
                halves.append(
                    (jnp.where(low_row, top, filler) if o == 0 else jnp.where(low_row, filler, top)).astype(BF16)
                )
            end = ending(b)
            ve, vo = values_of(p, b)
            dargs, dvs = [], []
            for o, (val, ds) in enumerate(((ve, halves[0]), (vo, halves[1]))):
                dn = ad[o, block(b), lanes(p)]
                fq = phq[p, block(b), o * feat_n : (o + 1) * feat_n]
                fk = phk[p, block(b), o * feat_n : (o + 1) * feat_n]
                at = jnp.where(maskt[b].astype(F32) > 0, dot_rt(fk, fq), 0.0).astype(BF16)
                dat = jnp.where(maskt[b].astype(F32) > 0, dot_rt(val.astype(BF16), dn), 0.0).astype(BF16)
                ev = jnp.where(end, val, 0.0).astype(BF16)
                dfk = dot(dat, fq) + dot(ev, ds)
                dargs.append((dfk * fk.astype(F32)).astype(BF16))
                dvs.append(dot(at, dn) + jnp.where(end, dot_rt(fk, ds), 0.0))
            wfull[grad_at(1, b) + (lanes(p),)] = arg_back(
                jnp.concatenate(dargs, 1), ks[p, block(b)], p
            ).astype(BF16)
            wfull[grad_at(2, b) + (lanes(p),)] = jnp.where(
                low_lane, dvs[0], dvs[1]
            ).astype(BF16)
            if b > 0:
                grad = keep_of(b) * grad + lst[b, p]

        k_a_start(4 + p, weight_grad(1, p, 2, p))

        @pl.when(p == 0)
        def _():
            k_a_finish(3)
            s_b_finish(0)
            s_b_finish(1)

        @pl.when(p >= 1)
        def _():
            k_a_finish(3 + p)

        @pl.when(p == 1)
        def _():
            s_b_finish(2)

        @pl.when(p == 2)
        def _():
            c_finish()
            s_b_finish(3)
            s_middle(0)
            s_middle(1)

        @pl.when(p == 3)
        def _():
            s_b_finish(4)
            s_middle(2)

        return 0

    lax.fori_loop(0, pairs, key_pair, 0)

    def input_block(b, gl1):
        dn1 = dot_rt(wfull[0, b, :WR], wqkv[:, :width])
        for j in range(1, 3):
            dn1 = dn1 + dot_rt(wfull[j, b, :WR], wqkv[:, j * width : (j + 1) * width])
        scaled, inverse = normalized(tok[wide(b)].astype(F32))
        igrad[wide(b)] += norm_back(dn1, g1[...], scaled, inverse)
        store_grad(b)

        @pl.when(b == 0)
        def _():
            k_a_finish(7)
            s_middle(3)

        @pl.when(b == 1)
        def _():
            s_b_finish(5)
            s_middle(4)

        return gl1 + jnp.sum(dn1 * scaled, 0, keepdims=True)

    vec[0:1] = lax.fori_loop(0, nw, input_block, zero_row)
    va_copy = remote(vec, va, va_s, va_r, core_dev)
    va_copy.start()
    k_b_finish(6)
    va_copy.wait_recv()
    vb[0] = vec[...] + va[...]
    vb_copies = [remote(vb.at[0], vb.at[k], vb_s, vb_r, peer_dev(k)) for k in range(1, npeer)]
    for copy in vb_copies:
        copy.start()
    k_b_finish(7)
    s_c_finish(0)
    s_c_finish(1)
    s_c_finish(2)
    s_middle(5)
    s_c_finish(3)
    s_c_finish(4)
    arrived(vb.at[pl.ds(1, npeer - 1)], vb_r)
    total = vb[peers[0]]
    for j in range(1, npeer):
        total = total + vb[peers[j]]
    vc[0] = total
    vc_copies = [remote(vc.at[0], vc.at[k], vc_s, vc_r, z_dev(k)) for k in range(1, tn)]
    for copy in vc_copies:
        copy.start()
    k_c_finish(6)
    k_c_finish(7)
    s_c_finish(5)
    d_finish()
    for i in range(4):
        k_d_finish(i)
    arrived(vc.at[pl.ds(1, tn - 1)], vc_r)
    total = vc[zs[0]]
    for j in range(1, tn):
        total = total + vc[zs[j]]
    own = vc[0, 4:5]
    for k in range(1, tn):
        own = own + vc[k, 4 + k : 5 + k]
    vec_out[...] = total
    vec_out[4:5] = own
    pltpu.make_async_copy(vec_out, vec_h, out_s.at[4]).start()
    k_d_finish(4)
    k_d_finish(6)
    k_d_finish(7)
    k_d_finish(5)
    e_finish()
    store_fin().start()
    for i in (0, 1, 2, 3, 4, 6, 7, 5):
        k_e_finish(i)
        store_fink(i).start()
    sent(vec, va_s)
    sent(vb.at[pl.ds(1, npeer - 1)], vb_s)
    sent(vc.at[pl.ds(1, tn - 1)], vc_s)
    sent(gbuf.at[:, 0], a_s)
    sent(rb, b_s)
    sent(rc, c_s)
    sent(fin.at[0, pl.ds(0, (npeer - 1) * rp)], d_s)
    sent(fin.at[0], e_s)
    sent(kbuf.at[:, 0], ka_s)
    sent(krb, kb_s)
    sent(krc.at[pl.ds(0, 2), pl.ds(1, tn - 1)], kc_s.at[0])
    sent(krc.at[pl.ds(0, 6), pl.ds(0, levels)], kc_s.at[1])
    sent(fink.at[:, 0, pl.ds(0, (npeer - 1) * rp)], kd_s)
    sent(fink.at[:, 0], ke_s)

    @pl.when(t < tn - 1)
    def _():
        sent(chf_out, chf_s)

    @pl.when(t > 0)
    def _():
        sent(chb_out, chb_s)

    pltpu.make_async_copy(vec_out, vec_h, out_s.at[4]).wait()
    pltpu.make_async_copy(layer_h, layer_h, out_s.at[0]).wait()
    pltpu.make_async_copy(igrad, igrad_h, out_s.at[1]).wait()
    store_fin().wait()
    pltpu.make_async_copy(fink, fink_h, out_s.at[3]).wait()


def finish_kernel(
    layer_in, igrad_in, fin_h, fink_h, vec_h, layer_out, igrad, gwq_h, gwo_h, gwi_h, gwd_h, gl1, gbo, gl2, gbi, gbd,
    layer_v, igrad_v, fin, fink, vec, rows_v, gwq, gwo, gwi, gwd, in_s, out_s,
):
    def move(src, dst, sem):
        copy = pltpu.make_async_copy(src, dst, sem)
        copy.start()
        return copy

    pairs = fink.shape[0] // 2
    width, pw = fink.shape[2:]
    kinds = ((fink_h, fink), (layer_in, layer_v), (igrad_in, igrad_v), (fin_h, fin), (vec_h, vec))
    a, b, c, d, e = (move(src, dst, in_s.at[n]) for n, (src, dst) in enumerate(kinds))
    stores = []
    a.wait()
    for k in range(2):
        rows = pl.ds(k * width // 2, width // 2)
        for p in range(pairs):
            at = slice(p * pw, (p + 1) * pw)
            gwq[rows, at] = fink[2 + p // 2, p % 2, rows].astype(F32)
            gwq[rows, width + p * pw : width + (p + 1) * pw] = fink[4 + p, 0, rows].astype(F32)
            gwq[rows, 2 * width + p * pw : 2 * width + (p + 1) * pw] = fink[4 + p, 1, rows].astype(F32)
        stores.append(move(gwq.at[rows], gwq_h.at[rows], out_s.at[k]))
    b.wait()
    stores.append(move(layer_v, layer_out, out_s.at[2]))
    c.wait()
    stores.append(move(igrad_v, igrad, out_s.at[3]))
    for p in range(pairs):
        gwo[:, p * pw : (p + 1) * pw] = fink[p // 2, p % 2].astype(F32)
    stores.append(move(gwo, gwo_h, out_s.at[4]))
    d.wait()
    gwi[...] = fin[0].astype(F32)
    stores.append(move(gwi, gwi_h, out_s.at[5]))
    gwd[...] = fin[1].astype(F32).T
    stores.append(move(gwd, gwd_h, out_s.at[6]))
    e.wait()
    for row, out in enumerate((gl1, gbo, gl2, gbd, gbi)):
        rows_v[row] = vec[row : row + 1]
        stores.append(move(rows_v.at[row], out, out_s.at[7 + row]))
    for copy in stores:
        copy.wait()


def local(
    tn,
    dpn,
    tokens,
    cotangent,
    seq_lengths,
    features,
    ln1_gain,
    w_qkv,
    w_out,
    b_out,
    ln2_gain,
    w_in,
    b_in,
    w_down,
    b_down,
):
    rows_n, width = tokens.shape
    heads, hw, feat_n = features.shape
    pairs, pw, nb = heads // 2, 2 * hw, rows_n // BR
    ffl = w_in.shape[1]
    npeer = dpn // 2
    rp = width // npeer
    vrows = -(-(4 + tn) // 8) * 8
    dma = pltpu.SemaphoreType.DMA
    anywhere = pl.BlockSpec(memory_space=pl.ANY)

    def scratch(shape, dtype=BF16):
        return pltpu.VMEM(shape, dtype)

    out = pl.pallas_call(
        functools.partial(layer_kernel, tn, dpn),
        out_shape=(
            jax.ShapeDtypeStruct((rows_n, width), BF16),
            jax.ShapeDtypeStruct((rows_n, width), F32),
            jax.ShapeDtypeStruct((2, width, width), BF16),
            jax.ShapeDtypeStruct((8, 2, width, pw), BF16),
            jax.ShapeDtypeStruct((vrows, width), F32),
        ),
        in_specs=[pl.BlockSpec(memory_space=pltpu.SMEM)]
        + [anywhere] * 12,
        out_specs=(anywhere,) * 5,
        scratch_shapes=[
            scratch((vrows, width), F32),
            scratch((2, width, width)),
            scratch((8, 2, width, pw)),
            scratch((1, width), F32),
            scratch((1, width), F32),
            scratch((width,)),
            scratch((ffl,)),
            scratch((width,)),
            scratch((rows_n, width)),
            scratch((rows_n, width)),
            scratch((heads, hw, feat_n)),
            scratch((width, 3 * width)),
            scratch((width, width)),
            scratch((rows_n, width), F32),
            scratch((tn, 2, width, ffl)),
            scratch((tn, 8, ffl), F32),
            scratch((rows_n, width)),
            scratch((pairs, rows_n, pw)),
            scratch((pairs, rows_n, pw)),
            scratch((pairs, rows_n, pw)),
            scratch((pairs, rows_n, 2 * feat_n)),
            scratch((pairs, rows_n, 2 * feat_n)),
            scratch((pairs, 2 * pw, 2 * feat_n)),
            scratch((2 * pw, 2 * pw)),
            scratch((2 * pw, pw)),
            scratch((nb, BR, BR)),
            scratch((nb, BR, BR)),
            scratch((nb + 1, pairs, pw + 16, feat_n), F32),
            scratch((nb, pairs, pw + 16, feat_n)),
            scratch((rows_n, width), F32),
            scratch((rows_n, width)),
            scratch((rows_n, width), F32),
            scratch((rows_n, width), F32),
            scratch((rows_n, 1), F32),
            scratch((rows_n, width)),
            scratch((2, rows_n, width)),
            scratch((pairs, pw + 16, feat_n)),
            scratch((pairs, pw + 16, feat_n)),
            scratch((pairs, pw + 16, feat_n)),
            scratch((pairs, pw + 16, feat_n)),
            scratch((tn, 2, width, width)),
            scratch((2, width, width)),
            scratch((4, npeer - 1, rp, width)),
            scratch((tn - 1, rp, width)),
            scratch((8, 2, width, pw)),
            scratch((4, width, pw)),
            scratch((8, npeer - 1, rp, pw)),
            scratch((8, max(tn, 2 * (tn - 1).bit_length()), rp, pw)),
            scratch((vrows, width), F32),
            scratch((vrows, width), F32),
            scratch((npeer, vrows, width), F32),
            scratch((tn, vrows, width), F32),
            dma((12,)),
            dma((5,)),
            dma(()),
            dma(()),
            dma(()),
            dma((tn - 1,)),
            dma(()),
            dma((tn - 1,)),
            dma(()),
            dma((tn - 1,)),
            dma(()),
            dma((pairs,)),
            dma(()),
            dma((pairs,)),
            dma(()),
            dma((2,)),
            dma(()),
            dma((tn,)),
            dma(()),
            dma((tn - 1,)),
            dma(()),
            dma(()),
            dma(()),
            dma(()),
            dma(()),
            dma((4,)),
            dma(()),
            dma((8,)),
            dma((2,)),
            dma((8, (tn - 1).bit_length())),
            dma(()),
            dma((8,)),
            dma(()),
            dma((8,)),
            dma(()),
            dma(()),
            dma(()),
            dma(()),
            dma(()),
            dma(()),
        ],
        compiler_params=pltpu.CompilerParams(
            collective_id=0, has_side_effects=True, vmem_limit_bytes=63 * 1024 * 1024
        ),
    )(
        seq_lengths,
        tokens,
        cotangent,
        features,
        ln1_gain[None],
        w_qkv,
        w_out,
        b_out,
        ln2_gain[None],
        w_in,
        b_in,
        w_down,
        b_down,
    )
    row = jax.ShapeDtypeStruct((1, width), F32)

    def square(n):
        return jax.ShapeDtypeStruct((width, n * width), F32)

    done = pl.pallas_call(
        finish_kernel,
        out_shape=(out[0], out[1], square(3), square(1), square(1), square(1)) + (row,) * 5,
        in_specs=[anywhere] * 5,
        out_specs=(anywhere,) * 11,
        scratch_shapes=[
            scratch((rows_n, width)),
            scratch((rows_n, width), F32),
            scratch((2, width, width)),
            scratch((8, 2, width, pw)),
            scratch((vrows, width), F32),
            scratch((5, 1, width), F32),
            scratch((width, 3 * width), F32),
            scratch((width, width), F32),
            scratch((width, width), F32),
            scratch((width, width), F32),
            dma((5,)),
            dma((12,)),
        ],
        compiler_params=pltpu.CompilerParams(vmem_limit_bytes=63 * 1024 * 1024),
    )(*out)
    layer_out, input_grad, gwq, gwo, gwi, gwd, gl1, gbo, gl2, gbi, gbd = done
    return (
        layer_out,
        input_grad,
        gl1[0],
        gwq,
        gwo,
        gbo[0],
        gl2[0],
        gwi,
        gbi[0],
        gwd,
        gbd[0],
    )


def solution(mesh):
    tn, dpn = mesh.shape["tensor"], mesh.shape["dp"]
    rows = P(("dp", "tensor"), None)
    return jax.shard_map(
        functools.partial(local, tn, dpn),
        mesh=mesh,
        in_specs=(
            rows,
            rows,
            P("dp", None),
            P(),
            P(),
            P(),
            P(),
            P(),
            P(),
            P(None, "tensor"),
            P("tensor"),
            P("tensor", None),
            P(),
        ),
        out_specs=(
            rows,
            rows,
            P(),
            P(),
            P(),
            P(),
            P(),
            P(None, "tensor"),
            P("tensor"),
            P("tensor", None),
            P(),
        ),
        check_vma=False,
    )
```
